32 devices in a mesh: seq: 8 (over z, y), wshard: 4 (over x, core).
Axes of the slice: x: 2, y: 2, z: 4, core: 2. Of those that a mesh axis runs over, the one named last changes fastest.
Arguments:
- inputs: bfloat16 [4, 8192, 768], P('wshard', 'seq'), may hold values from -6 to 6
- cotangent: bfloat16 [4, 8192, 768], P('wshard', 'seq'), may hold values from -6 to 6
- lengths: int32 [4, 3], P('wshard'), may hold values from 1024 to 4096, as said below
- in_proj: bfloat16 [768, 3352], P('wshard'), may hold values from -0.21875 to 0.21875
- out_proj: bfloat16 [1536, 768], P('wshard'), may hold values from -0.15625 to 0.15625
- conv_weight: bfloat16 [4, 1792], P(None, 'wshard'), may hold values from -3 to 3
- conv_bias: bfloat16 [1792], P('wshard'), may hold values from -3 to 3
- a_log: bfloat16 [24], P('wshard'), may hold values from -1 to 2
- d_skip: bfloat16 [24], P('wshard'), may hold values from 0.5 to 1.5
- dt_bias: bfloat16 [24], P('wshard'), may hold values from -8 to -3
- norm_gain: bfloat16 [768], P('wshard'), may hold values from 0.099609375 to 1.8984375
- gate_gain: bfloat16 [1536], P('wshard'), may hold values from 0.099609375 to 1.8984375
Outputs:
- mixed: bfloat16 [4, 8192, 768], P('wshard', 'seq')
- grad_input: bfloat16 [4, 8192, 768], P('wshard', 'seq')
- grad_in_proj: float32 [768, 3352], P('wshard')
- grad_out_proj: float32 [1536, 768], P('wshard')
- grad_conv_weight: float32 [4, 1792], P(None, 'wshard')
- grad_conv_bias: float32 [1792], P('wshard')
- grad_a_log: float32 [24], P('wshard')
- grad_d_skip: float32 [24], P('wshard')
- grad_dt_bias: float32 [24], P('wshard')
- grad_norm_gain: float32 [768], P('wshard')
- grad_gate_gain: float32 [1536], P('wshard')
The draws below stay inside these ranges and needn't reach their ends.
Inputs may be any that keep to these rules, and one draw needn't show every extreme that they name: `lengths`: each pack holds 3 documents laid end to end from position 0, each of 1024 to 4096 tokens, one exactly 4096; their sum is at most 8192, the rest is padding.
All inputs are finite; a program needn't handle non-finite values.
Results may differ from the reference program's by a relative error of at most 0.012.
Values may be sent and summed in bfloat16 or wider, within the bound.
No kernel may reach another device: no remote copies, remote signals or barrier semaphores. Data moves between devices by JAX's collectives and lax.ppermute only.
A program may use at most 256 MiB of HBM per device.

```python
from functools import partial
import jax
import jax.numpy as jnp
from jax import lax

D = 768
H = 24
P_SIZE = 64
N = 128
K = 4
Q = 256
LMIN = 1024
LMAX = 4096
DI = 1536
CONV = 1792
PROJ = 3352
PACKS = 4
PACK_LEN = 8192
NDOC = 3


def draw_lengths(key, part):
    key = jax.random.fold_in(key, 7)
    key_extra, key_which = jax.random.split(key)
    extra = jax.random.randint(key_extra, (PACKS, NDOC), 0, LMAX - LMIN + 1, dtype=jnp.int32)
    which = jax.random.randint(key_which, (PACKS, 1), 0, NDOC, dtype=jnp.int32)
    is_big = jnp.arange(NDOC, dtype=jnp.int32)[None, :] == which
    others = jnp.where(is_big, 0, extra)
    room = PACK_LEN - NDOC * LMIN - (LMAX - LMIN)
    total = jnp.sum(others, axis=1, keepdims=True, dtype=jnp.int32)
    scaled = jnp.where(total > room, others * room // jnp.maximum(total, 1), others)
    chosen = jnp.where(is_big, LMAX - LMIN, scaled)
    return (LMIN + chosen).astype(jnp.int32)


def shard_levels(stream_key, dims, cuts, smallest, largest):
    gain = 1.0
    for position, blocks in cuts:
        steps = jax.random.uniform(jax.random.fold_in(jax.random.fold_in(stream_key, 6), position), (blocks,), jnp.float32, smallest / len(cuts), largest / len(cuts))
        gain = gain * jnp.repeat(jnp.exp(steps), dims[position] // blocks).reshape((-1,) + (1,) * (len(dims) - 1 - position))
    return gain


def noise(rng, extent, deviation, limit, pieces=(), kind=jnp.bfloat16):
    entries = deviation * jax.random.normal(rng, extent, jnp.float32)
    if pieces:
        entries = entries * shard_levels(rng, extent, pieces, -0.22, 0.18)
    return jnp.clip(entries, -limit, limit).astype(kind)


def setup_inputs(seed: int = 0) -> dict:
    streams_of = jax.random.split(jax.random.key(seed), 13)
    inputs = noise(streams_of[0], (PACKS, PACK_LEN, D), 1.0, 6.0, ((0, 4), (1, 8)))
    cotangent = noise(streams_of[1], (PACKS, PACK_LEN, D), 1.0, 6.0, ((0, 4), (1, 8)))
    lengths = draw_lengths(jax.random.fold_in(streams_of[12], 71), 0)
    in_proj = noise(streams_of[3], (D, PROJ), D ** -0.5, 0.21875, ((0, 4),))
    out_proj = noise(streams_of[4], (DI, D), DI ** -0.5, 0.15625, ((0, 4),))
    conv_weight = noise(streams_of[5], (K, CONV), K ** -0.5, 3.0, ((1, 4),))
    conv_bias = noise(streams_of[6], (CONV,), 0.5, 3.0, ((0, 4),))
    a_log = jnp.clip(-1.0 + 3.0 * jax.random.uniform(streams_of[7], (H,), jnp.float32) ** shard_levels(streams_of[7], (H,), ((0, 4),), -0.2, 0.2), -1.0, 2.0).astype(jnp.bfloat16)
    d_skip = jnp.clip(0.5 + 1.0 * jax.random.uniform(streams_of[8], (H,), jnp.float32) ** shard_levels(streams_of[8], (H,), ((0, 4),), -0.2, 0.2), 0.5, 1.5).astype(jnp.bfloat16)
    dt_bias = jnp.clip(-8.0 + 5.0 * jax.random.uniform(streams_of[9], (H,), jnp.float32) ** shard_levels(streams_of[9], (H,), ((0, 4),), -0.2, 0.2), -8.0, -3.0).astype(jnp.bfloat16)
    norm_gain = jnp.clip(1.0 + 0.18 * jax.random.normal(streams_of[10], (D,), jnp.float32), 0.099609375, 1.8984375).astype(jnp.bfloat16)
    gate_gain = jnp.clip(1.0 + 0.18 * jax.random.normal(streams_of[11], (DI,), jnp.float32), 0.099609375, 1.8984375).astype(jnp.bfloat16)
    return dict(inputs=inputs, cotangent=cotangent, lengths=lengths, in_proj=in_proj, out_proj=out_proj, conv_weight=conv_weight, conv_bias=conv_bias, a_log=a_log, d_skip=d_skip, dt_bias=dt_bias, norm_gain=norm_gain, gate_gain=gate_gain)


highest = lax.Precision.HIGHEST
eps = 1e-05

@jax.custom_vjp
def low(v):
    return lax.optimization_barrier(v.astype(jnp.bfloat16)).astype(jnp.float32)

@jax.custom_vjp
def low_back(v):
    return v

def low_keep(v):
    return (low(v), None)

def low_pass(kept, grad):
    return (grad,)

def back_keep(v):
    return (v, None)

def back_low(kept, grad):
    return (low(grad),)
low.defvjp(low_keep, low_pass)
low_back.defvjp(back_keep, back_low)

def block_terms(decay_rows, seg_rows, seg_prev):
    cum_log = jnp.cumsum(decay_rows, axis=0)
    index_line = jnp.arange(seg_rows.shape[0])
    same_doc = (seg_rows[:, None] == seg_rows[None, :]) & (index_line[:, None] >= index_line[None, :])
    log_gap = cum_log.T[:, :, None] - cum_log.T[:, None, :]
    inside = jnp.where(same_doc[None], jnp.exp(jnp.where(same_doc[None], log_gap, 0.0)), 0.0)
    enter_decay = jnp.exp(cum_log) * (seg_rows == seg_prev).astype(jnp.float32)[:, None]
    ending = (seg_rows == seg_rows[-1]).astype(jnp.float32)[:, None] * jnp.exp(cum_log[-1][None, :] - cum_log)
    leave_decay = jnp.exp(cum_log[-1]) * (seg_rows[-1] == seg_prev).astype(jnp.float32)
    return (inside, enter_decay, ending, leave_decay)

def block_forward(params, carried, block_items):
    w_in, w_out, conv_w, conv_b, log_rate, skip_coef, dt_shift, gain_in, gain_gate = params
    state_now, tail_rows, tail_seg, seg_prev = carried
    block_rows, seg_rows, keep_mask = block_items
    normed = low(block_rows * lax.rsqrt(lax.optimization_barrier(jnp.mean(block_rows * block_rows, axis=-1, keepdims=True)) + eps) * gain_in)
    projected = low_back(jnp.dot(normed, w_in, precision=highest))
    gate_in = projected[:, :DI]
    conv_in = low(projected[:, DI:DI + CONV])
    dt_raw = projected[:, DI + CONV:]
    extended = jnp.concatenate([tail_rows, conv_in], axis=0)
    seg_ext = jnp.concatenate([tail_seg, seg_rows], axis=0)
    conv_pre = jnp.broadcast_to(conv_b, (Q, CONV))
    for offset in range(K):
        linked = (seg_ext[offset:offset + Q] == seg_rows).astype(jnp.float32)[:, None]
        conv_pre = conv_pre + conv_w[offset] * extended[offset:offset + Q] * linked
    conv_out = jax.nn.silu(conv_pre)
    head_values = conv_out[:, :DI].reshape(Q, H, P_SIZE)
    b_rows = conv_out[:, DI:DI + N]
    c_rows = conv_out[:, DI + N:]
    step_rows = jax.nn.softplus(dt_raw + dt_shift)
    decay_rows = step_rows * -jnp.exp(log_rate)
    inside, enter_decay, ending, leave_decay = block_terms(decay_rows, seg_rows, seg_prev)
    scores = jnp.dot(c_rows, b_rows.T, precision=highest)
    mixing = scores[None] * inside * step_rows.T[:, None, :]
    ssd_out = jnp.einsum('hts,shp->thp', mixing, head_values, precision=highest)
    ssd_out = ssd_out + enter_decay[:, :, None] * jnp.einsum('tn,hpn->thp', c_rows, state_now, precision=highest)
    ssd_out = ssd_out + skip_coef[None, :, None] * head_values
    new_state = leave_decay[:, None, None] * state_now + jnp.einsum('shp,sn->hpn', (step_rows * ending)[:, :, None] * head_values, b_rows, precision=highest)
    gated = ssd_out.reshape(Q, DI) * jax.nn.silu(gate_in)
    gate_normed = low(gated * lax.rsqrt(lax.optimization_barrier(jnp.mean(gated * gated, axis=-1, keepdims=True)) + eps) * gain_gate)
    branch = jnp.dot(gate_normed, w_out, precision=highest)
    result = keep_mask[:, None] * (block_rows + branch)
    return ((new_state, extended[Q:], seg_ext[Q:], seg_rows[-1]), result)

def pack_forward(params, pack_rows, seg_line):
    keep_line = (seg_line < NDOC).astype(jnp.float32)
    start = (jnp.zeros((H, P_SIZE, N), jnp.float32), jnp.zeros((K - 1, CONV), jnp.float32), jnp.full((K - 1,), -1, jnp.int32), jnp.array(-1, jnp.int32))
    stepper = jax.checkpoint(partial(block_forward, params))
    finish, outputs = lax.scan(stepper, start, (pack_rows.reshape(-1, Q, D), seg_line.reshape(-1, Q), keep_line.reshape(-1, Q)))
    return outputs.reshape(-1, D)

def reference(inputs, cotangent, lengths, in_proj, out_proj, conv_weight, conv_bias, a_log, d_skip, dt_bias, norm_gain, gate_gain):
    params = (in_proj.astype(jnp.float32), out_proj.astype(jnp.float32), conv_weight.astype(jnp.float32), conv_bias.astype(jnp.float32), a_log.astype(jnp.float32), d_skip.astype(jnp.float32), dt_bias.astype(jnp.float32), norm_gain.astype(jnp.float32), gate_gain.astype(jnp.float32))
    doc_ends = jnp.cumsum(lengths, axis=1, dtype=jnp.int32)
    positions = jnp.arange(PACK_LEN, dtype=jnp.int32)
    segments = lax.optimization_barrier(jnp.sum((positions[None, :, None] >= doc_ends[:, None, :]).astype(jnp.int32), axis=2)).astype(jnp.int32)

    def whole_layer(data_in, weights):

        def one_pack(pair):
            return pack_forward(weights, pair[0], pair[1])
        return lax.map(one_pack, (data_in, segments))
    data_in = inputs.astype(jnp.float32)
    outputs, pullback = jax.vjp(whole_layer, data_in, params)
    grad_data, grads = pullback(cotangent.astype(jnp.float32))
    return (outputs.astype(jnp.bfloat16), grad_data.astype(jnp.bfloat16), grads[0], grads[1], grads[2], grads[3], grads[4], grads[5], grads[6], grads[7], grads[8])
```

```python
import jax
import jax.numpy as jnp
from jax import lax
from jax.experimental import pallas as pl
from jax.experimental.pallas import tpu as pltpu
from jax.sharding import PartitionSpec as P

f32 = jnp.float32
bf16 = jnp.bfloat16
EPS = 1e-05
LOG2E = 1.4426950408889634
CH = 128
TB = 256
LONGEST = 4096
HIGH = lax.Precision.HIGHEST
VMEM = 60 * 1024 * 1024


def sigmoid(v):
    return 0.5 * jnp.tanh(0.5 * v) + 0.5


def dot(a, b):
    return jnp.dot(a, b, preferred_element_type=f32)


def dot_nt(a, b):
    return lax.dot_general(a, b, (((1,), (1,)), ((), ())), preferred_element_type=f32)


def two(v):
    hi = v.astype(bf16)
    return hi, (v - hi.astype(f32)).astype(bf16)


def spread(v, e2):
    return dot(jnp.concatenate(two(v), axis=1), e2)


def cost(us):
    return pl.CostEstimate(flops=int(us * 1.1e9), bytes_accessed=1 << 20, transcendentals=0)


def call(kernel, grid, ins, outs, scratch, us, args, name):
    return pl.pallas_call(
        kernel,
        grid_spec=pltpu.PrefetchScalarGridSpec(
            num_scalar_prefetch=1,
            grid=grid,
            in_specs=ins,
            out_specs=[o[0] for o in outs],
            scratch_shapes=scratch,
        ),
        out_shape=[jax.ShapeDtypeStruct(o[1], o[2]) for o in outs],
        compiler_params=pltpu.CompilerParams(
            vmem_limit_bytes=VMEM, dimension_semantics=("arbitrary",)
        ),
        cost_estimate=cost(us),
        name=name,
    )(*args)


def rows(block, cols, col=0):
    return pl.BlockSpec((block, cols), lambda i, s: (i, col))


def whole(shape):
    return pl.BlockSpec(shape, lambda i, s: (0,) * len(shape))


def norm_rows(uf, gain):
    scale = lax.rsqrt(jnp.mean(uf * uf, axis=-1, keepdims=True) + EPS)
    return (uf * scale * gain).astype(bf16)


def place(buf, ids, parts, width):
    for j, part in enumerate(parts):
        n = part.shape[0]
        at = pl.multiple_of(ids[j] * n, 64)
        buf[pl.ds(at, n), :width] = part[...]


def front_kernel(np_, di, conv, heads):
    def kernel(ids, u, ue, gain, *rest):
        parts = rest[:np_]
        (cw, cb, dtb, nr, tok, e2, nrm_o, xbc_o, xc_o, slope_o, xd_o, dts_o, cc_o, ct_o,
         st_o, db_o, end_o, tot_o, nrme_o, xbce_o, wbuf, ext, state, kd, sp) = rest[np_:]
        i = pl.program_id(0)
        n = (conv - di) // 2

        @pl.when(i == 0)
        def _():
            wbuf[:, conv:] = jnp.zeros((wbuf.shape[0], wbuf.shape[1] - conv), bf16)
            place(wbuf, ids, parts, conv + heads)
            nrme = norm_rows(ue[...].astype(f32), gain[...])
            nrme_o[...] = nrme
            pe = dot(nrme, wbuf[:, :conv]).astype(bf16)
            xbce_o[...] = pe
            ext[0:8, :] = pe.astype(f32)[8:16]
            state[...] = jnp.zeros_like(state)
            kd[...] = jnp.ones_like(kd)

        nrm = norm_rows(u[...].astype(f32), gain[...])
        nrm_o[...] = nrm
        pd = dot(nrm, wbuf[:, conv:])
        for c0 in range(0, conv, 256):
            px = dot(nrm, wbuf[:, c0 : c0 + 256]).astype(bf16)
            xbc_o[:, c0 : c0 + 256] = px
            ext[8 : 8 + TB, c0 : c0 + 256] = px.astype(f32)
        sh = pd + dtb[...]
        dt = jnp.maximum(sh, 0.0) + jnp.log1p(jnp.exp(-jnp.abs(sh)))
        dts_o[:, :128] = dt
        dts_o[:, 128:] = jax.nn.sigmoid(sh)
        a2 = dt * nr[...]
        ri = lax.broadcasted_iota(jnp.int32, (CH, CH), 0)
        ci = lax.broadcasted_iota(jnp.int32, (CH, CH), 1)
        low = (ri >= ci).astype(f32)
        pieces = [dt]
        leaves = []
        for k in range(TB // CH):
            r = slice(k * CH, (k + 1) * CH)
            c2 = jnp.dot(low, a2[r], precision=HIGH, preferred_element_type=f32)
            cc_o[r, :] = c2
            ct_o[:, r] = c2.T[: ct_o.shape[0], :]
            pieces.append(jnp.exp2(c2[CH - 1 :] - c2) * tok[r, 2:3])
            leaves.append(jnp.exp2(c2[CH - 1 :]) * tok[(k + 1) * CH - 1 : (k + 1) * CH, 1:2])
        lv = jnp.concatenate([jnp.broadcast_to(v, (8, 128)) for v in leaves], axis=0)
        sp[...] = spread(jnp.concatenate(pieces + [lv], axis=0), e2[...])
        for r0 in range(0, TB, 64):
            l0, l1, l2 = tok[r0 : r0 + 64, 3:4], tok[r0 : r0 + 64, 4:5], tok[r0 : r0 + 64, 5:6]
            for c0 in range(0, conv, 256):
                c = slice(c0, c0 + 256)
                pre = cb[:, c] + cw[3:4, c] * ext[8 + r0 : 72 + r0, c]
                pre = pre + cw[2:3, c] * (ext[7 + r0 : 71 + r0, c] * l2)
                pre = pre + cw[1:2, c] * (ext[6 + r0 : 70 + r0, c] * l1)
                pre = pre + cw[0:1, c] * (ext[5 + r0 : 69 + r0, c] * l0)
                sg = sigmoid(pre)
                xc = pre * sg
                xc_o[r0 : r0 + 64, c] = xc.astype(bf16)
                slope_o[r0 : r0 + 64, c] = (sg + xc * (1.0 - sg)).astype(bf16)
                if c0 < di:
                    xd_o[r0 : r0 + 64, c] = (xc * sp[r0 : r0 + 64, c]).astype(bf16)
        ext[0:8, :] = ext[TB : TB + 8, :]
        for k in range(TB // CH):
            r = slice(k * CH, (k + 1) * CH)
            st_o[k] = state[...].astype(bf16)
            db_o[k] = jnp.broadcast_to(kd[...], (8, 128))
            bt = xc_o[r, di : di + n].astype(f32).T.astype(bf16)
            for c0 in range(0, di, 256):
                c = slice(c0, c0 + 256)
                xw = (xd_o[r, c].astype(f32) * sp[TB + k * CH : TB + (k + 1) * CH, c]).astype(bf16)
                lvr = sp[2 * TB + 8 * k : 2 * TB + 8 * k + 1, c]
                state[:, c] = lvr * state[:, c] + dot(bt, xw)
            kd[...] = kd[...] * leaves[k]

        @pl.when(i == pl.num_programs(0) - 1)
        def _():
            end_o[...] = state[...]
            tot_o[...] = spread(jnp.broadcast_to(kd[...], (8, 128)), e2[...])

    return kernel


def inner_kernel(heads, di):
    p = di // heads
    per = 128 // p

    def kernel(ids, b, c, xd, cc, ct, tok, segr, y_o):
        s = dot_nt(c[...], b[...])
        ri = lax.broadcasted_iota(jnp.int32, (CH, CH), 0)
        ci = lax.broadcasted_iota(jnp.int32, (CH, CH), 1)
        bias = jnp.where((tok[:, 0:1] == segr[...]) & (ri >= ci), 0.0, -1e30)
        lanes = lax.broadcasted_iota(jnp.int32, (1, 128), 1) // p
        for j in range(heads // per):
            xp = xd[:, 128 * j : 128 * j + 128]
            ms, xs = [], []
            for q in range(per):
                h = per * j + q
                e = jnp.exp2(cc[:, h : h + 1] - ct[h : h + 1, :] + bias)
                ms.append((s * e).astype(bf16))
                xs.append(xp * (lanes == q).astype(f32).astype(bf16))
            out = dot(jnp.concatenate(ms, axis=1), jnp.concatenate(xs, axis=0))
            y_o[:, 128 * j : 128 * j + 128] = out.astype(bf16)

    return kernel


def gate_kernel(np_, di, d):
    def kernel(ids, nrm, yin, x, c_in, cc, tok, st, db, inc, u, cot, *rest):
        wz, wo = rest[:np_], rest[np_ : 2 * np_]
        (gain, dsk, e2, mixed_o, gn_o, dz_o, dy_o, edy_o, e_o, sf_o, dc_o, rin_o, gg_o, gs_o,
         rg_o, zbuf, obuf, z, yi, dgn, ee, pr) = rest[2 * np_ :]
        i = pl.program_id(0)

        @pl.when(i == 0)
        def _():
            place(zbuf, ids, wz, di)
            place(obuf, ids, wo, d)
            gg_o[...] = jnp.zeros_like(gg_o)
            gs_o[...] = jnp.zeros_like(gs_o)
            rg_o[...] = jnp.zeros_like(rg_o)

        keep = tok[:, 6:7]
        ef = cot[...].astype(f32) * keep
        e = ef.astype(bf16)
        e_o[...] = e
        nb = TB // CH
        ents = []
        for k in range(nb):
            r = slice(k * CH, (k + 1) * CH)
            ents.append(jnp.exp2(cc[r, :]) * tok[r, 1:2])
        ee[...] = spread(jnp.concatenate(ents + [db[k] for k in range(nb)], axis=0), e2[...])
        for k in range(nb):
            r = slice(k * CH, (k + 1) * CH)
            for c0 in range(0, di, 256):
                c = slice(c0, c0 + 256)
                dbr = ee[TB + 8 * k : TB + 8 * k + 1, c]
                sf = (st[k, :, c].astype(f32) + dbr * inc[:, c].astype(f32)).astype(bf16)
                sf_o[k, :, c] = sf
                yi[r, c] = dot(c_in[r, :], sf)
        z[...] = dot(nrm[...], zbuf[...])
        dgn[...] = dot_nt(e, obuf[...])

        def strip(t, carry):
            r = pl.ds(pl.multiple_of(t * 16, 16), 16)
            xs = x[r, :].astype(f32)
            eyi = ee[r, :] * yi[r, :]
            y = yin[r, :].astype(f32) + eyi + dsk[...] * xs
            zz = z[r, :]
            sg = sigmoid(zz)
            act = zz * sg
            g = y * act
            scale = lax.rsqrt(jnp.mean(g * g, axis=-1, keepdims=True) + EPS)
            ug = g * scale
            gn_o[r, :] = (ug * gain[...]).astype(bf16)
            dg0 = dgn[r, :]
            pg = dg0 * ug
            gg_o[...] += pg[0:8] + pg[8:16]
            dn = dg0 * gain[...]
            m = jnp.mean(dn * ug, axis=-1, keepdims=True)
            dg = scale * (dn - ug * m)
            dy = dg * act
            dz_o[r, :] = (dg * y * (sg + act * (1.0 - sg))).astype(bf16)
            dy_o[r, :] = dy.astype(bf16)
            ps = xs * dy
            gs_o[...] += ps[0:8] + ps[8:16]
            edy_o[r, :] = (dy * ee[r, :]).astype(bf16)
            pr[r, :] = (dy * eyi).astype(bf16)
            return carry

        lax.fori_loop(0, TB // 16, strip, 0)
        rin_o[...] = dot_nt(pr[...], e2[0:128, :])
        mixed_o[...] = (keep * (u[...].astype(f32) + dot(gn_o[...], obuf[...]))).astype(bf16)
        for k in range(nb):
            r = slice(k * CH, (k + 1) * CH)
            ctr = c_in[r, :].astype(f32).T.astype(bf16)
            for c0 in range(0, di, 256):
                c = slice(c0, c0 + 256)
                dcv = dot(ctr, edy_o[r, c])
                dc_o[k, :, c] = dcv
                rg_o[:, c] += ee[TB + 8 * k : TB + 8 * k + 1, c] * dcv

    return kernel


def inner_back_kernel(heads, di):
    p = di // heads
    per = 128 // p

    def kernel(ids, b, c, xd, dy, cc, ct, tok, segr, gxd_o, db_o, dc_o, rk_o, gs, rr):
        st = dot_nt(b[...], c[...])
        si = lax.broadcasted_iota(jnp.int32, (CH, CH), 0)
        ti = lax.broadcasted_iota(jnp.int32, (CH, CH), 1)
        bias = jnp.where((tok[:, 0:1] == segr[...]) & (ti >= si), 0.0, -1e30)
        lanes = lax.broadcasted_iota(jnp.int32, (1, 128), 1) // p
        rr[...] = jnp.zeros_like(rr)
        rk_o[...] = jnp.zeros_like(rk_o)
        gsum = jnp.zeros((CH, CH), f32)
        for j in range(heads // per):
            xp = xd[:, 128 * j : 128 * j + 128]
            dyp = dy[:, 128 * j : 128 * j + 128]
            dys = jnp.concatenate(
                [dyp * (lanes == q).astype(f32).astype(bf16) for q in range(per)], axis=0
            )
            gm = dot_nt(xp, dys)
            ms = []
            for q in range(per):
                h = per * j + q
                e = jnp.exp2(ct[h : h + 1, :] - cc[:, h : h + 1] + bias)
                ms.append((st * e).astype(bf16))
                ge = gm[:, q * CH : (q + 1) * CH] * e
                gsum = gsum + ge
                ex = ge * st
                rr[h : h + 1, :] = jnp.sum(ex, axis=0, keepdims=True)
                rk_o[:, h : h + 1] = jnp.sum(ex, axis=1, keepdims=True)
            out = dot(jnp.concatenate(ms, axis=1), dys)
            gxd_o[:, 128 * j : 128 * j + 128] = out.astype(bf16)
        rk_o[...] = rr[...].T - rk_o[...]
        db_o[...] = dot(gsum.astype(bf16), c[...])
        dc_o[...] = dot(gsum.T.astype(bf16), b[...])

    return kernel


def back_kernel(di, conv, heads):
    def kernel(ids, xc, b_in, slope, xbc, xbce, xd, dts, cc, tok, elink, gxd, dbi, dci, rk, rin, dy, edy,
               sf, dcs, gend, cw, dsk, nr, e2, gp_o, edge_o, gw_o, gb_o, ga_o, gdt_o,
               ds, sp, sr, ext, xw, xq, xe):
        i = pl.program_id(0)
        n = (conv - di) // 2
        nb = TB // CH

        @pl.when(i == 0)
        def _():
            ds[...] = gend[...].astype(f32)
            ext[TB : TB + 8, :] = jnp.zeros((8, conv), f32)
            gw_o[...] = jnp.zeros_like(gw_o)
            gb_o[...] = jnp.zeros_like(gb_o)
            ga_o[...] = jnp.zeros_like(ga_o)
            gdt_o[...] = jnp.zeros_like(gdt_o)

        dt = dts[:, :128]
        pieces, leaves = [dt], []
        for k in range(nb):
            r = slice(k * CH, (k + 1) * CH)
            c2 = cc[r, :]
            pieces.append(jnp.exp2(c2[CH - 1 :] - c2) * tok[r, 2:3])
            leaves.append(jnp.exp2(c2[CH - 1 :]) * tok[(k + 1) * CH - 1 : (k + 1) * CH, 1:2])
        lv = jnp.concatenate([jnp.broadcast_to(v, (8, 128)) for v in leaves], axis=0)
        sp[...] = spread(jnp.concatenate(pieces + [lv], axis=0), e2[...])
        lsum = [None] * nb
        for k in reversed(range(nb)):
            r = slice(k * CH, (k + 1) * CH)
            lacc = []
            gb = dbi[r, :]
            gc = dci[r, :]
            for c0 in range(0, di, 256):
                c = slice(c0, c0 + 256)
                dsv = ds[:, c]
                dsb = dsv.astype(bf16)
                sfv = sf[k, :, c]
                sr[r, c] = dot(b_in[r, :], dsb)
                xwv = (xd[r, c].astype(f32) * sp[TB + k * CH : TB + (k + 1) * CH, c]).astype(bf16)
                gb = gb + dot_nt(xwv, dsb)
                gc = gc + dot_nt(edy[r, c], sfv)
                lacc.append(jnp.sum(dsv * sfv.astype(f32), axis=0, keepdims=True))
                lvr = sp[2 * TB + 8 * k : 2 * TB + 8 * k + 1, c]
                ds[:, c] = lvr * dsv + dcs[k, :, c]
            lrow = jnp.broadcast_to(jnp.concatenate(lacc, axis=1), (8, di))
            lhi, llo = two(lrow)
            lsum[k] = (dot_nt(lhi, e2[0:128, :]) + dot_nt(llo, e2[0:128, :]))[0:1]
            ext[r, di : di + n] = gb * slope[r, di : di + n].astype(f32)
            ext[r, di + n :] = gc * slope[r, di + n :].astype(f32)

        def strip(t, carry):
            r = pl.ds(pl.multiple_of(t * 16, 16), 16)
            re = pl.ds(pl.multiple_of(TB + t * 16, 16), 16)
            x = xc[r, :].astype(f32)
            es = sp[re, :] * sr[r, :]
            q = gxd[r, :].astype(f32) + es
            gx = sp[r, :] * q + dsk[...] * dy[r, :].astype(f32)
            ext[r, 0:di] = gx * slope[r, 0:di].astype(f32)
            xq[r, :] = (x * q).astype(bf16)
            xe[r, :] = (x * es).astype(bf16)
            return carry

        lax.fori_loop(0, TB // 16, strip, 0)
        gdt = dot_nt(xq[...], e2[0:128, :])
        et = dot_nt(xe[...], e2[0:128, :]) * dt
        ri = lax.broadcasted_iota(jnp.int32, (CH, CH), 0)
        ci = lax.broadcasted_iota(jnp.int32, (CH, CH), 1)
        tri = jnp.concatenate([(ci >= ri).astype(f32), (ci < ri).astype(f32)], axis=1)
        for k in range(nb):
            r = slice(k * CH, (k + 1) * CH)
            v = jnp.concatenate([rk[r, :] + rin[r, :], et[r]], axis=0)
            ga = jnp.dot(tri, v, precision=HIGH, preferred_element_type=f32) + lsum[k] * leaves[k]
            dtk = dts[r, :128]
            ddt = (gdt[r] + ga * nr[...]) * dts[r, 128:]
            gad = ga * dtk
            acc_a, acc_d = gad[0:8], ddt[0:8]
            for q in range(8, CH, 8):
                acc_a = acc_a + gad[q : q + 8]
                acc_d = acc_d + ddt[q : q + 8]
            ga_o[...] += acc_a
            gdt_o[...] += acc_d
            gp_o[r, conv:] = ddt.astype(bf16)
        for r0 in range(0, TB, 64):
            for c0 in range(0, conv, 256):
                c = slice(c0, c0 + 256)
                g0 = ext[r0 : r0 + 64, c]
                xb = xbc[r0 : r0 + 64, c].astype(f32)
                gsum = cw[3:4, c] * g0
                ws = [None, None, None, g0 * xb]
                for s in (1, 2, 3):
                    gs = ext[r0 + s : r0 + s + 64, c] * tok[r0 : r0 + 64, 6 + s : 7 + s]
                    gsum = gsum + cw[3 - s : 4 - s, c] * gs
                    ws[3 - s] = gs * xb
                gp_o[r0 : r0 + 64, c] = gsum.astype(bf16)
                gb = g0[0:8]
                for q in range(8, 64, 8):
                    gb = gb + g0[q : q + 8]
                gb_o[:, c] += gb
                for o in range(4):
                    w = ws[o][0:8]
                    for q in range(8, 64, 8):
                        w = w + ws[o][q : q + 8]
                    gw_o[8 * o : 8 * o + 8, c] += w
        ext[TB : TB + 8, :] = ext[0:8, :]

        @pl.when(i == pl.num_programs(0) - 1)
        def _():
            zero = jnp.zeros((8, 256), f32)
            for c0 in range(0, conv, 256):
                c = slice(c0, c0 + 256)
                xb = xbce[8:16, c].astype(f32)
                ext[8:16, c] = ext[TB : TB + 8, c]
                ext[0:8, c] = zero
                gsum = zero
                for s in (1, 2, 3):
                    gs = ext[s : s + 8, c] * elink[:, 6 + s : 7 + s]
                    gsum = gsum + cw[3 - s : 4 - s, c] * gs
                    gw_o[8 * (3 - s) : 8 * (3 - s) + 8, c] += gs * xb
                edge_o[:, c] = jnp.concatenate([zero, gsum], axis=0).astype(bf16)

    return kernel


def input_kernel(np_, di, conv, heads):
    def kernel(ids, gpz, gpx, edge, u, e, *rest):
        wz, wx = rest[:np_], rest[np_ : 2 * np_]
        gain, gi_o, gg_o, zbuf, xbuf = rest[2 * np_ :]
        i = pl.program_id(0)

        @pl.when(i == 0)
        def _():
            xbuf[:, conv:] = jnp.zeros((xbuf.shape[0], xbuf.shape[1] - conv), bf16)
            place(zbuf, ids, wz, di)
            place(xbuf, ids, wx, conv + heads)
            gg_o[...] = jnp.zeros_like(gg_o)

        gn = dot_nt(gpz[...], zbuf[...]) + dot_nt(gpx[...], xbuf[...])
        last = (i == pl.num_programs(0) - 1).astype(f32)
        tail = dot_nt(edge[...], xbuf[:, :conv]) * last
        gn = jnp.concatenate([gn[: TB - 16], gn[TB - 16 :] + tail], axis=0)
        uf = u[...].astype(f32)
        scale = lax.rsqrt(jnp.mean(uf * uf, axis=-1, keepdims=True) + EPS)
        unit = uf * scale
        pg = gn * unit
        acc = pg[0:8]
        for q in range(8, TB, 8):
            acc = acc + pg[q : q + 8]
        gg_o[...] += acc
        dn = gn * gain[...]
        m = jnp.mean(dn * unit, axis=-1, keepdims=True)
        gi_o[...] = (e[...].astype(f32) + scale * (dn - unit * m)).astype(bf16)

    return kernel


def swap(v, axis, bit):
    return lax.ppermute(v, axis, [(k, k ^ bit) for k in range(lax.axis_size(axis))])


def shift(v, axis, steps):
    n = lax.axis_size(axis)
    return lax.ppermute(v, axis, [(k, k + steps) for k in range(n) if 0 <= k + steps < n])


def bits_of(n):
    return [1 << k for k in reversed(range((n - 1).bit_length()))]


def gather_parts(v, axis):
    parts = [v]
    for bit in bits_of(lax.axis_size(axis)):
        parts = parts + [swap(p, axis, bit) for p in parts]
    return parts


def part_ids(axis):
    ids = [lax.axis_index(axis)]
    for bit in bits_of(lax.axis_size(axis)):
        ids = ids + [k ^ bit for k in ids]
    return ids


def halve(v, axis, bit, at):
    send = lax.dynamic_index_in_dim(v, 1 - at, 0, keepdims=False)
    mine = lax.dynamic_index_in_dim(v, at, 0, keepdims=False)
    got = swap(send, axis, bit)
    return (mine.astype(f32) + got.astype(f32)).astype(bf16)


def reduce_rows(g):
    nw, ns = lax.axis_size("wshard"), lax.axis_size("seq")
    w, s = lax.axis_index("wshard"), lax.axis_index("seq")
    cols = g.shape[1]
    v = g.reshape(nw, -1, cols)
    bit = 1
    while bit < nw:
        v = v.reshape(-1, 2, v.shape[-2], cols).swapaxes(0, 1)
        v = halve(v, "wshard", bit, (w // bit) % 2)
        bit *= 2
    v = v.reshape(-1, cols)
    n = v.shape[0]
    for bit in [1 << k for k in range((ns - 1).bit_length())]:
        v = halve(v.reshape(2, -1, cols), "seq", bit, (s // bit) % 2)
    for bit in bits_of(ns):
        got = swap(v, "seq", bit)
        first = (s // bit) % 2 == 0
        v = jnp.concatenate([jnp.where(first, v, got), jnp.where(first, got, v)], axis=0)
    return v.astype(f32)


def pack_state(decay, state):
    hi, lo = two(decay)
    return jnp.concatenate([state.astype(bf16), hi, lo], axis=0)


def unpack_state(v, n):
    return v[n : n + 8].astype(f32)[:1] + v[n + 8 : n + 16].astype(f32)[:1], v[:n].astype(f32)


def carried(decay, state, sign):
    n = state.shape[0]
    tokens = carried_tokens[0]
    span = 1
    while span < -(-LONGEST // tokens):
        d, s = unpack_state(shift(pack_state(decay, state), "seq", sign * span), n)
        state = state + decay[:1] * s
        decay = decay * d
        span *= 2
    return shift(state.astype(bf16), "seq", sign)


carried_tokens = [1024]


def body(inputs, cotangent, lengths, in_proj, out_proj, conv_weight, conv_bias, a_log, d_skip,
         dt_bias, norm_gain, gate_gain):
    t, d = inputs.shape[1:]
    nw = lax.axis_size("wshard")
    di = out_proj.shape[0] * nw
    heads = a_log.shape[0] * nw
    conv = conv_bias.shape[0] * nw
    taps = conv_weight.shape[0]
    n = (conv - di) // 2
    p = di // heads
    docs = lengths.shape[1]
    nt, nc, nb = t // TB, t // CH, TB // CH
    wide = conv + 128
    carried_tokens[0] = t
    wx, wz = in_proj[:, di:], in_proj[:, :di]
    wx_parts = gather_parts(wx, "wshard")
    wz_parts = gather_parts(wz, "wshard")
    wo_parts = gather_parts(out_proj, "wshard")
    ids = jnp.stack(part_ids("wshard")).astype(jnp.int32)
    small = jnp.concatenate(
        [conv_weight.reshape(-1), conv_bias, a_log, d_skip, dt_bias, norm_gain, gate_gain]
    )[None]
    small = lax.all_gather(small, "wshard", axis=0, tiled=True).astype(f32)
    sizes = [taps * conv // nw, conv // nw, heads // nw, heads // nw, heads // nw, d // nw, di // nw]
    cut, off = [], 0
    for k in sizes:
        cut.append(small[:, off : off + k])
        off += k
    cw = cut[0].reshape(nw, taps, conv // nw).swapaxes(0, 1).reshape(taps, conv)
    cb, log_rate, skip, dtb, gain_in, gain_gate = [v.reshape(1, -1) for v in cut[1:]]
    rate = -jnp.exp(log_rate)
    pad = ((0, 0), (0, 128 - heads))
    nr = jnp.pad(rate, pad)
    nr2 = nr * LOG2E
    dtb = jnp.pad(dtb, pad)
    dsk = jnp.repeat(skip, p, axis=1)
    head_of = jnp.arange(di, dtype=jnp.int32) // p
    e1 = (jnp.arange(128, dtype=jnp.int32)[:, None] == head_of[None]).astype(bf16)
    e2 = jnp.concatenate([e1, e1], axis=0)
    first = lax.axis_index("seq") * t
    pos = first - 8 + jnp.arange(t + 16, dtype=jnp.int32)
    ends = jnp.cumsum(lengths[0], dtype=jnp.int32)
    seg = jnp.sum((pos[:, None] >= ends[None]).astype(jnp.int32), axis=1)
    seg = jnp.where(pos < 0, -1, seg)
    here = seg[: t + 8]
    own = seg[8 : t + 8]
    entering = jnp.repeat(seg[7 : t + 7 : CH], CH)
    leaving = jnp.repeat(seg[7 + CH : t + 8 : CH], CH)
    zero8 = jnp.zeros((8,), jnp.int32)
    back = [jnp.concatenate([zero8, (seg[8 - k : t + 8 - k] == own).astype(jnp.int32)]) for k in (3, 2, 1)]
    ahead = [(seg[k : t + 8 + k] == here).astype(jnp.int32) for k in (1, 2, 3)]
    cols = [here, jnp.concatenate([zero8, (entering == own).astype(jnp.int32)]),
            jnp.concatenate([zero8, (leaving == own).astype(jnp.int32)])]
    cols = cols + back + [(here < docs).astype(jnp.int32)] + ahead + [jnp.zeros_like(here)] * 6
    tok_all = jnp.stack(cols, axis=1).astype(f32)
    tok, elink = tok_all[8:], tok_all[:8]
    segr = own.astype(f32)[None]
    u, cot = inputs[0], cotangent[0]
    ue = shift(u[t - 16 :], "seq", 1)

    outs = [
        (rows(TB, d), (t, d), bf16),
        (rows(TB, conv), (t, conv), bf16),
        (rows(TB, conv), (t, conv), bf16),
        (rows(TB, conv), (t, conv), bf16),
        (rows(TB, di), (t, di), bf16),
        (rows(TB, 256), (t, 256), f32),
        (rows(TB, 128), (t, 128), f32),
        (pl.BlockSpec((32, TB), lambda i, s: (0, i)), (32, t), f32),
        (pl.BlockSpec((nb, n, di), lambda i, s: (i, 0, 0)), (nc, n, di), bf16),
        (pl.BlockSpec((nb, 8, 128), lambda i, s: (i, 0, 0)), (nc, 8, 128), f32),
        (whole((n, di)), (n, di), f32),
        (whole((8, di)), (8, di), f32),
        (whole((16, d)), (16, d), bf16),
        (whole((16, conv)), (16, conv), bf16),
    ]
    ins = [rows(TB, d), whole((16, d)), whole((1, d))] + [whole(v.shape) for v in wx_parts]
    ins += [whole((taps, conv)), whole((1, conv)), whole((1, 128)), whole((1, 128)), rows(TB, 16), whole((256, di))]
    scratch = [
        pltpu.VMEM((d, wide), bf16),
        pltpu.VMEM((TB + 8, conv), f32),
        pltpu.VMEM((n, di), f32),
        pltpu.VMEM((1, 128), f32),
        pltpu.VMEM((2 * TB + 8 * nb, di), f32),
    ]
    (nrm, xbc, xc, slope, xd, dts, cc, ct, st, dbf, end, tot, nrme, xbce) = call(
        front_kernel(nw, di, conv, heads), (nt,), ins, outs, scratch, 15,
        [ids, u, ue, gain_in] + wx_parts + [cw, cb, dtb, nr2, tok, e2], "front")
    incoming = carried(tot, end, 1)

    crow = pl.BlockSpec((32, CH), lambda i, s: (0, i))
    srow = pl.BlockSpec((1, CH), lambda i, s: (0, i))
    bspec, cspec = rows(CH, n, di // n), rows(CH, n, di // n + 1)
    (yin,) = call(
        inner_kernel(heads, di), (nc,),
        [bspec, cspec, rows(CH, di), rows(CH, 128), crow, rows(CH, 16), srow],
        [(rows(CH, di), (t, di), bf16)], [], 10,
        [ids, xc, xc, xd, cc, ct, tok, segr], "inner")

    blk = pl.BlockSpec((nb, n, di), lambda i, s: (i, 0, 0))
    outs = [
        (rows(TB, d), (t, d), bf16),
        (rows(TB, di), (t, di), bf16),
        (rows(TB, di), (t, di), bf16),
        (rows(TB, di), (t, di), bf16),
        (rows(TB, di), (t, di), bf16),
        (rows(TB, d), (t, d), bf16),
        (blk, (nc, n, di), bf16),
        (blk, (nc, n, di), f32),
        (rows(TB, 128), (t, 128), f32),
        (whole((8, di)), (8, di), f32),
        (whole((8, di)), (8, di), f32),
        (whole((n, di)), (n, di), f32),
    ]
    ins = [rows(TB, d), rows(TB, di), rows(TB, di), rows(TB, n, di // n + 1), rows(TB, 128), rows(TB, 16), blk,
           pl.BlockSpec((nb, 8, 128), lambda i, s: (i, 0, 0)), whole((n, di)), rows(TB, d), rows(TB, d)]
    ins += [whole(v.shape) for v in wz_parts + wo_parts]
    ins += [whole((1, di)), whole((1, di)), whole((256, di))]
    scratch = [pltpu.VMEM((d, di), bf16), pltpu.VMEM((di, d), bf16)]
    scratch += [pltpu.VMEM((TB, di), f32)] * 3 + [pltpu.VMEM((TB + 8 * nb, di), f32), pltpu.VMEM((TB, di), bf16)]
    (mixed, gn, dz, dy, edy, e, sf, dcs, rin, g_gate, g_skip, reach) = call(
        gate_kernel(nw, di, d), (nt,), ins, outs, scratch, 25,
        [ids, nrm, yin, xc, xc, cc, tok, st, dbf, incoming, u, cot] + wz_parts + wo_parts + [gain_gate, dsk, e2], "gate")
    gend = carried(tot, reach, -1)

    tn = (((0,), (0,)), ((), ()))
    gw_out = lax.dot_general(gn, e, tn, preferred_element_type=f32).astype(bf16)
    gw_z = lax.dot_general(nrm, dz, tn, preferred_element_type=f32).astype(bf16)

    outs = [
        (rows(CH, di), (t, di), bf16),
        (rows(CH, n), (t, n), f32),
        (rows(CH, n), (t, n), f32),
        (rows(CH, 128), (t, 128), f32),
    ]
    (gxd, dbi, dci, rk) = call(
        inner_back_kernel(heads, di), (nc,),
        [bspec, cspec, rows(CH, di), rows(CH, di), rows(CH, 128), crow, rows(CH, 16), srow],
        outs, [pltpu.VMEM((CH, CH), f32), pltpu.VMEM((128, CH), f32)], 20,
        [ids, xc, xc, xd, dy, cc, ct, tok, segr], "inner_back")

    def rev(block, width, col=0):
        return pl.BlockSpec((block, width), lambda i, s: (nt - 1 - i, col))

    rblk = pl.BlockSpec((nb, n, di), lambda i, s: (nt - 1 - i, 0, 0))
    ins = [rev(TB, di), rev(TB, n, di // n), rev(TB, conv), rev(TB, conv), whole((16, conv)), rev(TB, di),
           rev(TB, 256), rev(TB, 128), rev(TB, 16), whole((8, 16)), rev(TB, di), rev(TB, n), rev(TB, n),
           rev(TB, 128), rev(TB, 128), rev(TB, di), rev(TB, di), rblk, rblk, whole((n, di)),
           whole((taps, conv)), whole((1, di)), whole((1, 128)), whole((256, di))]
    outs = [
        (rev(TB, wide), (t, wide), bf16),
        (whole((16, conv)), (16, conv), bf16),
        (whole((8 * taps, conv)), (8 * taps, conv), f32),
        (whole((8, conv)), (8, conv), f32),
        (whole((8, 128)), (8, 128), f32),
        (whole((8, 128)), (8, 128), f32),
    ]
    scratch = [
        pltpu.VMEM((n, di), f32),
        pltpu.VMEM((2 * TB + 8 * nb, di), f32),
        pltpu.VMEM((TB, di), f32),
        pltpu.VMEM((TB + 8, conv), f32),
        pltpu.VMEM((8, 128), bf16),
        pltpu.VMEM((TB, di), bf16),
        pltpu.VMEM((TB, di), bf16),
    ]
    (gpx, edge, g_cw, g_cb, g_a, g_dt) = call(
        back_kernel(di, conv, heads), (nt,), ins, outs, scratch, 25,
        [ids, xc, xc, slope, xbc, xbce, xd, dts, cc, tok, elink, gxd, dbi, dci, rk, rin, dy, edy, sf, dcs, gend,
         cw, dsk, nr, e2], "back")

    gw_x = lax.dot_general(nrm, gpx, tn, preferred_element_type=f32)
    gw_e = lax.dot_general(nrme, edge, tn, preferred_element_type=f32)
    gw_x = jnp.concatenate([gw_x[:, :conv] + gw_e, gw_x[:, conv : conv + heads]], axis=1).astype(bf16)
    edge_in = shift(edge, "seq", -1)

    ins = [rows(TB, di), rows(TB, wide), whole((16, conv)), rows(TB, d), rows(TB, d)]
    ins += [whole(v.shape) for v in wz_parts + wx_parts] + [whole((1, d))]
    outs = [(rows(TB, d), (t, d), bf16), (whole((8, d)), (8, d), f32)]
    (grad_input, g_gain) = call(
        input_kernel(nw, di, conv, heads), (nt,), ins, outs,
        [pltpu.VMEM((d, di), bf16), pltpu.VMEM((d, wide), bf16)], 12,
        [ids, dz, gpx, edge_in, u, e] + wz_parts + wx_parts + [gain_in], "input")

    r_out, r_z, r_x = reduce_rows(gw_out), reduce_rows(gw_z), reduce_rows(gw_x)
    parts = [
        g_cw.reshape(taps, 8, conv).sum(1).reshape(-1),
        g_cb.sum(0),
        g_a.sum(0)[:heads] * rate[0],
        g_skip.sum(0).reshape(heads, p).sum(1),
        g_dt.sum(0)[:heads],
        g_gain.sum(0),
        g_gate.sum(0),
    ]
    total = lax.psum(jnp.concatenate(parts), ("seq", "wshard"))
    w = lax.axis_index("wshard")
    res, off = [], 0
    for k, part in enumerate(parts):
        v = total[off : off + part.shape[0]]
        off += part.shape[0]
        v = v.reshape(taps, conv) if k == 0 else v
        width = v.shape[-1] // nw
        res.append(lax.dynamic_slice_in_dim(v, w * width, width, axis=v.ndim - 1))
    return (mixed[None], grad_input[None], jnp.concatenate([r_z, r_x], axis=1), r_out) + tuple(res)


def solution(mesh):
    wide = P("wshard", "seq", None)
    mat = P("wshard", None)
    taps = P(None, "wshard")
    vec = P("wshard")
    return jax.shard_map(
        body,
        mesh=mesh,
        in_specs=(wide, wide, mat, mat, mat, taps) + (vec,) * 6,
        out_specs=(wide, wide, mat, mat, taps) + (vec,) * 6,
        check_vma=False,
    )
```

```python
import jax
import jax.numpy as jnp
from jax import lax
from jax.experimental import pallas as pl
from jax.experimental.pallas import tpu as pltpu
from jax.sharding import PartitionSpec as P

f32 = jnp.float32
bf16 = jnp.bfloat16
EPS = 1e-05
LOG2E = 1.4426950408889634
CH = 128
TB = 256
LONGEST = 4096
HIGH = lax.Precision.HIGHEST
VMEM = 60 * 1024 * 1024


def sigmoid(v):
    return 0.5 * jnp.tanh(0.5 * v) + 0.5


def dot(a, b):
    return jnp.dot(a, b, preferred_element_type=f32)


def dot_nt(a, b):
    return lax.dot_general(a, b, (((1,), (1,)), ((), ())), preferred_element_type=f32)


def two(v):
    hi = v.astype(bf16)
    return hi, (v - hi.astype(f32)).astype(bf16)


def spread(v, e2):
    return dot(jnp.concatenate(two(v), axis=1), e2)


def cost(us):
    return pl.CostEstimate(flops=int(us * 1.1e8), bytes_accessed=1 << 20, transcendentals=0)


def call(kernel, grid, ins, outs, scratch, us, args, name):
    return pl.pallas_call(
        kernel,
        grid_spec=pltpu.PrefetchScalarGridSpec(
            num_scalar_prefetch=1,
            grid=grid,
            in_specs=ins,
            out_specs=[o[0] for o in outs],
            scratch_shapes=scratch,
        ),
        out_shape=[jax.ShapeDtypeStruct(o[1], o[2]) for o in outs],
        compiler_params=pltpu.CompilerParams(
            vmem_limit_bytes=VMEM, dimension_semantics=("arbitrary",)
        ),
        cost_estimate=cost(us),
        name=name,
    )(*args)


def rows(block, cols, col=0):
    return pl.BlockSpec((block, cols), lambda i, s: (i, col))


def whole(shape):
    return pl.BlockSpec(shape, lambda i, s: (0,) * len(shape))


def norm_rows(uf, gain):
    scale = lax.rsqrt(jnp.mean(uf * uf, axis=-1, keepdims=True) + EPS)
    return (uf * scale * gain).astype(bf16)


def place(buf, ids, parts, width):
    for j, part in enumerate(parts):
        n = part.shape[0]
        at = pl.multiple_of(ids[j] * n, 64)
        buf[pl.ds(at, n), :width] = part[...]


def front_kernel(np_, di, conv, heads):
    def kernel(ids, u, ue, gain, *rest):
        parts = rest[:np_]
        (cw, cb, dtb, nr, tok, e2, nrm_o, xbc_o, xc_o, slope_o, xd_o, dts_o, cc_o, ct_o,
         st_o, db_o, end_o, tot_o, nrme_o, xbce_o, wbuf, ext, state, kd, sp) = rest[np_:]
        i = pl.program_id(0)
        n = (conv - di) // 2

        @pl.when(i == 0)
        def _():
            wbuf[:, conv:] = jnp.zeros((wbuf.shape[0], wbuf.shape[1] - conv), bf16)
            place(wbuf, ids, parts, conv + heads)
            nrme = norm_rows(ue[...].astype(f32), gain[...])
            nrme_o[...] = nrme
            pe = dot(nrme, wbuf[:, :conv]).astype(bf16)
            xbce_o[...] = pe
            ext[0:8, :] = pe.astype(f32)[8:16]
            state[...] = jnp.zeros_like(state)
            kd[...] = jnp.ones_like(kd)

        nrm = norm_rows(u[...].astype(f32), gain[...])
        nrm_o[...] = nrm
        pd = dot(nrm, wbuf[:, conv:])
        for c0 in range(0, conv, 256):
            px = dot(nrm, wbuf[:, c0 : c0 + 256]).astype(bf16)
            xbc_o[:, c0 : c0 + 256] = px
            ext[8 : 8 + TB, c0 : c0 + 256] = px.astype(f32)
        sh = pd + dtb[...]
        dt = jnp.maximum(sh, 0.0) + jnp.log1p(jnp.exp(-jnp.abs(sh)))
        dts_o[:, :128] = dt
        dts_o[:, 128:] = jax.nn.sigmoid(sh)
        a2 = dt * nr[...]
        ri = lax.broadcasted_iota(jnp.int32, (CH, CH), 0)
        ci = lax.broadcasted_iota(jnp.int32, (CH, CH), 1)
        low = (ri >= ci).astype(f32)
        pieces = [dt]
        leaves = []
        for k in range(TB // CH):
            r = slice(k * CH, (k + 1) * CH)
            c2 = jnp.dot(low, a2[r], precision=HIGH, preferred_element_type=f32)
            cc_o[r, :] = c2
            ct_o[:, r] = c2.T[: ct_o.shape[0], :]
            pieces.append(jnp.exp2(c2[CH - 1 :] - c2) * tok[r, 2:3])
            leaves.append(jnp.exp2(c2[CH - 1 :]) * tok[(k + 1) * CH - 1 : (k + 1) * CH, 1:2])
        lv = jnp.concatenate([jnp.broadcast_to(v, (8, 128)) for v in leaves], axis=0)
        sp[...] = spread(jnp.concatenate(pieces + [lv], axis=0), e2[...])
        for r0 in range(0, TB, 64):
            l0, l1, l2 = tok[r0 : r0 + 64, 3:4], tok[r0 : r0 + 64, 4:5], tok[r0 : r0 + 64, 5:6]
            for c0 in range(0, conv, 256):
                c = slice(c0, c0 + 256)
                pre = cb[:, c] + cw[3:4, c] * ext[8 + r0 : 72 + r0, c]
                pre = pre + cw[2:3, c] * (ext[7 + r0 : 71 + r0, c] * l2)
                pre = pre + cw[1:2, c] * (ext[6 + r0 : 70 + r0, c] * l1)
                pre = pre + cw[0:1, c] * (ext[5 + r0 : 69 + r0, c] * l0)
                sg = sigmoid(pre)
                xc = pre * sg
                xc_o[r0 : r0 + 64, c] = xc.astype(bf16)
                slope_o[r0 : r0 + 64, c] = (sg + xc * (1.0 - sg)).astype(bf16)
                if c0 < di:
                    xd_o[r0 : r0 + 64, c] = (xc * sp[r0 : r0 + 64, c]).astype(bf16)
        ext[0:8, :] = ext[TB : TB + 8, :]
        for k in range(TB // CH):
            r = slice(k * CH, (k + 1) * CH)
            st_o[k] = state[...].astype(bf16)
            db_o[k] = jnp.broadcast_to(kd[...], (8, 128))
            bt = xc_o[r, di : di + n].astype(f32).T.astype(bf16)
            for c0 in range(0, di, 256):
                c = slice(c0, c0 + 256)
                xw = (xd_o[r, c].astype(f32) * sp[TB + k * CH : TB + (k + 1) * CH, c]).astype(bf16)
                lvr = sp[2 * TB + 8 * k : 2 * TB + 8 * k + 1, c]
                state[:, c] = lvr * state[:, c] + dot(bt, xw)
            kd[...] = kd[...] * leaves[k]

        @pl.when(i == pl.num_programs(0) - 1)
        def _():
            end_o[...] = state[...]
            tot_o[...] = spread(jnp.broadcast_to(kd[...], (8, 128)), e2[...])

    return kernel


def inner_kernel(heads, di):
    p = di // heads
    per = 128 // p

    def kernel(ids, b, c, xd, cc, ct, tok, segr, y_o):
        s = dot_nt(c[...], b[...])
        ri = lax.broadcasted_iota(jnp.int32, (CH, CH), 0)
        ci = lax.broadcasted_iota(jnp.int32, (CH, CH), 1)
        bias = jnp.where((tok[:, 0:1] == segr[...]) & (ri >= ci), 0.0, -1e30)
        lanes = lax.broadcasted_iota(jnp.int32, (1, 128), 1) // p
        for j in range(heads // per):
            xp = xd[:, 128 * j : 128 * j + 128]
            ms, xs = [], []
            for q in range(per):
                h = per * j + q
                e = jnp.exp2(cc[:, h : h + 1] - ct[h : h + 1, :] + bias)
                ms.append((s * e).astype(bf16))
                xs.append(xp * (lanes == q).astype(f32).astype(bf16))
            out = dot(jnp.concatenate(ms, axis=1), jnp.concatenate(xs, axis=0))
            y_o[:, 128 * j : 128 * j + 128] = out.astype(bf16)

    return kernel


def gate_kernel(np_, di, d):
    def kernel(ids, nrm, yin, x, c_in, cc, tok, st, db, inc, u, cot, *rest):
        wz, wo = rest[:np_], rest[np_ : 2 * np_]
        (gain, dsk, e2, mixed_o, gn_o, dz_o, dy_o, edy_o, e_o, sf_o, dc_o, rin_o, gg_o, gs_o,
         rg_o, zbuf, obuf, z, yi, dgn, ee, pr) = rest[2 * np_ :]
        i = pl.program_id(0)

        @pl.when(i == 0)
        def _():
            place(zbuf, ids, wz, di)
            place(obuf, ids, wo, d)
            gg_o[...] = jnp.zeros_like(gg_o)
            gs_o[...] = jnp.zeros_like(gs_o)
            rg_o[...] = jnp.zeros_like(rg_o)

        keep = tok[:, 6:7]
        ef = cot[...].astype(f32) * keep
        e = ef.astype(bf16)
        e_o[...] = e
        nb = TB // CH
        ents = []
        for k in range(nb):
            r = slice(k * CH, (k + 1) * CH)
            ents.append(jnp.exp2(cc[r, :]) * tok[r, 1:2])
        ee[...] = spread(jnp.concatenate(ents + [db[k] for k in range(nb)], axis=0), e2[...])
        for k in range(nb):
            r = slice(k * CH, (k + 1) * CH)
            for c0 in range(0, di, 256):
                c = slice(c0, c0 + 256)
                dbr = ee[TB + 8 * k : TB + 8 * k + 1, c]
                sf = (st[k, :, c].astype(f32) + dbr * inc[:, c].astype(f32)).astype(bf16)
                sf_o[k, :, c] = sf
                yi[r, c] = dot(c_in[r, :], sf)
        z[...] = dot(nrm[...], zbuf[...])
        dgn[...] = dot_nt(e, obuf[...])

        def strip(t, carry):
            r = pl.ds(pl.multiple_of(t * 16, 16), 16)
            xs = x[r, :].astype(f32)
            eyi = ee[r, :] * yi[r, :]
            y = yin[r, :].astype(f32) + eyi + dsk[...] * xs
            zz = z[r, :]
            sg = sigmoid(zz)
            act = zz * sg
            g = y * act
            scale = lax.rsqrt(jnp.mean(g * g, axis=-1, keepdims=True) + EPS)
            ug = g * scale
            gn_o[r, :] = (ug * gain[...]).astype(bf16)
            dg0 = dgn[r, :]
            pg = dg0 * ug
            gg_o[...] += pg[0:8] + pg[8:16]
            dn = dg0 * gain[...]
            m = jnp.mean(dn * ug, axis=-1, keepdims=True)
            dg = scale * (dn - ug * m)
            dy = dg * act
            dz_o[r, :] = (dg * y * (sg + act * (1.0 - sg))).astype(bf16)
            dy_o[r, :] = dy.astype(bf16)
            ps = xs * dy
            gs_o[...] += ps[0:8] + ps[8:16]
            edy_o[r, :] = (dy * ee[r, :]).astype(bf16)
            pr[r, :] = (dy * eyi).astype(bf16)
            return carry

        lax.fori_loop(0, TB // 16, strip, 0)
        rin_o[...] = dot_nt(pr[...], e2[0:128, :])
        mixed_o[...] = (keep * (u[...].astype(f32) + dot(gn_o[...], obuf[...]))).astype(bf16)
        for k in range(nb):
            r = slice(k * CH, (k + 1) * CH)
            ctr = c_in[r, :].astype(f32).T.astype(bf16)
            for c0 in range(0, di, 256):
                c = slice(c0, c0 + 256)
                dcv = dot(ctr, edy_o[r, c])
                dc_o[k, :, c] = dcv
                rg_o[:, c] += ee[TB + 8 * k : TB + 8 * k + 1, c] * dcv

    return kernel


def inner_back_kernel(p, h0, h1):
    per = 128 // p

    def kernel(ids, b, c, xd, dy, cc, ct, tok, segr, gxd_o, db_o, dc_o, rk_o, rr):
        st = dot_nt(b[...], c[...])
        si = lax.broadcasted_iota(jnp.int32, (CH, CH), 0)
        ti = lax.broadcasted_iota(jnp.int32, (CH, CH), 1)
        bias = jnp.where((tok[:, 0:1] == segr[...]) & (ti >= si), 0.0, -1e30)
        lanes = lax.broadcasted_iota(jnp.int32, (1, 128), 1) // p
        rr[...] = jnp.zeros_like(rr)
        rk_o[...] = jnp.zeros_like(rk_o)
        gsum = jnp.zeros((CH, CH), f32)
        for j in range((h1 - h0) // per):
            xp = xd[:, 128 * j : 128 * j + 128]
            dyp = dy[:, 128 * j : 128 * j + 128]
            dys = jnp.concatenate(
                [dyp * (lanes == q).astype(f32).astype(bf16) for q in range(per)], axis=0
            )
            gm = dot_nt(xp, dys)
            ms = []
            for q in range(per):
                h = h0 + per * j + q
                e = jnp.exp2(ct[h : h + 1, :] - cc[:, h : h + 1] + bias)
                ms.append((st * e).astype(bf16))
                ge = gm[:, q * CH : (q + 1) * CH] * e
                gsum = gsum + ge
                ex = ge * st
                rr[h : h + 1, :] = jnp.sum(ex, axis=0, keepdims=True)
                rk_o[:, h : h + 1] = jnp.sum(ex, axis=1, keepdims=True)
            out = dot(jnp.concatenate(ms, axis=1), dys)
            gxd_o[:, 128 * j : 128 * j + 128] = out.astype(bf16)
        rk_o[...] = rr[...].T - rk_o[...]
        db_o[...] = dot(gsum.astype(bf16), c[...])
        dc_o[...] = dot(gsum.T.astype(bf16), b[...])

    return kernel


def back_kernel(w, n, h0, h1, last_part):
    cols = w + 2 * n if last_part else w

    def kernel(ids, x_in, b_in, slope, xbc, xbce, xd, dts, cc, tok, elink, gxd, dbi, dci, rk, rin,
               dy, edy, sf, dcs, gend, cw, dsk, nr, e2, *rest):
        if last_part:
            slope2, xbc2, xbce2, cw2, dbp, dcp, ddtp = rest[:7]
            gp_o, edge_o, gw_o, gb_o, ga_o, gdt_o = rest[7:13]
        else:
            gp_o, edge_o, gw_o, gb_o, ga_o, gdt_o, dbp_o, dcp_o, ddtp_o = rest[:9]
        ds, sp, sr, ext, xq, xe = rest[-6:]
        i = pl.program_id(0)
        nb = TB // CH

        def pick(a, a2, r, c0):
            return a[r, c0 : c0 + 256] if c0 < w else a2[r, c0 - w : c0 - w + 256]

        @pl.when(i == 0)
        def _():
            ds[...] = gend[...].astype(f32)
            ext[TB : TB + 8, :] = jnp.zeros((8, cols), f32)
            gw_o[...] = jnp.zeros_like(gw_o)
            gb_o[...] = jnp.zeros_like(gb_o)
            ga_o[...] = jnp.zeros_like(ga_o)
            gdt_o[...] = jnp.zeros_like(gdt_o)

        if not last_part:
            slope2 = xbc2 = xbce2 = cw2 = None
        dt = dts[:, :128]
        pieces, leaves = [dt], []
        for k in range(nb):
            r = slice(k * CH, (k + 1) * CH)
            c2 = cc[r, :]
            pieces.append(jnp.exp2(c2[CH - 1 :] - c2) * tok[r, 2:3])
            leaves.append(jnp.exp2(c2[CH - 1 :]) * tok[(k + 1) * CH - 1 : (k + 1) * CH, 1:2])
        lv = jnp.concatenate([jnp.broadcast_to(v, (8, 128)) for v in leaves], axis=0)
        sp[...] = spread(jnp.concatenate(pieces + [lv], axis=0), e2[...])
        lsum = [None] * nb
        for k in reversed(range(nb)):
            r = slice(k * CH, (k + 1) * CH)
            lacc = []
            gb = dbi[r, :]
            gc = dci[r, :]
            for c0 in range(0, w, 256):
                c = slice(c0, c0 + 256)
                dsv = ds[:, c]
                dsb = dsv.astype(bf16)
                sfv = sf[k, :, c]
                sr[r, c] = dot(b_in[r, :], dsb)
                xwv = (xd[r, c].astype(f32) * sp[TB + k * CH : TB + (k + 1) * CH, c]).astype(bf16)
                gb = gb + dot_nt(xwv, dsb)
                gc = gc + dot_nt(edy[r, c], sfv)
                lacc.append(jnp.sum(dsv * sfv.astype(f32), axis=0, keepdims=True))
                lvr = sp[2 * TB + 8 * k : 2 * TB + 8 * k + 1, c]
                ds[:, c] = lvr * dsv + dcs[k, :, c]
            lrow = jnp.broadcast_to(jnp.concatenate(lacc, axis=1), (8, w))
            lhi, llo = two(lrow)
            lsum[k] = (dot_nt(lhi, e2[0:128, :]) + dot_nt(llo, e2[0:128, :]))[0:1]
            if last_part:
                ext[r, w : w + n] = (gb + dbp[r, :]) * slope2[r, :n].astype(f32)
                ext[r, w + n :] = (gc + dcp[r, :]) * slope2[r, n:].astype(f32)
            else:
                dbp_o[r, :] = gb
                dcp_o[r, :] = gc

        def strip(t, carry):
            r = pl.ds(pl.multiple_of(t * 16, 16), 16)
            re = pl.ds(pl.multiple_of(TB + t * 16, 16), 16)
            x = x_in[r, :].astype(f32)
            es = sp[re, :] * sr[r, :]
            q = gxd[r, :].astype(f32) + es
            gx = sp[r, :] * q + dsk[...] * dy[r, :].astype(f32)
            ext[r, 0:w] = gx * slope[r, :].astype(f32)
            xq[r, :] = (x * q).astype(bf16)
            xe[r, :] = (x * es).astype(bf16)
            return carry

        lax.fori_loop(0, TB // 16, strip, 0)
        gdt = dot_nt(xq[...], e2[0:128, :])
        et = dot_nt(xe[...], e2[0:128, :]) * dt
        ri = lax.broadcasted_iota(jnp.int32, (CH, CH), 0)
        ci = lax.broadcasted_iota(jnp.int32, (CH, CH), 1)
        hl = lax.broadcasted_iota(jnp.int32, (1, 128), 1)
        hm = ((hl >= h0) & (hl < h1)).astype(f32)
        tri = jnp.concatenate([(ci >= ri).astype(f32), (ci < ri).astype(f32)], axis=1)
        for k in range(nb):
            r = slice(k * CH, (k + 1) * CH)
            v = jnp.concatenate([rk[r, :] + rin[r, :] * hm, et[r]], axis=0)
            ga = jnp.dot(tri, v, precision=HIGH, preferred_element_type=f32) + lsum[k] * leaves[k]
            ddt = (gdt[r] + ga * nr[...]) * dts[r, 128:]
            gad = ga * dts[r, :128]
            acc_a, acc_d = gad[0:8], ddt[0:8]
            for q in range(8, CH, 8):
                acc_a = acc_a + gad[q : q + 8]
                acc_d = acc_d + ddt[q : q + 8]
            ga_o[...] += acc_a
            gdt_o[...] += acc_d
            if last_part:
                gp_o[r, cols:] = (ddt + ddtp[r, :]).astype(bf16)
            else:
                ddtp_o[r, :] = ddt
        for r0 in range(0, TB, 64):
            rs = slice(r0, r0 + 64)
            for c0 in range(0, cols, 256):
                c = slice(c0, c0 + 256)
                g0 = ext[rs, c]
                xb = pick(xbc, xbc2, rs, c0).astype(f32)
                gsum = pick(cw, cw2, slice(3, 4), c0) * g0
                ws = [None, None, None, g0 * xb]
                for s in (1, 2, 3):
                    gs = ext[r0 + s : r0 + s + 64, c] * tok[rs, 6 + s : 7 + s]
                    gsum = gsum + pick(cw, cw2, slice(3 - s, 4 - s), c0) * gs
                    ws[3 - s] = gs * xb
                gp_o[rs, c] = gsum.astype(bf16)
                gb = g0[0:8]
                for q in range(8, 64, 8):
                    gb = gb + g0[q : q + 8]
                gb_o[:, c] += gb
                for o in range(4):
                    v = ws[o][0:8]
                    for q in range(8, 64, 8):
                        v = v + ws[o][q : q + 8]
                    gw_o[8 * o : 8 * o + 8, c] += v
        ext[TB : TB + 8, :] = ext[0:8, :]

        @pl.when(i == pl.num_programs(0) - 1)
        def _():
            zero = jnp.zeros((8, 256), f32)
            for c0 in range(0, cols, 256):
                c = slice(c0, c0 + 256)
                xb = pick(xbce, xbce2, slice(8, 16), c0).astype(f32)
                ext[8:16, c] = ext[TB : TB + 8, c]
                ext[0:8, c] = zero
                gsum = zero
                for s in (1, 2, 3):
                    gs = ext[s : s + 8, c] * elink[:, 6 + s : 7 + s]
                    gsum = gsum + pick(cw, cw2, slice(3 - s, 4 - s), c0) * gs
                    gw_o[8 * (3 - s) : 8 * (3 - s) + 8, c] += gs * xb
                edge_o[:, c] = jnp.concatenate([zero, gsum], axis=0).astype(bf16)

    return kernel


def input_kernel(np_, di, conv, heads):
    def kernel(ids, gpz, gpa, gpb, ea, eb, u, e, *rest):
        wz, wx = rest[:np_], rest[np_ : 2 * np_]
        gain, gi_o, gg_o, zbuf, xbuf = rest[2 * np_ :]
        i = pl.program_id(0)

        @pl.when(i == 0)
        def _():
            xbuf[:, conv:] = jnp.zeros((xbuf.shape[0], xbuf.shape[1] - conv), bf16)
            place(zbuf, ids, wz, di)
            place(xbuf, ids, wx, conv + heads)
            gg_o[...] = jnp.zeros_like(gg_o)

        wa = gpa.shape[1]
        gn = dot_nt(gpz[...], zbuf[...]) + dot_nt(gpa[...], xbuf[:, :wa]) + dot_nt(gpb[...], xbuf[:, wa:])
        last = (i == pl.num_programs(0) - 1).astype(f32)
        tail = (dot_nt(ea[...], xbuf[:, :wa]) + dot_nt(eb[...], xbuf[:, wa:conv])) * last
        gn = jnp.concatenate([gn[: TB - 16], gn[TB - 16 :] + tail], axis=0)
        uf = u[...].astype(f32)
        scale = lax.rsqrt(jnp.mean(uf * uf, axis=-1, keepdims=True) + EPS)
        unit = uf * scale
        pg = gn * unit
        acc = pg[0:8]
        for q in range(8, TB, 8):
            acc = acc + pg[q : q + 8]
        gg_o[...] += acc
        dn = gn * gain[...]
        m = jnp.mean(dn * unit, axis=-1, keepdims=True)
        gi_o[...] = (e[...].astype(f32) + scale * (dn - unit * m)).astype(bf16)

    return kernel


def swap(v, axis, bit):
    return lax.ppermute(v, axis, [(k, k ^ bit) for k in range(lax.axis_size(axis))])


def shift(v, axis, steps):
    n = lax.axis_size(axis)
    return lax.ppermute(v, axis, [(k, k + steps) for k in range(n) if 0 <= k + steps < n])


def bits_of(n):
    return [1 << k for k in reversed(range((n - 1).bit_length()))]


def after(v, dep):
    return lax.optimization_barrier((v, dep))[0]


def gather_parts(v, axis):
    parts = [v]
    for bit in bits_of(lax.axis_size(axis)):
        parts = parts + [swap(p, axis, bit) for p in parts]
    return parts


def in_order(parts, axis):
    at = lax.axis_index(axis)
    n = lax.axis_size(axis)
    v = jnp.stack(parts)
    rest = v.shape[1:]
    bits = bits_of(n)
    v = v.reshape((2,) * len(bits) + rest)
    for k, bit in enumerate(reversed(bits)):
        v = jnp.where((at // bit) % 2 == 0, v, jnp.flip(v, k))
    order = tuple(reversed(range(len(bits))))
    return v.transpose(order + tuple(range(len(bits), v.ndim))).reshape((n,) + rest)


def part_ids(axis):
    ids = [lax.axis_index(axis)]
    for bit in bits_of(lax.axis_size(axis)):
        ids = ids + [k ^ bit for k in ids]
    return ids


def reduce_steps(gs):
    nw, ns = lax.axis_size("wshard"), lax.axis_size("seq")
    w, s = lax.axis_index("wshard"), lax.axis_index("seq")
    n = min(g.shape[0] for g in gs) // nw

    def pick(at):
        out = []
        for g in gs:
            v = g.reshape(nw // 2, 2, -1, g.shape[-1])
            v = lax.dynamic_index_in_dim(v, at, 1, keepdims=False)
            k = v.shape[1] // n
            out += [v[:, q * n : (q + 1) * n] for q in range(k)]
        return jnp.concatenate(out, axis=2) if len(out) > 1 else out[0]

    def add(a, b):
        return (a.astype(f32) + b.astype(f32)).astype(bf16)

    steps = [("wshard", 1 << k) for k in range(1, (nw - 1).bit_length())]
    steps += [("seq", 1 << k) for k in range((ns - 1).bit_length())]
    send, keep = pick(1 - w % 2), pick(w % 2)
    yield send
    v = add(keep, swap(send, "wshard", 1))
    for axis, bit in steps:
        at = ((w if axis == "wshard" else s) // bit) % 2
        if axis == "wshard":
            v = v.reshape(-1, 2, n, v.shape[-1]).swapaxes(0, 1)
        else:
            v = v.reshape(2, -1, v.shape[-1])
        send = lax.dynamic_index_in_dim(v, 1 - at, 0, keepdims=False)
        keep = lax.dynamic_index_in_dim(v, at, 0, keepdims=False)
        yield send
        v = add(keep, swap(send, axis, bit))
    for bit in bits_of(ns):
        yield v
        got = swap(v, "seq", bit)
        first = (s // bit) % 2 == 0
        v = jnp.concatenate([jnp.where(first, v, got), jnp.where(first, got, v)], axis=0)
    yield v.astype(f32)


def reduce_small(v):
    for axis in ("wshard", "seq"):
        for bit in reversed(bits_of(lax.axis_size(axis))):
            v = v + swap(v, axis, bit)
    return v


def pack_state(decay, state):
    hi, lo = two(decay)
    return jnp.concatenate([state.astype(bf16), hi, lo], axis=0)


def unpack_state(v, n):
    return v[n : n + 8].astype(f32)[:1] + v[n + 8 : n + 16].astype(f32)[:1], v[:n].astype(f32)


def carried(decay, state, sign, tokens):
    n = state.shape[0]
    span = 1
    while span < -(-LONGEST // tokens):
        d, s = unpack_state(shift(pack_state(decay, state), "seq", sign * span), n)
        state = state + decay[:1] * s
        decay = decay * d
        span *= 2
    return shift(state.astype(bf16), "seq", sign)


def body(inputs, cotangent, lengths, in_proj, out_proj, conv_weight, conv_bias, a_log, d_skip,
         dt_bias, norm_gain, gate_gain):
    t, d = inputs.shape[1:]
    nw = lax.axis_size("wshard")
    di = out_proj.shape[0] * nw
    heads = a_log.shape[0] * nw
    conv = conv_bias.shape[0] * nw
    taps = conv_weight.shape[0]
    n = (conv - di) // 2
    p = di // heads
    docs = lengths.shape[1]
    nt, nc, nb = t // TB, t // CH, TB // CH
    wide = conv + 128
    wx, wz = in_proj[:, di:], in_proj[:, :di]
    pc = conv // nw
    width = -(-max(pc, di // nw, 384) // 128) * 128

    def line(*vs):
        vs = [v if v.ndim == 2 else v[None] for v in vs]
        vs = [jnp.pad(v, ((0, 0), (0, (width if k == len(vs) - 1 else 128 * (k + 1)) - 128 * k - v.shape[1])))
              for k, v in enumerate(vs)]
        return jnp.concatenate(vs, axis=1)

    small = jnp.concatenate(
        [line(conv_weight), line(conv_bias), line(gate_gain), line(norm_gain), line(a_log, d_skip, dt_bias)], axis=0)
    small = in_order(gather_parts(small, "wshard"), "wshard").astype(f32)
    wx_parts = gather_parts(wx, "wshard")
    wz_parts = gather_parts(after(wz, wx_parts[1]), "wshard")
    wo_parts = gather_parts(after(out_proj, wx_parts[1]), "wshard")
    ids = jnp.stack(part_ids("wshard")).astype(jnp.int32)
    hw = heads // nw
    cw = small[:, :taps, :pc].swapaxes(0, 1).reshape(taps, conv)
    cb = small[:, taps, :pc].reshape(1, conv)
    gain_gate = small[:, taps + 1, : di // nw].reshape(1, di)
    gain_in = small[:, taps + 2, : d // nw].reshape(1, d)
    log_rate, skip, dtb = [small[:, taps + 3, 128 * k : 128 * k + hw].reshape(1, heads) for k in range(3)]
    rate = -jnp.exp(log_rate)
    pad = ((0, 0), (0, 128 - heads))
    nr = jnp.pad(rate, pad)
    nr2 = nr * LOG2E
    dtb = jnp.pad(dtb, pad)
    dsk = jnp.repeat(skip, p, axis=1)
    head_of = jnp.arange(di, dtype=jnp.int32) // p
    e1 = (jnp.arange(128, dtype=jnp.int32)[:, None] == head_of[None]).astype(bf16)
    e2 = jnp.concatenate([e1, e1], axis=0)
    first = lax.axis_index("seq") * t
    pos = first - 8 + jnp.arange(t + 16, dtype=jnp.int32)
    ends = jnp.cumsum(lengths[0], dtype=jnp.int32)
    seg = jnp.sum((pos[:, None] >= ends[None]).astype(jnp.int32), axis=1)
    seg = jnp.where(pos < 0, -1, seg)
    here = seg[: t + 8]
    own = seg[8 : t + 8]
    entering = jnp.repeat(seg[7 : t + 7 : CH], CH)
    leaving = jnp.repeat(seg[7 + CH : t + 8 : CH], CH)
    zero8 = jnp.zeros((8,), jnp.int32)
    back = [jnp.concatenate([zero8, (seg[8 - k : t + 8 - k] == own).astype(jnp.int32)]) for k in (3, 2, 1)]
    ahead = [(seg[k : t + 8 + k] == here).astype(jnp.int32) for k in (1, 2, 3)]
    cols = [here, jnp.concatenate([zero8, (entering == own).astype(jnp.int32)]),
            jnp.concatenate([zero8, (leaving == own).astype(jnp.int32)])]
    cols = cols + back + [(here < docs).astype(jnp.int32)] + ahead + [jnp.zeros_like(here)] * 6
    tok_all = jnp.stack(cols, axis=1).astype(f32)
    tok, elink = tok_all[8:], tok_all[:8]
    segr = own.astype(f32)[None]
    u, cot = inputs[0], cotangent[0]
    ue = shift(u[t - 16 :], "seq", 1)

    outs = [
        (rows(TB, d), (t, d), bf16),
        (rows(TB, conv), (t, conv), bf16),
        (rows(TB, conv), (t, conv), bf16),
        (rows(TB, conv), (t, conv), bf16),
        (rows(TB, di), (t, di), bf16),
        (rows(TB, 256), (t, 256), f32),
        (rows(TB, 128), (t, 128), f32),
        (pl.BlockSpec((32, TB), lambda i, s: (0, i)), (32, t), f32),
        (pl.BlockSpec((nb, n, di), lambda i, s: (i, 0, 0)), (nc, n, di), bf16),
        (pl.BlockSpec((nb, 8, 128), lambda i, s: (i, 0, 0)), (nc, 8, 128), f32),
        (whole((n, di)), (n, di), f32),
        (whole((8, di)), (8, di), f32),
        (whole((16, d)), (16, d), bf16),
        (whole((16, conv)), (16, conv), bf16),
    ]
    ins = [rows(TB, d), whole((16, d)), whole((1, d))] + [whole(v.shape) for v in wx_parts]
    ins += [whole((taps, conv)), whole((1, conv)), whole((1, 128)), whole((1, 128)), rows(TB, 16), whole((256, di))]
    scratch = [
        pltpu.VMEM((d, wide), bf16),
        pltpu.VMEM((TB + 8, conv), f32),
        pltpu.VMEM((n, di), f32),
        pltpu.VMEM((1, 128), f32),
        pltpu.VMEM((2 * TB + 8 * nb, di), f32),
    ]
    (nrm, xbc, xc, slope, xd, dts, cc, ct, st, dbf, end, tot, nrme, xbce) = call(
        front_kernel(nw, di, conv, heads), (nt,), ins, outs, scratch, 15,
        [ids, u, ue, gain_in] + wx_parts + [cw, cb, dtb, nr2, tok, e2], "front")
    incoming = carried(tot, end, 1, t)

    crow = pl.BlockSpec((32, CH), lambda i, s: (0, i))
    srow = pl.BlockSpec((1, CH), lambda i, s: (0, i))
    bspec, cspec = rows(CH, n, di // n), rows(CH, n, di // n + 1)
    (yin,) = call(
        inner_kernel(heads, di), (nc,),
        [bspec, cspec, rows(CH, di), rows(CH, 128), crow, rows(CH, 16), srow],
        [(rows(CH, di), (t, di), bf16)], [], 10,
        [ids, xc, xc, xd, cc, ct, tok, segr], "inner")

    blk = pl.BlockSpec((nb, n, di), lambda i, s: (i, 0, 0))
    outs = [
        (rows(TB, d), (t, d), bf16),
        (rows(TB, di), (t, di), bf16),
        (rows(TB, di), (t, di), bf16),
        (rows(TB, di), (t, di), bf16),
        (rows(TB, di), (t, di), bf16),
        (rows(TB, d), (t, d), bf16),
        (blk, (nc, n, di), bf16),
        (blk, (nc, n, di), f32),
        (rows(TB, 128), (t, 128), f32),
        (whole((8, di)), (8, di), f32),
        (whole((8, di)), (8, di), f32),
        (whole((n, di)), (n, di), f32),
    ]
    ins = [rows(TB, d), rows(TB, di), rows(TB, di), rows(TB, n, di // n + 1), rows(TB, 128), rows(TB, 16), blk,
           pl.BlockSpec((nb, 8, 128), lambda i, s: (i, 0, 0)), whole((n, di)), rows(TB, d), rows(TB, d)]
    ins += [whole(v.shape) for v in wz_parts + wo_parts]
    ins += [whole((1, di)), whole((1, di)), whole((256, di))]
    scratch = [pltpu.VMEM((d, di), bf16), pltpu.VMEM((di, d), bf16)]
    scratch += [pltpu.VMEM((TB, di), f32)] * 3 + [pltpu.VMEM((TB + 8 * nb, di), f32), pltpu.VMEM((TB, di), bf16)]
    (mixed, gn, dz, dy, edy, e, sf, dcs, rin, g_gate, g_skip, reach) = call(
        gate_kernel(nw, di, d), (nt,), ins, outs, scratch, 25,
        [ids, nrm, yin, xc, xc, cc, tok, st, dbf, incoming, u, cot] + wz_parts + wo_parts + [gain_gate, dsk, e2], "gate")
    gend = carried(tot, reach, -1, t)

    tn = (((0,), (0,)), ((), ()))
    gw_out = lax.dot_general(gn, e, tn, preferred_element_type=f32).astype(bf16)
    gw_z = lax.dot_general(nrm, dz, tn, preferred_element_type=f32).astype(bf16)

    oz = reduce_steps([gw_out, gw_z])
    oz_out = next(oz)
    hh, hw2 = heads // 2, di // 2

    def half_inner(k, dep):
        outs = [
            (rows(CH, hw2), (t, hw2), bf16),
            (rows(CH, n), (t, n), f32),
            (rows(CH, n), (t, n), f32),
            (rows(CH, 128), (t, 128), f32),
        ]
        return call(
            inner_back_kernel(p, hh * k, hh * (k + 1)), (nc,),
            [bspec, cspec, rows(CH, hw2, k), rows(CH, hw2, k), rows(CH, 128), crow, rows(CH, 16), srow],
            outs, [pltpu.VMEM((128, CH), f32)], 12,
            [ids, xc, xc, xd, after(dy, dep), cc, ct, tok, segr], "inner_back")

    def rev(block, width, col=0):
        return pl.BlockSpec((block, width), lambda i, s: (nt - 1 - i, col))

    def at(shape, col):
        return pl.BlockSpec(shape, lambda i, s: (0, col))

    def half_back(k, inner, dep, extra):
        gxd, dbi, dci, rk = inner
        last = k == 1
        cols = hw2 + 2 * n if last else hw2
        rblk = pl.BlockSpec((nb, n, hw2), lambda i, s: (nt - 1 - i, 0, k))
        ins = [rev(TB, hw2, k), rev(TB, n, di // n), rev(TB, hw2, k), rev(TB, hw2, k), at((16, hw2), k),
               rev(TB, hw2, k), rev(TB, 256), rev(TB, 128), rev(TB, 16), whole((8, 16)), rev(TB, hw2),
               rev(TB, n), rev(TB, n), rev(TB, 128), rev(TB, 128), rev(TB, hw2, k), rev(TB, hw2, k), rblk, rblk,
               at((n, hw2), k), at((taps, hw2), k), at((1, hw2), k), whole((1, 128)), at((256, hw2), k)]
        args = [ids, xc, xc, slope, xbc, xbce, xd, dts, cc, tok, elink, after(gxd, dep), dbi, dci, rk, rin, dy,
                edy, sf, dcs, gend, cw, dsk, nr, e2]
        outs = [
            (rev(TB, cols + 128 * last), (t, cols + 128 * last), bf16),
            (whole((16, cols)), (16, cols), bf16),
            (whole((8 * taps, cols)), (8 * taps, cols), f32),
            (whole((8, cols)), (8, cols), f32),
            (whole((8, 128)), (8, 128), f32),
            (whole((8, 128)), (8, 128), f32),
        ]
        if last:
            ins += [rev(TB, 2 * n, di // (2 * n)), rev(TB, 2 * n, di // (2 * n)), at((16, 2 * n), di // (2 * n)),
                    at((taps, 2 * n), di // (2 * n)), rev(TB, n), rev(TB, n), rev(TB, 128)]
            args += [slope, xbc, xbce, cw] + list(extra)
        else:
            outs += [(rev(TB, n), (t, n), f32), (rev(TB, n), (t, n), f32), (rev(TB, 128), (t, 128), f32)]
        scratch = [
            pltpu.VMEM((n, hw2), f32),
            pltpu.VMEM((2 * TB + 8 * nb, hw2), f32),
            pltpu.VMEM((TB, hw2), f32),
            pltpu.VMEM((TB + 8, cols), f32),
            pltpu.VMEM((TB, hw2), bf16),
            pltpu.VMEM((TB, hw2), bf16),
        ]
        return call(back_kernel(hw2, n, hh * k, hh * (k + 1), last), (nt,), ins, outs, scratch, 15, args, "back")

    in_a = half_inner(0, oz_out)
    oz_out = next(oz, oz_out)
    in_b = half_inner(1, (oz_out, in_a[0]))
    (gpa, edge_a, gw_a, gb_a, ga_a, gdt_a, dbp, dcp, ddtp) = half_back(0, in_a, in_b[0], None)
    oz_out = next(oz, oz_out)
    (gpb, edge_b, gw_b, gb_b, ga_b, gdt_b) = half_back(1, in_b, (oz_out, gpa), (dbp, dcp, ddtp))
    oz_out = next(oz, oz_out)

    gw_xa = lax.dot_general(nrm, gpa, tn, preferred_element_type=f32)
    gw_xa = (gw_xa + lax.dot_general(nrme, edge_a, tn, preferred_element_type=f32)).astype(bf16)
    gw_xb = lax.dot_general(nrm, after(gpb, oz_out), tn, preferred_element_type=f32)
    cb2 = conv - hw2
    gw_xe = lax.dot_general(nrme, edge_b, tn, preferred_element_type=f32)
    gw_xb = jnp.concatenate([gw_xb[:, :cb2] + gw_xe, gw_xb[:, cb2 : cb2 + heads]], axis=1).astype(bf16)
    ea_in, eb_in = shift(edge_a, "seq", -1), shift(edge_b, "seq", -1)

    ins = [rows(TB, di), rows(TB, hw2), rows(TB, wide - hw2), whole((16, hw2)), whole((16, cb2)), rows(TB, d), rows(TB, d)]
    ins += [whole(v.shape) for v in wz_parts + wx_parts] + [whole((1, d))]
    outs = [(rows(TB, d), (t, d), bf16), (whole((8, d)), (8, d), f32)]
    x_chain = reduce_steps([gw_xa, gw_xb])
    x_out = next(x_chain)
    (grad_input, g_gain) = call(
        input_kernel(nw, di, conv, heads), (nt,), ins, outs,
        [pltpu.VMEM((d, di), bf16), pltpu.VMEM((d, wide), bf16)], 12,
        [ids, dz, after(gpa, x_out), gpb, ea_in, eb_in, u, e] + wz_parts + wx_parts + [gain_in], "input")
    g_cw = jnp.concatenate([gw_a, gw_b], axis=1)
    g_cb = jnp.concatenate([gb_a, gb_b], axis=1)
    g_a, g_dt = ga_a + ga_b, gdt_a + gdt_b
    next(x_chain)
    x_out = next(x_chain)
    r_oz, r_x = list(oz)[-1], list(x_chain)[-1]
    k = r_oz.shape[1] - di
    r_out = jnp.concatenate([r_oz[:, q * d : (q + 1) * d] for q in range(k // d)], axis=0)
    r_z = r_oz[:, k:]
    parts = [
        g_cw.reshape(taps, 8, conv).sum(1).reshape(-1),
        g_cb.sum(0),
        g_gain.sum(0),
        g_gate.sum(0),
        g_a.sum(0)[:heads] * rate[0],
        g_skip.sum(0).reshape(heads, p).sum(1),
        g_dt.sum(0)[:heads],
    ]
    total = reduce_small(after(jnp.concatenate(parts), x_out))
    w = lax.axis_index("wshard")
    res, off = [], 0
    for k, part in enumerate(parts):
        v = total[off : off + part.shape[0]]
        off += part.shape[0]
        v = v.reshape(taps, conv) if k == 0 else v
        width = v.shape[-1] // nw
        res.append(lax.dynamic_slice_in_dim(v, w * width, width, axis=v.ndim - 1))
    res = [res[k] for k in (0, 1, 4, 5, 6, 2, 3)]
    return (mixed[None], grad_input[None], jnp.concatenate([r_z, r_x], axis=1), r_out) + tuple(res)


def solution(mesh):
    wide = P("wshard", "seq", None)
    mat = P("wshard", None)
    taps = P(None, "wshard")
    vec = P("wshard")
    return jax.shard_map(
        body,
        mesh=mesh,
        in_specs=(wide, wide, mat, mat, mat, taps) + (vec,) * 6,
        out_specs=(wide, wide, mat, mat, taps) + (vec,) * 6,
        check_vma=False,
    )
```

```python
import jax
import jax.numpy as jnp
from jax import lax
from jax.experimental import pallas as pl
from jax.experimental.pallas import tpu as pltpu
from jax.sharding import PartitionSpec as P

f32 = jnp.float32
bf16 = jnp.bfloat16
EPS = 1e-05
LOG2E = 1.4426950408889634
CH = 128
TB = 256
LONGEST = 4096
HIGH = lax.Precision.HIGHEST
MB = 1024 * 1024
VMEM = 60 * MB


def sigmoid(v):
    return 0.5 * jnp.tanh(0.5 * v) + 0.5


def dot(a, b):
    return jnp.dot(a, b, preferred_element_type=f32)


def dot_nt(a, b):
    return lax.dot_general(a, b, (((1,), (1,)), ((), ())), preferred_element_type=f32)


def two(v):
    hi = v.astype(bf16)
    return hi, (v - hi.astype(f32)).astype(bf16)


def spread(v, e2):
    return dot(jnp.concatenate(two(v), axis=1), e2)


def head_sums(row, e2):
    hi, lo = two(jnp.broadcast_to(row, (8, row.shape[1])))
    return dot_nt(hi, e2[0:128, :]) + dot_nt(lo, e2[0:128, :])


def cost(us):
    return pl.CostEstimate(flops=int(us * 1.1e8), bytes_accessed=1 << 20, transcendentals=0)


def call(kernel, grid, ins, outs, scratch, us, args, name):
    return pl.pallas_call(
        kernel,
        grid_spec=pltpu.PrefetchScalarGridSpec(
            num_scalar_prefetch=1,
            grid=grid,
            in_specs=ins,
            out_specs=[o[0] for o in outs],
            scratch_shapes=scratch,
        ),
        out_shape=[jax.ShapeDtypeStruct(o[1], o[2]) for o in outs],
        compiler_params=pltpu.CompilerParams(
            vmem_limit_bytes=VMEM, dimension_semantics=("arbitrary",)
        ),
        cost_estimate=cost(us),
        name=name,
    )(*args)


def rows(block, cols, col=0):
    return pl.BlockSpec((block, cols), lambda i, s: (i, col))


def whole(shape):
    return pl.BlockSpec(shape, lambda i, s: (0,) * len(shape))


def norm_rows(uf, gain):
    scale = lax.rsqrt(jnp.mean(uf * uf, axis=-1, keepdims=True) + EPS)
    return (uf * scale * gain).astype(bf16)


def place(buf, ids, parts, width):
    for j, part in enumerate(parts):
        n = part.shape[0]
        at = pl.multiple_of(ids[j] * n, 64)
        buf[pl.ds(at, n), :width] = part[...]


def front_kernel(np_, di, conv, heads):
    def kernel(ids, u, ue, gain, *rest):
        parts = rest[:np_]
        (cw, cb, dtb, nr, tok, e2, nrm_o, xbc_o, xc_o, slope_o, xd_o, dts_o, cc_o, ct_o,
         st_o, db_o, end_o, tot_o, nrme_o, xbce_o, wbuf, ext, state, kd, sp) = rest[np_:]
        i = pl.program_id(0)
        n = (conv - di) // 2

        @pl.when(i == 0)
        def _():
            wbuf[:, conv:] = jnp.zeros((wbuf.shape[0], wbuf.shape[1] - conv), bf16)
            place(wbuf, ids, parts, conv + heads)
            nrme = norm_rows(ue[...].astype(f32), gain[...])
            nrme_o[...] = nrme
            pe = dot(nrme, wbuf[:, :conv]).astype(bf16)
            xbce_o[...] = pe
            ext[0:8, :] = pe.astype(f32)[8:16]
            state[...] = jnp.zeros_like(state)
            kd[...] = jnp.ones_like(kd)

        nrm = norm_rows(u[...].astype(f32), gain[...])
        nrm_o[...] = nrm
        pd = dot(nrm, wbuf[:, conv:])
        for c0 in range(0, conv, 256):
            px = dot(nrm, wbuf[:, c0 : c0 + 256]).astype(bf16)
            xbc_o[:, c0 : c0 + 256] = px
            ext[8 : 8 + TB, c0 : c0 + 256] = px.astype(f32)
        sh = pd + dtb[...]
        dt = jnp.maximum(sh, 0.0) + jnp.log1p(jnp.exp(-jnp.abs(sh)))
        dts_o[:, :128] = dt
        dts_o[:, 128:] = jax.nn.sigmoid(sh)
        a2 = dt * nr[...]
        ri = lax.broadcasted_iota(jnp.int32, (CH, CH), 0)
        ci = lax.broadcasted_iota(jnp.int32, (CH, CH), 1)
        low = (ri >= ci).astype(f32)
        pieces = [dt]
        leaves = []
        for k in range(TB // CH):
            r = slice(k * CH, (k + 1) * CH)
            c2 = jnp.dot(low, a2[r], precision=HIGH, preferred_element_type=f32)
            cc_o[r, :] = c2
            ct_o[:, r] = c2.T[: ct_o.shape[0], :]
            pieces.append(jnp.exp2(c2[CH - 1 :] - c2) * tok[r, 2:3])
            leaves.append(jnp.exp2(c2[CH - 1 :]) * tok[(k + 1) * CH - 1 : (k + 1) * CH, 1:2])
        lv = jnp.concatenate([jnp.broadcast_to(v, (8, 128)) for v in leaves], axis=0)
        sp[...] = spread(jnp.concatenate(pieces + [lv], axis=0), e2[...])
        for r0 in range(0, TB, 64):
            l0, l1, l2 = tok[r0 : r0 + 64, 3:4], tok[r0 : r0 + 64, 4:5], tok[r0 : r0 + 64, 5:6]
            for c0 in range(0, conv, 256):
                c = slice(c0, c0 + 256)
                pre = cb[:, c] + cw[3:4, c] * ext[8 + r0 : 72 + r0, c]
                pre = pre + cw[2:3, c] * (ext[7 + r0 : 71 + r0, c] * l2)
                pre = pre + cw[1:2, c] * (ext[6 + r0 : 70 + r0, c] * l1)
                pre = pre + cw[0:1, c] * (ext[5 + r0 : 69 + r0, c] * l0)
                sg = sigmoid(pre)
                xc = pre * sg
                xc_o[r0 : r0 + 64, c] = xc.astype(bf16)
                slope_o[r0 : r0 + 64, c] = (sg + xc * (1.0 - sg)).astype(bf16)
                if c0 < di:
                    xd_o[r0 : r0 + 64, c] = (xc * sp[r0 : r0 + 64, c]).astype(bf16)
        ext[0:8, :] = ext[TB : TB + 8, :]
        for k in range(TB // CH):
            r = slice(k * CH, (k + 1) * CH)
            st_o[k] = state[...].astype(bf16)
            db_o[k] = jnp.broadcast_to(kd[...], (8, 128))
            bt = xc_o[r, di : di + n].astype(f32).T.astype(bf16)
            for c0 in range(0, di, 256):
                c = slice(c0, c0 + 256)
                xw = (xd_o[r, c].astype(f32) * sp[TB + k * CH : TB + (k + 1) * CH, c]).astype(bf16)
                lvr = sp[2 * TB + 8 * k : 2 * TB + 8 * k + 1, c]
                state[:, c] = lvr * state[:, c] + dot(bt, xw)
            kd[...] = kd[...] * leaves[k]

        @pl.when(i == pl.num_programs(0) - 1)
        def _():
            end_o[...] = state[...]
            tot_o[...] = spread(jnp.broadcast_to(kd[...], (8, 128)), e2[...])

    return kernel


def inner_kernel(heads, di):
    p = di // heads
    per = 128 // p

    def kernel(ids, b, c, xd, cc, ct, tok, segr, y_o):
        s = dot_nt(c[...], b[...])
        ri = lax.broadcasted_iota(jnp.int32, (CH, CH), 0)
        ci = lax.broadcasted_iota(jnp.int32, (CH, CH), 1)
        bias = jnp.where((tok[:, 0:1] == segr[...]) & (ri >= ci), 0.0, -1e30)
        lanes = lax.broadcasted_iota(jnp.int32, (1, 128), 1) // p
        for j in range(heads // per):
            xp = xd[:, 128 * j : 128 * j + 128]
            ms, xs = [], []
            for q in range(per):
                h = per * j + q
                e = jnp.exp2(cc[:, h : h + 1] - ct[h : h + 1, :] + bias)
                ms.append((s * e).astype(bf16))
                xs.append(xp * (lanes == q).astype(f32).astype(bf16))
            out = dot(jnp.concatenate(ms, axis=1), jnp.concatenate(xs, axis=0))
            y_o[:, 128 * j : 128 * j + 128] = out.astype(bf16)

    return kernel


def gate_kernel(np_, di, d):
    def kernel(ids, nrm, yin, x, c_in, cc, tok, st, db, inc, u, cot, *rest):
        wz, wo = rest[:np_], rest[np_ : 2 * np_]
        (gain, dsk, e2, mixed_o, gn_o, dz_o, dy_o, edy_o, e_o, sf_o, dc_o, rin_o, gs_o,
         rg_o, zbuf, obuf, z, yi, dgn, ee, pr, gs) = rest[2 * np_ :]
        i = pl.program_id(0)

        @pl.when(i == 0)
        def _():
            place(zbuf, ids, wz, di)
            place(obuf, ids, wo, d)
            gs[...] = jnp.zeros_like(gs)
            rg_o[...] = jnp.zeros_like(rg_o)

        keep = tok[:, 6:7]
        ef = cot[...].astype(f32) * keep
        e = ef.astype(bf16)
        e_o[...] = e
        nb = TB // CH
        ents = []
        for k in range(nb):
            r = slice(k * CH, (k + 1) * CH)
            ents.append(jnp.exp2(cc[r, :]) * tok[r, 1:2])
        ee[...] = spread(jnp.concatenate(ents + [db[k] for k in range(nb)], axis=0), e2[...])
        for k in range(nb):
            r = slice(k * CH, (k + 1) * CH)
            for c0 in range(0, di, 256):
                c = slice(c0, c0 + 256)
                dbr = ee[TB + 8 * k : TB + 8 * k + 1, c]
                sf = (st[k, :, c].astype(f32) + dbr * inc[:, c].astype(f32)).astype(bf16)
                sf_o[k, :, c] = sf
                yi[r, c] = dot(c_in[r, :], sf)
        z[...] = dot(nrm[...], zbuf[...])
        dgn[...] = dot_nt(e, obuf[...])

        def strip(r):
            xs = x[r, :].astype(f32)
            eyi = ee[r, :] * yi[r, :]
            y = yin[r, :].astype(f32) + eyi + dsk[...] * xs
            zz = z[r, :]
            sg = sigmoid(zz)
            act = zz * sg
            g = y * act
            scale = lax.rsqrt(jnp.mean(g * g, axis=-1, keepdims=True) + EPS)
            ug = g * scale
            gn_o[r, :] = (ug * gain[...]).astype(bf16)
            dg0 = dgn[r, :]
            dn = dg0 * gain[...]
            m = jnp.mean(dn * ug, axis=-1, keepdims=True)
            dg = scale * (dn - ug * m)
            dy = dg * act
            dz_o[r, :] = (dg * y * (sg + act * (1.0 - sg))).astype(bf16)
            dy_o[r, :] = dy.astype(bf16)
            ps = xs * dy
            gs[...] += ps[0:8] + ps[8:16]
            edy_o[r, :] = (dy * ee[r, :]).astype(bf16)
            pr[r, :] = (dy * eyi).astype(bf16)

        for t in range(TB // 16):
            strip(slice(t * 16, t * 16 + 16))
        rin_o[...] = dot_nt(pr[...], e2[0:128, :])
        mixed_o[...] = (keep * (u[...].astype(f32) + dot(gn_o[...], obuf[...]))).astype(bf16)
        for k in range(nb):
            r = slice(k * CH, (k + 1) * CH)
            ctr = c_in[r, :].astype(f32).T.astype(bf16)
            for c0 in range(0, di, 256):
                c = slice(c0, c0 + 256)
                dcv = dot(ctr, edy_o[r, c])
                dc_o[k, :, c] = dcv.astype(bf16)
                rg_o[:, c] += ee[TB + 8 * k : TB + 8 * k + 1, c] * dcv

        @pl.when(i == pl.num_programs(0) - 1)
        def _():
            gs_o[...] = head_sums(jnp.sum(gs[...], axis=0, keepdims=True), e2)

    return kernel


def inner_back_kernel(p, h0, h1):
    per = 128 // p

    def kernel(ids, b, c, xd, dy, cc, ct, tok, segr, gxd_o, db_o, dc_o, rk_o, rr):
        st = dot_nt(b[...], c[...])
        si = lax.broadcasted_iota(jnp.int32, (CH, CH), 0)
        ti = lax.broadcasted_iota(jnp.int32, (CH, CH), 1)
        bias = jnp.where((tok[:, 0:1] == segr[...]) & (ti >= si), 0.0, -1e30)
        lanes = lax.broadcasted_iota(jnp.int32, (1, 128), 1) // p
        rr[...] = jnp.zeros_like(rr)
        rk_o[...] = jnp.zeros_like(rk_o)
        gsum = jnp.zeros((CH, CH), f32)
        for j in range((h1 - h0) // per):
            xp = xd[:, 128 * j : 128 * j + 128]
            dyp = dy[:, 128 * j : 128 * j + 128]
            dys = jnp.concatenate(
                [dyp * (lanes == q).astype(f32).astype(bf16) for q in range(per)], axis=0
            )
            gm = dot_nt(xp, dys)
            ms = []
            for q in range(per):
                h = h0 + per * j + q
                e = jnp.exp2(ct[h : h + 1, :] - cc[:, h : h + 1] + bias)
                ms.append((st * e).astype(bf16))
                ge = gm[:, q * CH : (q + 1) * CH] * e
                gsum = gsum + ge
                ex = ge * st
                rr[h : h + 1, :] = jnp.sum(ex, axis=0, keepdims=True)
                rk_o[:, h : h + 1] = jnp.sum(ex, axis=1, keepdims=True)
            out = dot(jnp.concatenate(ms, axis=1), dys)
            gxd_o[:, 128 * j : 128 * j + 128] = out.astype(bf16)
        rk_o[...] = rr[...].T - rk_o[...]
        db_o[...] = dot(gsum.astype(bf16), c[...])
        dc_o[...] = dot(gsum.T.astype(bf16), b[...])

    return kernel


def back_kernel(w, n, h0, h1, last_part):
    cols = w + 2 * n if last_part else w

    def kernel(ids, x_in, b_in, slope, xbc, xbce, xd, dts, cc, tok, elink, gxd, dbi, dci, rk, rin,
               dy, edy, sf, dcs, gend, cw, dsk, nr, e2, *rest):
        if last_part:
            slope2, xbc2, xbce2, cw2, dbp, dcp, ddtp, gsk = rest[:8]
            gp_o, edge_o, sum_o = rest[8:11]
        else:
            gp_o, edge_o, sum_o, dbp_o, dcp_o, ddtp_o = rest[:6]
        ds, sp, sr, ext, xq, xe, gw_o, gb_o, ga_o, gdt_o = rest[-10:]
        i = pl.program_id(0)
        nb = TB // CH

        def pick(a, a2, r, c0):
            return a[r, c0 : c0 + 256] if c0 < w else a2[r, c0 - w : c0 - w + 256]

        @pl.when(i == 0)
        def _():
            ds[...] = gend[...].astype(f32)
            ext[TB : TB + 8, :] = jnp.zeros((8, cols), f32)
            gw_o[...] = jnp.zeros_like(gw_o)
            gb_o[...] = jnp.zeros_like(gb_o)
            ga_o[...] = jnp.zeros_like(ga_o)
            gdt_o[...] = jnp.zeros_like(gdt_o)

        if not last_part:
            slope2 = xbc2 = xbce2 = cw2 = None
        dt = dts[:, :128]
        pieces, leaves = [dt], []
        for k in range(nb):
            r = slice(k * CH, (k + 1) * CH)
            c2 = cc[r, :]
            pieces.append(jnp.exp2(c2[CH - 1 :] - c2) * tok[r, 2:3])
            leaves.append(jnp.exp2(c2[CH - 1 :]) * tok[(k + 1) * CH - 1 : (k + 1) * CH, 1:2])
        lv = jnp.concatenate([jnp.broadcast_to(v, (8, 128)) for v in leaves], axis=0)
        sp[...] = spread(jnp.concatenate(pieces + [lv], axis=0), e2[...])
        lsum = [None] * nb
        for k in reversed(range(nb)):
            r = slice(k * CH, (k + 1) * CH)
            lacc = []
            gb = dbi[r, :]
            gc = dci[r, :]
            for c0 in range(0, w, 256):
                c = slice(c0, c0 + 256)
                dsv = ds[:, c]
                dsb = dsv.astype(bf16)
                sfv = sf[k, :, c]
                sr[r, c] = dot(b_in[r, :], dsb)
                xwv = (xd[r, c].astype(f32) * sp[TB + k * CH : TB + (k + 1) * CH, c]).astype(bf16)
                gb = gb + dot_nt(xwv, dsb)
                gc = gc + dot_nt(edy[r, c], sfv)
                lacc.append(jnp.sum(dsv * sfv.astype(f32), axis=0, keepdims=True))
                lvr = sp[2 * TB + 8 * k : 2 * TB + 8 * k + 1, c]
                ds[:, c] = lvr * dsv + dcs[k, :, c].astype(f32)
            lsum[k] = head_sums(jnp.concatenate(lacc, axis=1), e2)[0:1]
            if last_part:
                ext[r, w : w + n] = (gb + dbp[r, :]) * slope2[r, :n].astype(f32)
                ext[r, w + n :] = (gc + dcp[r, :]) * slope2[r, n:].astype(f32)
            else:
                dbp_o[r, :] = gb
                dcp_o[r, :] = gc

        def strip(r, re):
            x = x_in[r, :].astype(f32)
            es = sp[re, :] * sr[r, :]
            q = gxd[r, :].astype(f32) + es
            gx = sp[r, :] * q + dsk[...] * dy[r, :].astype(f32)
            ext[r, 0:w] = gx * slope[r, :].astype(f32)
            xq[r, :] = (x * q).astype(bf16)
            xe[r, :] = (x * es).astype(bf16)

        for t in range(TB // 16):
            strip(slice(t * 16, t * 16 + 16), slice(TB + t * 16, TB + t * 16 + 16))
        gdt = dot_nt(xq[...], e2[0:128, :])
        et = dot_nt(xe[...], e2[0:128, :]) * dt
        ri = lax.broadcasted_iota(jnp.int32, (CH, CH), 0)
        ci = lax.broadcasted_iota(jnp.int32, (CH, CH), 1)
        hl = lax.broadcasted_iota(jnp.int32, (1, 128), 1)
        hm = ((hl >= h0) & (hl < h1)).astype(f32)
        tri = jnp.concatenate([(ci >= ri).astype(f32), (ci < ri).astype(f32)], axis=1)
        for k in range(nb):
            r = slice(k * CH, (k + 1) * CH)
            v = jnp.concatenate([rk[r, :] + rin[r, :] * hm, et[r]], axis=0)
            ga = jnp.dot(tri, v, precision=HIGH, preferred_element_type=f32) + lsum[k] * leaves[k]
            ddt = (gdt[r] + ga * nr[...]) * dts[r, 128:]
            gad = ga * dts[r, :128]
            acc_a, acc_d = gad[0:8], ddt[0:8]
            for q in range(8, CH, 8):
                acc_a = acc_a + gad[q : q + 8]
                acc_d = acc_d + ddt[q : q + 8]
            ga_o[...] += acc_a
            gdt_o[...] += acc_d
            if last_part:
                gp_o[r, cols:] = (ddt + ddtp[r, :]).astype(bf16)
            else:
                ddtp_o[r, :] = ddt
        for r0 in range(0, TB, 64):
            rs = slice(r0, r0 + 64)
            for c0 in range(0, cols, 256):
                c = slice(c0, c0 + 256)
                g0 = ext[rs, c]
                xb = pick(xbc, xbc2, rs, c0).astype(f32)
                gsum = pick(cw, cw2, slice(3, 4), c0) * g0
                ws = [None, None, None, g0 * xb]
                for s in (1, 2, 3):
                    gs = ext[r0 + s : r0 + s + 64, c] * tok[rs, 6 + s : 7 + s]
                    gsum = gsum + pick(cw, cw2, slice(3 - s, 4 - s), c0) * gs
                    ws[3 - s] = gs * xb
                gp_o[rs, c] = gsum.astype(bf16)
                gb = g0[0:8]
                for q in range(8, 64, 8):
                    gb = gb + g0[q : q + 8]
                gb_o[:, c] += gb
                for o in range(4):
                    v = ws[o][0:8]
                    for q in range(8, 64, 8):
                        v = v + ws[o][q : q + 8]
                    gw_o[8 * o : 8 * o + 8, c] += v
        ext[TB : TB + 8, :] = ext[0:8, :]

        @pl.when(i == pl.num_programs(0) - 1)
        def _():
            zero = jnp.zeros((8, 256), f32)
            for c0 in range(0, cols, 256):
                c = slice(c0, c0 + 256)
                xb = pick(xbce, xbce2, slice(8, 16), c0).astype(f32)
                ext[8:16, c] = ext[TB : TB + 8, c]
                ext[0:8, c] = zero
                gsum = zero
                for s in (1, 2, 3):
                    gs = ext[s : s + 8, c] * elink[:, 6 + s : 7 + s]
                    gsum = gsum + pick(cw, cw2, slice(3 - s, 4 - s), c0) * gs
                    gw_o[8 * (3 - s) : 8 * (3 - s) + 8, c] += gs * xb
                edge_o[:, c] = jnp.concatenate([zero, gsum], axis=0).astype(bf16)
                sums = [jnp.sum(gw_o[8 * o : 8 * o + 8, c], axis=0, keepdims=True) for o in range(4)]
                sums.append(jnp.sum(gb_o[:, c], axis=0, keepdims=True))
                sum_o[:, c] = jnp.concatenate(sums + [zero[0:3]], axis=0)
            sum_o[5:6, 0:128] = jnp.sum(ga_o[...], axis=0, keepdims=True)
            sum_o[6:7, 0:128] = jnp.sum(gdt_o[...], axis=0, keepdims=True)
            if last_part:
                sum_o[7:8, 0:128] = gsk[0:1, :]

    return kernel


def input_kernel(np_, di, conv, heads):
    def kernel(ids, gpz, gpa, gpb, ea, eb, u, e, *rest):
        wz, wx = rest[:np_], rest[np_ : 2 * np_]
        gain, gi_o, zbuf, xbuf = rest[2 * np_ :]
        i = pl.program_id(0)

        @pl.when(i == 0)
        def _():
            xbuf[:, conv:] = jnp.zeros((xbuf.shape[0], xbuf.shape[1] - conv), bf16)
            place(zbuf, ids, wz, di)
            place(xbuf, ids, wx, conv + heads)

        wa = gpa.shape[1]
        gn = dot_nt(gpz[...], zbuf[...]) + dot_nt(gpa[...], xbuf[:, :wa]) + dot_nt(gpb[...], xbuf[:, wa:])
        last = (i == pl.num_programs(0) - 1).astype(f32)
        tail = (dot_nt(ea[...], xbuf[:, :wa]) + dot_nt(eb[...], xbuf[:, wa:conv])) * last
        gn = jnp.concatenate([gn[: TB - 16], gn[TB - 16 :] + tail], axis=0)
        uf = u[...].astype(f32)
        scale = lax.rsqrt(jnp.mean(uf * uf, axis=-1, keepdims=True) + EPS)
        unit = uf * scale
        dn = gn * gain[...]
        m = jnp.mean(dn * unit, axis=-1, keepdims=True)
        gi_o[...] = (e[...].astype(f32) + scale * (dn - unit * m)).astype(bf16)

    return kernel


def swap(v, axis, bit):
    return lax.ppermute(v, axis, [(k, k ^ bit) for k in range(lax.axis_size(axis))])


def shift(v, axis, steps):
    n = lax.axis_size(axis)
    return lax.ppermute(v, axis, [(k, k + steps) for k in range(n) if 0 <= k + steps < n])


def bits_of(n):
    return [1 << k for k in reversed(range((n - 1).bit_length()))]


def after(v, dep):
    if dep is None:
        return v
    return lax.optimization_barrier((v, dep))[0]


def gather_parts(v, axis):
    parts = [v]
    for bit in bits_of(lax.axis_size(axis)):
        parts = parts + [swap(p, axis, bit) for p in parts]
    return parts


def in_order(parts, axis):
    at = lax.axis_index(axis)
    n = lax.axis_size(axis)
    v = jnp.stack(parts)
    rest = v.shape[1:]
    bits = bits_of(n)
    v = v.reshape((2,) * len(bits) + rest)
    for k, bit in enumerate(reversed(bits)):
        v = jnp.where((at // bit) % 2 == 0, v, jnp.flip(v, k))
    order = tuple(reversed(range(len(bits))))
    return v.transpose(order + tuple(range(len(bits), v.ndim))).reshape((n,) + rest)


def part_ids(axis):
    ids = [lax.axis_index(axis)]
    for bit in bits_of(lax.axis_size(axis)):
        ids = ids + [k ^ bit for k in ids]
    return ids


def add(a, b):
    return (a.astype(f32) + b.astype(f32)).astype(bf16)


def pair_steps(gs):
    nw = lax.axis_size("wshard")
    w = lax.axis_index("wshard")
    n = min(g.shape[0] for g in gs) // nw

    def pick(at):
        out = []
        for g in gs:
            v = g.reshape(nw // 2, 2, -1, g.shape[-1])
            v = lax.dynamic_index_in_dim(v, at, 1, keepdims=False)
            k = v.shape[1] // n
            out += [v[:, q * n : (q + 1) * n] for q in range(k)]
        return jnp.concatenate(out, axis=2) if len(out) > 1 else out[0]

    send, keep = pick(1 - w % 2), pick(w % 2)
    dep = yield send
    yield add(keep, swap(after(send, dep), "wshard", 1))


def other_steps(v):
    nw = lax.axis_size("wshard")
    w = lax.axis_index("wshard")
    n = v.shape[1]
    for bit in [1 << k for k in range(1, (nw - 1).bit_length())]:
        at = (w // bit) % 2
        v = v.reshape(-1, 2, n, v.shape[-1]).swapaxes(0, 1)
        send = lax.dynamic_index_in_dim(v, 1 - at, 0, keepdims=False)
        keep = lax.dynamic_index_in_dim(v, at, 0, keepdims=False)
        dep = yield send
        v = add(keep, swap(after(send, dep), "wshard", bit))
    yield v.reshape(n, -1)


def seq_steps(v):
    ns = lax.axis_size("seq")
    s = lax.axis_index("seq")
    for bit in [1 << k for k in range((ns - 1).bit_length())]:
        at = (s // bit) % 2
        v = v.reshape(2, -1, v.shape[-1])
        send = lax.dynamic_index_in_dim(v, 1 - at, 0, keepdims=False)
        keep = lax.dynamic_index_in_dim(v, at, 0, keepdims=False)
        dep = yield send
        v = add(keep, swap(after(send, dep), "seq", bit))
    for bit in bits_of(ns):
        dep = yield v
        got = swap(after(v, dep), "seq", bit)
        first = (s // bit) % 2 == 0
        v = jnp.concatenate([jnp.where(first, v, got), jnp.where(first, got, v)], axis=0)
    yield v.astype(f32)


def small_steps(v):
    for axis in ("wshard", "seq"):
        for bit in reversed(bits_of(lax.axis_size(axis))):
            dep = yield v
            v = v + swap(after(v, dep), axis, bit)
    yield v


def pack_state(decay, state):
    hi, lo = two(decay)
    return jnp.concatenate([state.astype(bf16), hi, lo], axis=0)


def unpack_state(v, n):
    return v[n : n + 8].astype(f32)[:1] + v[n + 8 : n + 16].astype(f32)[:1], v[:n].astype(f32)


def carried(decay, state, sign, tokens):
    n = state.shape[0]
    span = 1
    while span < -(-LONGEST // tokens):
        send = pack_state(decay, state)
        dep = yield send
        d, s = unpack_state(shift(after(send, dep), "seq", sign * span), n)
        state = state + decay[:1] * s
        decay = decay * d
        span *= 2
    send = state.astype(bf16)
    dep = yield send
    yield shift(after(send, dep), "seq", sign)


class Steps:
    def __init__(self, gen):
        self.gen = gen
        self.value = next(gen)

    def step(self, dep=None):
        try:
            self.value = self.gen.send(dep)
        except StopIteration:
            pass
        return self.value

    def finish(self):
        for self.value in self.gen:
            pass
        return self.value


def body(inputs, cotangent, lengths, in_proj, out_proj, conv_weight, conv_bias, a_log, d_skip,
         dt_bias, norm_gain, gate_gain):
    t, d = inputs.shape[1:]
    nw = lax.axis_size("wshard")
    di = out_proj.shape[0] * nw
    heads = a_log.shape[0] * nw
    conv = conv_bias.shape[0] * nw
    taps = conv_weight.shape[0]
    n = (conv - di) // 2
    p = di // heads
    docs = lengths.shape[1]
    nt, nc, nb = t // TB, t // CH, TB // CH
    wide = conv + 128
    wx, wz = in_proj[:, di:], in_proj[:, :di]
    pc = conv // nw
    width = -(-max(pc, di // nw, 384) // 128) * 128

    def line(*vs):
        vs = [v if v.ndim == 2 else v[None] for v in vs]
        vs = [jnp.pad(v, ((0, 0), (0, (width if k == len(vs) - 1 else 128 * (k + 1)) - 128 * k - v.shape[1])))
              for k, v in enumerate(vs)]
        return jnp.concatenate(vs, axis=1)

    small = jnp.concatenate(
        [line(conv_weight), line(conv_bias), line(gate_gain), line(norm_gain), line(a_log, d_skip, dt_bias)], axis=0)
    small = in_order(gather_parts(small, "wshard"), "wshard").astype(f32)
    wx_parts = gather_parts(wx, "wshard")
    wz_parts = gather_parts(after(wz, wx_parts[1]), "wshard")
    wo_parts = gather_parts(after(out_proj, wx_parts[1]), "wshard")
    ids = jnp.stack(part_ids("wshard")).astype(jnp.int32)
    hw = heads // nw
    cw = small[:, :taps, :pc].swapaxes(0, 1).reshape(taps, conv)
    cb = small[:, taps, :pc].reshape(1, conv)
    gain_gate = small[:, taps + 1, : di // nw].reshape(1, di)
    gain_in = small[:, taps + 2, : d // nw].reshape(1, d)
    log_rate, skip, dtb = [small[:, taps + 3, 128 * k : 128 * k + hw].reshape(1, heads) for k in range(3)]
    rate = -jnp.exp(log_rate)
    pad = ((0, 0), (0, 128 - heads))
    nr = jnp.pad(rate, pad)
    nr2 = nr * LOG2E
    dtb = jnp.pad(dtb, pad)
    dsk = jnp.repeat(skip, p, axis=1)
    head_of = jnp.arange(di, dtype=jnp.int32) // p
    e1 = (jnp.arange(128, dtype=jnp.int32)[:, None] == head_of[None]).astype(bf16)
    e2 = jnp.concatenate([e1, e1], axis=0)
    first = lax.axis_index("seq") * t
    pos = first - 8 + jnp.arange(t + 16, dtype=jnp.int32)
    ends = jnp.cumsum(lengths[0], dtype=jnp.int32)
    seg = jnp.sum((pos[:, None] >= ends[None]).astype(jnp.int32), axis=1)
    seg = jnp.where(pos < 0, -1, seg)
    here = seg[: t + 8]
    own = seg[8 : t + 8]
    entering = jnp.repeat(seg[7 : t + 7 : CH], CH)
    leaving = jnp.repeat(seg[7 + CH : t + 8 : CH], CH)
    zero8 = jnp.zeros((8,), jnp.int32)
    back = [jnp.concatenate([zero8, (seg[8 - k : t + 8 - k] == own).astype(jnp.int32)]) for k in (3, 2, 1)]
    ahead = [(seg[k : t + 8 + k] == here).astype(jnp.int32) for k in (1, 2, 3)]
    cols = [here, jnp.concatenate([zero8, (entering == own).astype(jnp.int32)]),
            jnp.concatenate([zero8, (leaving == own).astype(jnp.int32)])]
    cols = cols + back + [(here < docs).astype(jnp.int32)] + ahead + [jnp.zeros_like(here)] * 6
    tok_all = jnp.stack(cols, axis=1).astype(f32)
    tok, elink = tok_all[8:], tok_all[:8]
    segr = own.astype(f32)[None]
    u, cot = inputs[0], cotangent[0]
    ue = shift(u[t - 16 :], "seq", 1)

    outs = [
        (rows(TB, d), (t, d), bf16),
        (rows(TB, conv), (t, conv), bf16),
        (rows(TB, conv), (t, conv), bf16),
        (rows(TB, conv), (t, conv), bf16),
        (rows(TB, di), (t, di), bf16),
        (rows(TB, 256), (t, 256), f32),
        (rows(TB, 128), (t, 128), f32),
        (pl.BlockSpec((32, TB), lambda i, s: (0, i)), (32, t), f32),
        (pl.BlockSpec((nb, n, di), lambda i, s: (i, 0, 0)), (nc, n, di), bf16),
        (pl.BlockSpec((nb, 8, 128), lambda i, s: (i, 0, 0)), (nc, 8, 128), f32),
        (whole((n, di)), (n, di), f32),
        (whole((8, di)), (8, di), f32),
        (whole((16, d)), (16, d), bf16),
        (whole((16, conv)), (16, conv), bf16),
    ]
    ins = [rows(TB, d), whole((16, d)), whole((1, d))] + [whole(v.shape) for v in wx_parts]
    ins += [whole((taps, conv)), whole((1, conv)), whole((1, 128)), whole((1, 128)), rows(TB, 16), whole((256, di))]
    scratch = [
        pltpu.VMEM((d, wide), bf16),
        pltpu.VMEM((TB + 8, conv), f32),
        pltpu.VMEM((n, di), f32),
        pltpu.VMEM((1, 128), f32),
        pltpu.VMEM((2 * TB + 8 * nb, di), f32),
    ]
    (nrm, xbc, xc, slope, xd, dts, cc, ct, st, dbf, end, tot, nrme, xbce) = call(
        front_kernel(nw, di, conv, heads), (nt,), ins, outs, scratch, 15,
        [ids, u, ue, gain_in] + wx_parts + [cw, cb, dtb, nr2, tok, e2], "front")
    incoming = Steps(carried(tot, end, 1, t)).finish()

    crow = pl.BlockSpec((32, CH), lambda i, s: (0, i))
    srow = pl.BlockSpec((1, CH), lambda i, s: (0, i))
    bspec, cspec = rows(CH, n, di // n), rows(CH, n, di // n + 1)
    (yin,) = call(
        inner_kernel(heads, di), (nc,),
        [bspec, cspec, rows(CH, di), rows(CH, 128), crow, rows(CH, 16), srow],
        [(rows(CH, di), (t, di), bf16)], [], 10,
        [ids, xc, xc, xd, cc, ct, tok, segr], "inner")

    blk = pl.BlockSpec((nb, n, di), lambda i, s: (i, 0, 0))
    outs = [
        (rows(TB, d), (t, d), bf16),
        (rows(TB, di), (t, di), bf16),
        (rows(TB, di), (t, di), bf16),
        (rows(TB, di), (t, di), bf16),
        (rows(TB, di), (t, di), bf16),
        (rows(TB, d), (t, d), bf16),
        (blk, (nc, n, di), bf16),
        (blk, (nc, n, di), bf16),
        (rows(TB, 128), (t, 128), f32),
        (whole((8, 128)), (8, 128), f32),
        (whole((n, di)), (n, di), f32),
    ]
    ins = [rows(TB, d), rows(TB, di), rows(TB, di), rows(TB, n, di // n + 1), rows(TB, 128), rows(TB, 16), blk,
           pl.BlockSpec((nb, 8, 128), lambda i, s: (i, 0, 0)), whole((n, di)), rows(TB, d), rows(TB, d)]
    ins += [whole(v.shape) for v in wz_parts + wo_parts]
    ins += [whole((1, di)), whole((1, di)), whole((256, di))]
    scratch = [pltpu.VMEM((d, di), bf16), pltpu.VMEM((di, d), bf16)]
    scratch += [pltpu.VMEM((TB, di), f32)] * 3
    scratch += [pltpu.VMEM((TB + 8 * nb, di), f32), pltpu.VMEM((TB, di), bf16), pltpu.VMEM((8, di), f32)]
    (mixed, gn, dz, dy, edy, e, sf, dcs, rin, g_skip, reach) = call(
        gate_kernel(nw, di, d), (nt,), ins, outs, scratch, 25,
        [ids, nrm, yin, xc, xc, cc, tok, st, dbf, incoming, u, cot] + wz_parts + wo_parts + [gain_gate, dsk, e2], "gate")
    tn = (((0,), (0,)), ((), ()))

    def outer(a, b):
        return lax.dot_general(a, b, tn, preferred_element_type=f32)

    back_state = Steps(carried(tot, reach, -1, t))
    s1 = back_state.value
    gw_out = outer(after(gn, s1), e).astype(bf16)
    gw_z = outer(nrm, after(dz, s1)).astype(bf16)
    s2 = back_state.step()
    oz_p = Steps(pair_steps([gw_out, gw_z]))
    oz_w = Steps(other_steps(oz_p.step(s2)))
    oz2 = oz_w.value
    hh, hw2 = heads // 2, di // 2

    def half_inner(k, dep):
        outs = [
            (rows(CH, hw2), (t, hw2), bf16),
            (rows(CH, n), (t, n), f32),
            (rows(CH, n), (t, n), f32),
            (rows(CH, 128), (t, 128), f32),
        ]
        return call(
            inner_back_kernel(p, hh * k, hh * (k + 1)), (nc,),
            [bspec, cspec, rows(CH, hw2, k), rows(CH, hw2, k), rows(CH, 128), crow, rows(CH, 16), srow],
            outs, [pltpu.VMEM((128, CH), f32)], 12,
            [ids, xc, xc, xd, after(dy, dep), cc, ct, tok, segr], "inner_back")

    def rev(block, width, col=0):
        return pl.BlockSpec((block, width), lambda i, s: (nt - 1 - i, col))

    def at(shape, col):
        return pl.BlockSpec(shape, lambda i, s: (0, col))

    def half_back(k, inner, dep, gend, extra):
        gxd, dbi, dci, rk = inner
        last = k == 1
        cols = hw2 + 2 * n if last else hw2
        rblk = pl.BlockSpec((nb, n, hw2), lambda i, s: (nt - 1 - i, 0, k))
        ins = [rev(TB, hw2, k), rev(TB, n, di // n), rev(TB, hw2, k), rev(TB, hw2, k), at((16, hw2), k),
               rev(TB, hw2, k), rev(TB, 256), rev(TB, 128), rev(TB, 16), whole((8, 16)), rev(TB, hw2),
               rev(TB, n), rev(TB, n), rev(TB, 128), rev(TB, 128), rev(TB, hw2, k), rev(TB, hw2, k), rblk, rblk,
               at((n, hw2), k), at((taps, hw2), k), at((1, hw2), k), whole((1, 128)), at((256, hw2), k)]
        args = [ids, xc, xc, slope, xbc, xbce, xd, dts, cc, tok, elink, after(gxd, dep), dbi, dci, rk, rin, dy,
                edy, sf, dcs, gend, cw, dsk, nr, e2]
        outs = [
            (rev(TB, cols + 128 * last), (t, cols + 128 * last), bf16),
            (whole((16, cols)), (16, cols), bf16),
            (whole((8, cols)), (8, cols), f32),
        ]
        if last:
            ins += [rev(TB, 2 * n, di // (2 * n)), rev(TB, 2 * n, di // (2 * n)), at((16, 2 * n), di // (2 * n)),
                    at((taps, 2 * n), di // (2 * n)), rev(TB, n), rev(TB, n), rev(TB, 128), whole((8, 128))]
            args += [slope, xbc, xbce, cw] + list(extra)
        else:
            outs += [(rev(TB, n), (t, n), f32), (rev(TB, n), (t, n), f32), (rev(TB, 128), (t, 128), f32)]
        scratch = [
            pltpu.VMEM((n, hw2), f32),
            pltpu.VMEM((2 * TB + 8 * nb, hw2), f32),
            pltpu.VMEM((TB, hw2), f32),
            pltpu.VMEM((TB + 8, cols), f32),
            pltpu.VMEM((TB, hw2), bf16),
            pltpu.VMEM((TB, hw2), bf16),
            pltpu.VMEM((8 * taps, cols), f32),
            pltpu.VMEM((8, cols), f32),
            pltpu.VMEM((8, 128), f32),
            pltpu.VMEM((8, 128), f32),
        ]
        return call(back_kernel(hw2, n, hh * k, hh * (k + 1), last), (nt,), ins, outs, scratch, 15, args, "back")

    in_a = half_inner(0, (s2, oz2))
    s3 = back_state.step(oz2)
    s3, in_a0 = lax.optimization_barrier((s3, in_a[0]))
    in_b = half_inner(1, (s3, in_a0))
    back_state.step(in_a[0])
    gend = back_state.finish()
    oz_w.step()
    oz_s = Steps(seq_steps(oz_w.finish()))
    oz3 = oz_s.value
    (gpa, edge_a, sum_a, dbp, dcp, ddtp) = half_back(0, in_a, (in_b[0], oz3), gend, None)
    oz4 = oz_s.step(in_b[0])
    gw_xa = (outer(nrm, after(gpa, oz4)) + outer(nrme, edge_a)).astype(bf16)
    xa_p = Steps(pair_steps([gw_xa]))
    xa1 = xa_p.value
    (gpb, edge_b, sum_b) = half_back(1, in_b, (oz4, xa1), gend, (dbp, dcp, ddtp, g_skip))
    oz5 = oz_s.step(gpa)
    oz5, gpb_late = lax.optimization_barrier((oz5, gpb))
    gw_xb = outer(nrm, gpb_late)
    cb2 = conv - hw2
    gw_xb = jnp.concatenate(
        [gw_xb[:, :cb2] + outer(nrme, edge_b), gw_xb[:, cb2 : cb2 + heads]], axis=1).astype(bf16)
    xb_p = Steps(pair_steps([gw_xb]))
    x_w = Steps(other_steps(jnp.concatenate([xa_p.step(), xb_p.step()], axis=2)))
    x2 = x_w.value
    oz6 = oz_s.step(gpb)
    ea_in, eb_in = shift(edge_a, "seq", -1), shift(edge_b, "seq", -1)

    ins = [rows(TB, di), rows(TB, hw2), rows(TB, wide - hw2), whole((16, hw2)), whole((16, cb2)), rows(TB, d), rows(TB, d)]
    ins += [whole(v.shape) for v in wz_parts + wx_parts] + [whole((1, d))]
    outs = [(rows(TB, d), (t, d), bf16)]
    (grad_input,) = call(
        input_kernel(nw, di, conv, heads), (nt,), ins, outs,
        [pltpu.VMEM((d, di), bf16), pltpu.VMEM((d, wide), bf16)], 12,
        [ids, dz, after(gpa, (x2, oz6)), gpb, ea_in, eb_in, u, e] + wz_parts + wx_parts + [gain_in], "input")
    sums = Steps(small_steps(jnp.concatenate([sum_a, sum_b], axis=1)))
    sums.step(x2)
    x_s = Steps(seq_steps(x_w.finish()))
    oz_s.step(x2)
    oz_s.step(grad_input)
    sums.step(grad_input)
    dep = x_s.step(grad_input)
    oz_s.step(dep)
    for _ in range(3):
        sums.step(dep)
        dep = x_s.step()
    r_x, r_oz, total = x_s.finish(), oz_s.finish(), sums.finish()
    k = r_oz.shape[1] - di
    r_out = jnp.concatenate([r_oz[:, q * d : (q + 1) * d] for q in range(k // d)], axis=0)
    r_z = r_oz[:, k:]
    w = lax.axis_index("wshard")

    def mine(v):
        width = v.shape[-1] // nw
        return lax.dynamic_slice_in_dim(v, w * width, width, axis=v.ndim - 1)

    by_head = total[5:8, :heads] + total[5:8, hw2 : hw2 + heads]
    by_head = mine(by_head * jnp.concatenate([rate, jnp.ones((2, heads), f32)], axis=0))
    res = [mine(total[:taps]), mine(total[taps]), by_head[0], by_head[2], by_head[1]]
    res.append((jnp.sum(r_z * wz.astype(f32), axis=1) + jnp.sum(r_x * wx.astype(f32), axis=1)) / norm_gain.astype(f32))
    res.append(jnp.sum(r_out * out_proj.astype(f32), axis=1) / gate_gain.astype(f32))
    return (mixed[None], grad_input[None], jnp.concatenate([r_z, r_x], axis=1), r_out) + tuple(res)


def solution(mesh):
    wide = P("wshard", "seq", None)
    mat = P("wshard", None)
    taps = P(None, "wshard")
    vec = P("wshard")
    return jax.shard_map(
        body,
        mesh=mesh,
        in_specs=(wide, wide, mat, mat, mat, taps) + (vec,) * 6,
        out_specs=(wide, wide, mat, mat, taps) + (vec,) * 6,
        check_vma=False,
    )
```

```python
import jax
import jax.numpy as jnp
from jax import lax
from jax.experimental import pallas as pl
from jax.experimental.pallas import tpu as pltpu
from jax.sharding import PartitionSpec as P

f32 = jnp.float32
bf16 = jnp.bfloat16
EPS = 1e-05
LOG2E = 1.4426950408889634
CH = 128
TB = 256
TI = 256
LONGEST = 4096
HIGH = lax.Precision.HIGHEST
MB = 1024 * 1024
VMEM = 60 * MB


def sigmoid(v):
    return 0.5 * jnp.tanh(0.5 * v) + 0.5


def dot(a, b):
    return jnp.dot(a, b, preferred_element_type=f32)


def dot_nt(a, b):
    return lax.dot_general(a, b, (((1,), (1,)), ((), ())), preferred_element_type=f32)


def two(v):
    hi = v.astype(bf16)
    return hi, (v - hi.astype(f32)).astype(bf16)


def spread(v, e2):
    return dot(jnp.concatenate(two(v), axis=1), e2)


def head_sums(row, e2):
    hi, lo = two(jnp.broadcast_to(row, (8, row.shape[1])))
    return dot_nt(hi, e2[0:128, :]) + dot_nt(lo, e2[0:128, :])


def cost(us):
    return pl.CostEstimate(flops=int(us * 1.1e8), bytes_accessed=1 << 20, transcendentals=0)


def call(kernel, grid, ins, outs, scratch, us, args, name):
    return pl.pallas_call(
        kernel,
        grid_spec=pltpu.PrefetchScalarGridSpec(
            num_scalar_prefetch=1,
            grid=grid,
            in_specs=ins,
            out_specs=[o[0] for o in outs],
            scratch_shapes=scratch,
        ),
        out_shape=[jax.ShapeDtypeStruct(o[1], o[2]) for o in outs],
        compiler_params=pltpu.CompilerParams(
            vmem_limit_bytes=VMEM, dimension_semantics=("arbitrary",)
        ),
        cost_estimate=cost(us),
        name=name,
    )(*args)


def rows(block, cols, col=0):
    return pl.BlockSpec((block, cols), lambda i, s: (i, col))


def whole(shape):
    return pl.BlockSpec(shape, lambda i, s: (0,) * len(shape))


def norm_rows(uf, gain):
    scale = lax.rsqrt(jnp.mean(uf * uf, axis=-1, keepdims=True) + EPS)
    return (uf * scale * gain).astype(bf16)


def place(buf, ids, parts, width):
    for j, part in enumerate(parts):
        n = part.shape[0]
        at = pl.multiple_of(ids[j] * n, 64)
        buf[pl.ds(at, n), :width] = part[...]


def front_kernel(np_, di, conv, heads):
    def kernel(ids, u, ue, gain, *rest):
        parts = rest[:np_]
        (cw, cb, dtb, nr, tok, e2, nrm_o, xbc_o, xc_o, slope_o, xd_o, dts_o, cc_o, ct_o,
         st_o, db_o, end_o, tot_o, nrme_o, xbce_o, wbuf, ext, state, kd, sp) = rest[np_:]
        i = pl.program_id(0)
        n = (conv - di) // 2

        @pl.when(i == 0)
        def _():
            wbuf[:, conv:] = jnp.zeros((wbuf.shape[0], wbuf.shape[1] - conv), bf16)
            place(wbuf, ids, parts, conv + heads)
            nrme = norm_rows(ue[...].astype(f32), gain[...])
            nrme_o[...] = nrme
            pe = dot(nrme, wbuf[:, :conv]).astype(bf16)
            xbce_o[...] = pe
            ext[0:8, :] = pe.astype(f32)[8:16]
            state[...] = jnp.zeros_like(state)
            kd[...] = jnp.ones_like(kd)

        nrm = norm_rows(u[...].astype(f32), gain[...])
        nrm_o[...] = nrm
        pd = dot(nrm, wbuf[:, conv:])
        for c0 in range(0, conv, 256):
            px = dot(nrm, wbuf[:, c0 : c0 + 256]).astype(bf16)
            xbc_o[:, c0 : c0 + 256] = px
            ext[8 : 8 + TB, c0 : c0 + 256] = px.astype(f32)
        sh = pd + dtb[...]
        dt = jnp.maximum(sh, 0.0) + jnp.log1p(jnp.exp(-jnp.abs(sh)))
        dts_o[:, :128] = dt
        dts_o[:, 128:] = jax.nn.sigmoid(sh)
        a2 = dt * nr[...]
        ri = lax.broadcasted_iota(jnp.int32, (CH, CH), 0)
        ci = lax.broadcasted_iota(jnp.int32, (CH, CH), 1)
        low = (ri >= ci).astype(f32)
        pieces = [dt]
        leaves = []
        for k in range(TB // CH):
            r = slice(k * CH, (k + 1) * CH)
            c2 = jnp.dot(low, a2[r], precision=HIGH, preferred_element_type=f32)
            cc_o[r, :] = c2
            ct_o[:, r] = c2.T[: ct_o.shape[0], :]
            pieces.append(jnp.exp2(c2[CH - 1 :] - c2) * tok[r, 2:3])
            leaves.append(jnp.exp2(c2[CH - 1 :]) * tok[(k + 1) * CH - 1 : (k + 1) * CH, 1:2])
        lv = jnp.concatenate([jnp.broadcast_to(v, (8, 128)) for v in leaves], axis=0)
        sp[...] = spread(jnp.concatenate(pieces + [lv], axis=0), e2[...])
        for r0 in range(0, TB, 64):
            l0, l1, l2 = tok[r0 : r0 + 64, 3:4], tok[r0 : r0 + 64, 4:5], tok[r0 : r0 + 64, 5:6]
            for c0 in range(0, conv, 256):
                c = slice(c0, c0 + 256)
                pre = cb[:, c] + cw[3:4, c] * ext[8 + r0 : 72 + r0, c]
                pre = pre + cw[2:3, c] * (ext[7 + r0 : 71 + r0, c] * l2)
                pre = pre + cw[1:2, c] * (ext[6 + r0 : 70 + r0, c] * l1)
                pre = pre + cw[0:1, c] * (ext[5 + r0 : 69 + r0, c] * l0)
                sg = sigmoid(pre)
                xc = pre * sg
                xc_o[r0 : r0 + 64, c] = xc.astype(bf16)
                slope_o[r0 : r0 + 64, c] = (sg + xc * (1.0 - sg)).astype(bf16)
                if c0 < di:
                    xd_o[r0 : r0 + 64, c] = (xc * sp[r0 : r0 + 64, c]).astype(bf16)
        ext[0:8, :] = ext[TB : TB + 8, :]
        for k in range(TB // CH):
            r = slice(k * CH, (k + 1) * CH)
            st_o[k] = state[...].astype(bf16)
            db_o[k] = jnp.broadcast_to(kd[...], (8, 128))
            bt = xc_o[r, di : di + n].astype(f32).T.astype(bf16)
            for c0 in range(0, di, 256):
                c = slice(c0, c0 + 256)
                xw = (xd_o[r, c].astype(f32) * sp[TB + k * CH : TB + (k + 1) * CH, c]).astype(bf16)
                lvr = sp[2 * TB + 8 * k : 2 * TB + 8 * k + 1, c]
                state[:, c] = lvr * state[:, c] + dot(bt, xw)
            kd[...] = kd[...] * leaves[k]

        @pl.when(i == pl.num_programs(0) - 1)
        def _():
            end_o[...] = state[...]
            tot_o[...] = spread(jnp.broadcast_to(kd[...], (8, 128)), e2[...])

    return kernel


def inner_kernel(heads, di):
    p = di // heads
    per = 128 // p

    def kernel(ids, b, c, xd, cc, ct, tok, segr, y_o):
        ri = lax.broadcasted_iota(jnp.int32, (CH, CH), 0)
        ci = lax.broadcasted_iota(jnp.int32, (CH, CH), 1)
        lanes = lax.broadcasted_iota(jnp.int32, (1, 128), 1) // p
        for k in range(b.shape[0] // CH):
            r = slice(k * CH, (k + 1) * CH)
            s = dot_nt(c[r, :], b[r, :])
            bias = jnp.where((tok[r, 0:1] == segr[:, r]) & (ri >= ci), 0.0, -1e30)
            for j in range(heads // per):
                xp = xd[r, 128 * j : 128 * j + 128]
                ms, xs = [], []
                for q in range(per):
                    h = per * j + q
                    e = jnp.exp2(cc[r, h : h + 1] - ct[h : h + 1, r] + bias)
                    ms.append((s * e).astype(bf16))
                    xs.append(xp * (lanes == q).astype(f32).astype(bf16))
                out = dot(jnp.concatenate(ms, axis=1), jnp.concatenate(xs, axis=0))
                y_o[r, 128 * j : 128 * j + 128] = out.astype(bf16)

    return kernel


def gate_kernel(np_, di, d):
    def kernel(ids, nrm, yin, x, c_in, cc, tok, st, db, inc, u, cot, *rest):
        wz, wo = rest[:np_], rest[np_ : 2 * np_]
        (gain, dsk, e2, mixed_o, gn_o, dz_o, dy_o, edy_o, e_o, sf_o, dc_o, rin_o, gs_o,
         rg_o, zbuf, obuf, z, yi, dgn, ee, pr, gs) = rest[2 * np_ :]
        i = pl.program_id(0)

        @pl.when(i == 0)
        def _():
            place(zbuf, ids, wz, di)
            place(obuf, ids, wo, d)
            gs[...] = jnp.zeros_like(gs)
            rg_o[...] = jnp.zeros_like(rg_o)

        keep = tok[:, 6:7]
        ef = cot[...].astype(f32) * keep
        e = ef.astype(bf16)
        e_o[...] = e
        nb = TB // CH
        ents = []
        for k in range(nb):
            r = slice(k * CH, (k + 1) * CH)
            ents.append(jnp.exp2(cc[r, :]) * tok[r, 1:2])
        ee[...] = spread(jnp.concatenate(ents + [db[k] for k in range(nb)], axis=0), e2[...])
        for k in range(nb):
            r = slice(k * CH, (k + 1) * CH)
            for c0 in range(0, di, 256):
                c = slice(c0, c0 + 256)
                dbr = ee[TB + 8 * k : TB + 8 * k + 1, c]
                sf = (st[k, :, c].astype(f32) + dbr * inc[:, c].astype(f32)).astype(bf16)
                sf_o[k, :, c] = sf
                yi[r, c] = dot(c_in[r, :], sf)
        z[...] = dot(nrm[...], zbuf[...])
        dgn[...] = dot_nt(e, obuf[...])

        def strip(r):
            xs = x[r, :].astype(f32)
            eyi = ee[r, :] * yi[r, :]
            y = yin[r, :].astype(f32) + eyi + dsk[...] * xs
            zz = z[r, :]
            sg = sigmoid(zz)
            act = zz * sg
            g = y * act
            scale = lax.rsqrt(jnp.mean(g * g, axis=-1, keepdims=True) + EPS)
            ug = g * scale
            gn_o[r, :] = (ug * gain[...]).astype(bf16)
            dg0 = dgn[r, :]
            dn = dg0 * gain[...]
            m = jnp.mean(dn * ug, axis=-1, keepdims=True)
            dg = scale * (dn - ug * m)
            dy = dg * act
            dz_o[r, :] = (dg * y * (sg + act * (1.0 - sg))).astype(bf16)
            dy_o[r, :] = dy.astype(bf16)
            ps = xs * dy
            gs[...] += ps[0:8] + ps[8:16]
            edy_o[r, :] = (dy * ee[r, :]).astype(bf16)
            pr[r, :] = (dy * eyi).astype(bf16)

        for t in range(TB // 16):
            strip(slice(t * 16, t * 16 + 16))
        rin_o[...] = dot_nt(pr[...], e2[0:128, :])
        mixed_o[...] = (keep * (u[...].astype(f32) + dot(gn_o[...], obuf[...]))).astype(bf16)
        for k in range(nb):
            r = slice(k * CH, (k + 1) * CH)
            ctr = c_in[r, :].astype(f32).T.astype(bf16)
            for c0 in range(0, di, 256):
                c = slice(c0, c0 + 256)
                dcv = dot(ctr, edy_o[r, c])
                dc_o[k, :, c] = dcv.astype(bf16)
                rg_o[:, c] += ee[TB + 8 * k : TB + 8 * k + 1, c] * dcv

        @pl.when(i == pl.num_programs(0) - 1)
        def _():
            gs_o[...] = head_sums(jnp.sum(gs[...], axis=0, keepdims=True), e2)

    return kernel


def inner_back_kernel(p, h0, h1):
    per = 128 // p

    def kernel(ids, b, c, xd, dy, cc, ct, hot, tok, segr, gxd_o, db_o, dc_o, rk_o, rr):
        si = lax.broadcasted_iota(jnp.int32, (CH, CH), 0)
        ti = lax.broadcasted_iota(jnp.int32, (CH, CH), 1)
        lanes = lax.broadcasted_iota(jnp.int32, (1, 128), 1) // p
        rr[...] = jnp.zeros_like(rr)
        for k in range(b.shape[0] // CH):
            r = slice(k * CH, (k + 1) * CH)
            st = dot_nt(b[r, :], c[r, :])
            bias = jnp.where((tok[r, 0:1] == segr[:, r]) & (ti >= si), 0.0, -1e30)
            gsum = jnp.zeros((CH, CH), f32)
            ksum = jnp.zeros((CH, 128), f32)
            for j in range((h1 - h0) // per):
                xp = xd[r, 128 * j : 128 * j + 128]
                dyp = dy[r, 128 * j : 128 * j + 128]
                dys = jnp.concatenate(
                    [dyp * (lanes == q).astype(f32).astype(bf16) for q in range(per)], axis=0
                )
                gm = dot_nt(xp, dys)
                ms, exs = [], []
                for q in range(per):
                    h = h0 + per * j + q
                    e = jnp.exp2(ct[h : h + 1, r] - cc[r, h : h + 1] + bias)
                    ms.append((st * e).astype(bf16))
                    ge = gm[:, q * CH : (q + 1) * CH] * e
                    gsum = gsum + ge
                    ex = (ge * st).astype(bf16)
                    exs.append(ex)
                    rr[h : h + 1, r] = jnp.sum(ex.astype(f32), axis=0, keepdims=True)
                ksum = ksum + dot(jnp.concatenate(exs, axis=1), hot[per * CH * j : per * CH * (j + 1), :])
                out = dot(jnp.concatenate(ms, axis=1), dys)
                gxd_o[r, 128 * j : 128 * j + 128] = out.astype(bf16)
            rk_o[r, :] = rr[:, r].T - ksum
            db_o[r, :] = dot(gsum.astype(bf16), c[r, :])
            dc_o[r, :] = dot(gsum.T.astype(bf16), b[r, :])

    return kernel


def back_kernel(w, n, h0, h1, last_part):
    cols = w + 2 * n if last_part else w

    def kernel(ids, x_in, b_in, slope, xbc, xbce, xd, dts, cc, tok, elink, gxd, dbi, dci, rk, rin,
               dy, edy, sf, dcs, gend, cw, dsk, nr, e2, *rest):
        if last_part:
            slope2, xbc2, xbce2, cw2, dbp, dcp, ddtp, gsk = rest[:8]
            gp_o, edge_o, sum_o = rest[8:11]
        else:
            gp_o, edge_o, sum_o, dbp_o, dcp_o, ddtp_o = rest[:6]
        ds, sp, sr, ext, xq, xe, gw_o, gb_o, ga_o, gdt_o = rest[-10:]
        i = pl.program_id(0)
        nb = TB // CH

        def pick(a, a2, r, c0):
            return a[r, c0 : c0 + 256] if c0 < w else a2[r, c0 - w : c0 - w + 256]

        @pl.when(i == 0)
        def _():
            ds[...] = gend[...].astype(f32)
            ext[TB : TB + 8, :] = jnp.zeros((8, cols), f32)
            gw_o[...] = jnp.zeros_like(gw_o)
            gb_o[...] = jnp.zeros_like(gb_o)
            ga_o[...] = jnp.zeros_like(ga_o)
            gdt_o[...] = jnp.zeros_like(gdt_o)

        if not last_part:
            slope2 = xbc2 = xbce2 = cw2 = None
        dt = dts[:, :128]
        pieces, leaves = [dt], []
        for k in range(nb):
            r = slice(k * CH, (k + 1) * CH)
            c2 = cc[r, :]
            pieces.append(jnp.exp2(c2[CH - 1 :] - c2) * tok[r, 2:3])
            leaves.append(jnp.exp2(c2[CH - 1 :]) * tok[(k + 1) * CH - 1 : (k + 1) * CH, 1:2])
        lv = jnp.concatenate([jnp.broadcast_to(v, (8, 128)) for v in leaves], axis=0)
        sp[...] = spread(jnp.concatenate(pieces + [lv], axis=0), e2[...])
        lsum = [None] * nb
        for k in reversed(range(nb)):
            r = slice(k * CH, (k + 1) * CH)
            lacc = []
            gb = dbi[r, :]
            gc = dci[r, :]
            for c0 in range(0, w, 256):
                c = slice(c0, c0 + 256)
                dsv = ds[:, c]
                dsb = dsv.astype(bf16)
                sfv = sf[k, :, c]
                sr[r, c] = dot(b_in[r, :], dsb)
                xwv = (xd[r, c].astype(f32) * sp[TB + k * CH : TB + (k + 1) * CH, c]).astype(bf16)
                gb = gb + dot_nt(xwv, dsb)
                gc = gc + dot_nt(edy[r, c], sfv)
                lacc.append(jnp.sum(dsv * sfv.astype(f32), axis=0, keepdims=True))
                lvr = sp[2 * TB + 8 * k : 2 * TB + 8 * k + 1, c]
                ds[:, c] = lvr * dsv + dcs[k, :, c].astype(f32)
            lsum[k] = head_sums(jnp.concatenate(lacc, axis=1), e2)[0:1]
            if last_part:
                ext[r, w : w + n] = (gb + dbp[r, :]) * slope2[r, :n].astype(f32)
                ext[r, w + n :] = (gc + dcp[r, :]) * slope2[r, n:].astype(f32)
            else:
                dbp_o[r, :] = gb
                dcp_o[r, :] = gc

        def strip(r, re):
            x = x_in[r, :].astype(f32)
            es = sp[re, :] * sr[r, :]
            q = gxd[r, :].astype(f32) + es
            gx = sp[r, :] * q + dsk[...] * dy[r, :].astype(f32)
            ext[r, 0:w] = gx * slope[r, :].astype(f32)
            xq[r, :] = (x * q).astype(bf16)
            xe[r, :] = (x * es).astype(bf16)

        for t in range(TB // 16):
            strip(slice(t * 16, t * 16 + 16), slice(TB + t * 16, TB + t * 16 + 16))
        gdt = dot_nt(xq[...], e2[0:128, :])
        et = dot_nt(xe[...], e2[0:128, :]) * dt
        ri = lax.broadcasted_iota(jnp.int32, (CH, CH), 0)
        ci = lax.broadcasted_iota(jnp.int32, (CH, CH), 1)
        hl = lax.broadcasted_iota(jnp.int32, (1, 128), 1)
        hm = ((hl >= h0) & (hl < h1)).astype(f32)
        tri = jnp.concatenate([(ci >= ri).astype(f32), (ci < ri).astype(f32)], axis=1)
        for k in range(nb):
            r = slice(k * CH, (k + 1) * CH)
            v = jnp.concatenate([rk[r, :] + rin[r, :] * hm, et[r]], axis=0)
            ga = jnp.dot(tri, v, precision=HIGH, preferred_element_type=f32) + lsum[k] * leaves[k]
            ddt = (gdt[r] + ga * nr[...]) * dts[r, 128:]
            gad = ga * dts[r, :128]
            acc_a, acc_d = gad[0:8], ddt[0:8]
            for q in range(8, CH, 8):
                acc_a = acc_a + gad[q : q + 8]
                acc_d = acc_d + ddt[q : q + 8]
            ga_o[...] += acc_a
            gdt_o[...] += acc_d
            if last_part:
                gp_o[r, cols:] = (ddt + ddtp[r, :]).astype(bf16)
            else:
                ddtp_o[r, :] = ddt
        for r0 in range(0, TB, 64):
            rs = slice(r0, r0 + 64)
            for c0 in range(0, cols, 256):
                c = slice(c0, c0 + 256)
                g0 = ext[rs, c]
                xb = pick(xbc, xbc2, rs, c0).astype(f32)
                gsum = pick(cw, cw2, slice(3, 4), c0) * g0
                ws = [None, None, None, g0 * xb]
                for s in (1, 2, 3):
                    gs = ext[r0 + s : r0 + s + 64, c] * tok[rs, 6 + s : 7 + s]
                    gsum = gsum + pick(cw, cw2, slice(3 - s, 4 - s), c0) * gs
                    ws[3 - s] = gs * xb
                gp_o[rs, c] = gsum.astype(bf16)
                gb = g0[0:8]
                for q in range(8, 64, 8):
                    gb = gb + g0[q : q + 8]
                gb_o[:, c] += gb
                for o in range(4):
                    v = ws[o][0:8]
                    for q in range(8, 64, 8):
                        v = v + ws[o][q : q + 8]
                    gw_o[8 * o : 8 * o + 8, c] += v
        ext[TB : TB + 8, :] = ext[0:8, :]

        @pl.when(i == pl.num_programs(0) - 1)
        def _():
            zero = jnp.zeros((8, 256), f32)
            for c0 in range(0, cols, 256):
                c = slice(c0, c0 + 256)
                xb = pick(xbce, xbce2, slice(8, 16), c0).astype(f32)
                ext[8:16, c] = ext[TB : TB + 8, c]
                ext[0:8, c] = zero
                gsum = zero
                for s in (1, 2, 3):
                    gs = ext[s : s + 8, c] * elink[:, 6 + s : 7 + s]
                    gsum = gsum + pick(cw, cw2, slice(3 - s, 4 - s), c0) * gs
                    gw_o[8 * (3 - s) : 8 * (3 - s) + 8, c] += gs * xb
                edge_o[:, c] = jnp.concatenate([zero, gsum], axis=0).astype(bf16)
                sums = [jnp.sum(gw_o[8 * o : 8 * o + 8, c], axis=0, keepdims=True) for o in range(4)]
                sums.append(jnp.sum(gb_o[:, c], axis=0, keepdims=True))
                sum_o[:, c] = jnp.concatenate(sums + [zero[0:3]], axis=0)
            sum_o[5:6, 0:128] = jnp.sum(ga_o[...], axis=0, keepdims=True)
            sum_o[6:7, 0:128] = jnp.sum(gdt_o[...], axis=0, keepdims=True)
            if last_part:
                sum_o[7:8, 0:128] = gsk[0:1, :]

    return kernel


def input_kernel(np_, di, conv, heads):
    def kernel(ids, gpz, gpa, gpb, ea, eb, u, e, *rest):
        wz, wx = rest[:np_], rest[np_ : 2 * np_]
        gain, gi_o, zbuf, xbuf, gn = rest[2 * np_ :]
        i = pl.program_id(0)

        @pl.when(i == 0)
        def _():
            xbuf[:, conv:] = jnp.zeros((xbuf.shape[0], xbuf.shape[1] - conv), bf16)
            place(zbuf, ids, wz, di)
            place(xbuf, ids, wx, conv + heads)

        wa = gpa.shape[1]
        wd = u.shape[1]
        last = (i == pl.num_programs(0) - 1).astype(f32)
        for c0 in range(0, wd, 256):
            c = slice(c0, c0 + 256)
            g = dot_nt(gpz[...], zbuf[c, :]) + dot_nt(gpa[...], xbuf[c, :wa]) + dot_nt(gpb[...], xbuf[c, wa:])
            tail = (dot_nt(ea[...], xbuf[c, :wa]) + dot_nt(eb[...], xbuf[c, wa:conv])) * last
            gn[: TB - 16, c] = g[: TB - 16]
            gn[TB - 16 :, c] = g[TB - 16 :] + tail
        for r0 in range(0, TB, 16):
            r = slice(r0, r0 + 16)
            uf = u[r, :].astype(f32)
            scale = lax.rsqrt(jnp.mean(uf * uf, axis=-1, keepdims=True) + EPS)
            unit = uf * scale
            dn = gn[r, :] * gain[...]
            m = jnp.mean(dn * unit, axis=-1, keepdims=True)
            gi_o[r, :] = (e[r, :].astype(f32) + scale * (dn - unit * m)).astype(bf16)

    return kernel


def swap(v, axis, bit):
    return lax.ppermute(v, axis, [(k, k ^ bit) for k in range(lax.axis_size(axis))])


def shift(v, axis, steps):
    n = lax.axis_size(axis)
    return lax.ppermute(v, axis, [(k, k + steps) for k in range(n) if 0 <= k + steps < n])


def bits_of(n):
    return [1 << k for k in reversed(range((n - 1).bit_length()))]


def after(v, dep):
    if dep is None:
        return v
    return lax.optimization_barrier((v, dep))[0]


def gather_parts(v, axis):
    parts = [v]
    for bit in bits_of(lax.axis_size(axis)):
        parts = parts + [swap(p, axis, bit) for p in parts]
    return parts


def in_order(parts, axis):
    at = lax.axis_index(axis)
    n = lax.axis_size(axis)
    v = jnp.stack(parts)
    rest = v.shape[1:]
    bits = bits_of(n)
    v = v.reshape((2,) * len(bits) + rest)
    for k, bit in enumerate(reversed(bits)):
        v = jnp.where((at // bit) % 2 == 0, v, jnp.flip(v, k))
    order = tuple(reversed(range(len(bits))))
    return v.transpose(order + tuple(range(len(bits), v.ndim))).reshape((n,) + rest)


def part_ids(axis):
    ids = [lax.axis_index(axis)]
    for bit in bits_of(lax.axis_size(axis)):
        ids = ids + [k ^ bit for k in ids]
    return ids


def add(a, b):
    return (a.astype(f32) + b.astype(f32)).astype(bf16)


def pair_steps(gs):
    nw = lax.axis_size("wshard")
    w = lax.axis_index("wshard")
    n = min(g.shape[0] for g in gs) // nw

    def pick(at):
        out = []
        for g in gs:
            v = g.reshape(nw // 2, 2, -1, g.shape[-1])
            v = lax.dynamic_index_in_dim(v, at, 1, keepdims=False)
            k = v.shape[1] // n
            out += [v[:, q * n : (q + 1) * n] for q in range(k)]
        return jnp.concatenate(out, axis=2) if len(out) > 1 else out[0]

    send, keep = pick(1 - w % 2), pick(w % 2)
    dep = yield send
    yield add(keep, swap(after(send, dep), "wshard", 1))


def other_steps(v):
    nw = lax.axis_size("wshard")
    w = lax.axis_index("wshard")
    n = v.shape[1]
    for bit in [1 << k for k in range(1, (nw - 1).bit_length())]:
        at = (w // bit) % 2
        v = v.reshape(-1, 2, n, v.shape[-1]).swapaxes(0, 1)
        send = lax.dynamic_index_in_dim(v, 1 - at, 0, keepdims=False)
        keep = lax.dynamic_index_in_dim(v, at, 0, keepdims=False)
        dep = yield send
        v = add(keep, swap(after(send, dep), "wshard", bit))
    yield v.reshape(n, -1)


def pairs_of(n):
    bits = [1 << k for k in range((n - 1).bit_length())]
    return [bits[k : k + 2] for k in range(0, len(bits), 2)]


def swap_all(parts, axis, bits):
    got = parts[:1]
    for m in range(1, 1 << len(bits)):
        got.append(swap(parts[m], axis, sum(bit for k, bit in enumerate(bits) if (m >> k) & 1)))
    return got


def by_index(got, at, bits):
    for k, bit in enumerate(bits):
        here = (at // bit) % 2 == 1
        got = [jnp.where(here, got[m ^ (1 << k)], got[m]) for m in range(len(got))]
    return got


def seq_steps(v):
    groups = pairs_of(lax.axis_size("seq"))
    s = lax.axis_index("seq")
    single = groups.pop() if len(groups[-1]) == 1 else None
    for bits in groups:
        n = 1 << len(bits)
        at = (s // bits[0]) % n
        v = v.reshape(n, -1, v.shape[-1])
        send = [lax.dynamic_index_in_dim(v, at ^ m, 0, keepdims=False) for m in range(n)]
        dep = yield tuple(send)
        got = swap_all(after(send, dep), "seq", bits)
        v = sum(g.astype(f32) for g in got).astype(bf16)
    if single:
        dep = yield v
        v = add(v, swap(after(v, dep), "seq", single[0]))
    for bits in reversed(groups):
        dep = yield v
        v = after(v, dep)
        got = swap_all([v] * (1 << len(bits)), "seq", bits)
        dep = yield tuple(got[1:])
        v = jnp.concatenate(by_index(after(tuple(got), dep), s, bits), axis=0)
    yield v.astype(f32)


def small_steps(v):
    for axis in ("wshard", "seq"):
        at = lax.axis_index(axis)
        for bits in pairs_of(lax.axis_size(axis)):
            dep = yield v
            v = after(v, dep)
            v = sum(by_index(swap_all([v] * (1 << len(bits)), axis, bits), at, bits))
    yield v


def pack_state(decay, state):
    hi, lo = two(decay)
    return jnp.concatenate([state.astype(bf16), hi, lo], axis=0)


def unpack_state(v, n):
    return v[n : n + 8].astype(f32)[:1] + v[n + 8 : n + 16].astype(f32)[:1], v[:n].astype(f32)


def carried(decay, state, sign, tokens):
    n = state.shape[0]
    span = 1
    while span < -(-LONGEST // tokens):
        send = pack_state(decay, state)
        dep = yield send
        d, s = unpack_state(shift(after(send, dep), "seq", sign * span), n)
        state = state + decay[:1] * s
        decay = decay * d
        span *= 2
    send = state.astype(bf16)
    dep = yield send
    yield shift(after(send, dep), "seq", sign)


class Steps:
    def __init__(self, gen):
        self.gen = gen
        self.value = next(gen)

    def step(self, dep=None):
        try:
            self.value = self.gen.send(dep)
        except StopIteration:
            pass
        return self.value

    def finish(self):
        for self.value in self.gen:
            pass
        return self.value


def body(inputs, cotangent, lengths, in_proj, out_proj, conv_weight, conv_bias, a_log, d_skip,
         dt_bias, norm_gain, gate_gain):
    t, d = inputs.shape[1:]
    nw = lax.axis_size("wshard")
    di = out_proj.shape[0] * nw
    heads = a_log.shape[0] * nw
    conv = conv_bias.shape[0] * nw
    taps = conv_weight.shape[0]
    n = (conv - di) // 2
    p = di // heads
    docs = lengths.shape[1]
    nt, nc, nb = t // TB, t // CH, TB // CH
    wide = conv + 128
    wx, wz = in_proj[:, di:], in_proj[:, :di]
    pc = conv // nw
    width = -(-max(pc, di // nw, 384) // 128) * 128


    def line(*vs):
        vs = [v if v.ndim == 2 else v[None] for v in vs]
        vs = [jnp.pad(v, ((0, 0), (0, (width if k == len(vs) - 1 else 128 * (k + 1)) - 128 * k - v.shape[1])))
              for k, v in enumerate(vs)]
        return jnp.concatenate(vs, axis=1)

    small = jnp.concatenate(
        [line(conv_weight), line(conv_bias), line(gate_gain), line(norm_gain), line(a_log, d_skip, dt_bias)], axis=0)
    wx_parts = gather_parts(wx, "wshard")
    small = in_order(gather_parts(after(small, wx_parts[nw // 2]), "wshard"), "wshard").astype(f32)
    wz_parts = gather_parts(after(wz, wx_parts[1]), "wshard")
    wo_parts = gather_parts(after(out_proj, wx_parts[1]), "wshard")
    ids = jnp.stack(part_ids("wshard")).astype(jnp.int32)
    hw = heads // nw
    cw = small[:, :taps, :pc].swapaxes(0, 1).reshape(taps, conv)
    cb = small[:, taps, :pc].reshape(1, conv)
    gain_gate = small[:, taps + 1, : di // nw].reshape(1, di)
    gain_in = small[:, taps + 2, : d // nw].reshape(1, d)
    log_rate, skip, dtb = [small[:, taps + 3, 128 * k : 128 * k + hw].reshape(1, heads) for k in range(3)]
    rate = -jnp.exp(log_rate)
    pad = ((0, 0), (0, 128 - heads))
    nr = jnp.pad(rate, pad)
    nr2 = nr * LOG2E
    dtb = jnp.pad(dtb, pad)
    dsk = jnp.repeat(skip, p, axis=1)
    head_of = jnp.arange(di, dtype=jnp.int32) // p
    e1 = (jnp.arange(128, dtype=jnp.int32)[:, None] == head_of[None]).astype(bf16)
    e2 = jnp.concatenate([e1, e1], axis=0)
    lane = jnp.arange(128, dtype=jnp.int32)
    block = jnp.arange(heads * CH, dtype=jnp.int32) // CH
    hot = (block[:, None] == lane[None]).astype(bf16)
    first = lax.axis_index("seq") * t
    pos = first - 8 + jnp.arange(t + 16, dtype=jnp.int32)
    ends = jnp.cumsum(lengths[0], dtype=jnp.int32)
    seg = jnp.sum((pos[:, None] >= ends[None]).astype(jnp.int32), axis=1)
    seg = jnp.where(pos < 0, -1, seg)
    here = seg[: t + 8]
    own = seg[8 : t + 8]
    entering = jnp.repeat(seg[7 : t + 7 : CH], CH)
    leaving = jnp.repeat(seg[7 + CH : t + 8 : CH], CH)
    zero8 = jnp.zeros((8,), jnp.int32)
    back = [jnp.concatenate([zero8, (seg[8 - k : t + 8 - k] == own).astype(jnp.int32)]) for k in (3, 2, 1)]
    ahead = [(seg[k : t + 8 + k] == here).astype(jnp.int32) for k in (1, 2, 3)]
    cols = [here, jnp.concatenate([zero8, (entering == own).astype(jnp.int32)]),
            jnp.concatenate([zero8, (leaving == own).astype(jnp.int32)])]
    cols = cols + back + [(here < docs).astype(jnp.int32)] + ahead + [jnp.zeros_like(here)] * 6
    tok_all = jnp.stack(cols, axis=1).astype(f32)
    tok, elink = tok_all[8:], tok_all[:8]
    segr = own.astype(f32)[None]
    u, cot = inputs[0], cotangent[0]
    ue = shift(u[t - 16 :], "seq", 1)

    outs = [
        (rows(TB, d), (t, d), bf16),
        (rows(TB, conv), (t, conv), bf16),
        (rows(TB, conv), (t, conv), bf16),
        (rows(TB, conv), (t, conv), bf16),
        (rows(TB, di), (t, di), bf16),
        (rows(TB, 256), (t, 256), f32),
        (rows(TB, 128), (t, 128), f32),
        (pl.BlockSpec((32, TB), lambda i, s: (0, i)), (32, t), f32),
        (pl.BlockSpec((nb, n, di), lambda i, s: (i, 0, 0)), (nc, n, di), bf16),
        (pl.BlockSpec((nb, 8, 128), lambda i, s: (i, 0, 0)), (nc, 8, 128), f32),
        (whole((n, di)), (n, di), f32),
        (whole((8, di)), (8, di), f32),
        (whole((16, d)), (16, d), bf16),
        (whole((16, conv)), (16, conv), bf16),
    ]
    ins = [rows(TB, d), whole((16, d)), whole((1, d))] + [whole(v.shape) for v in wx_parts]
    ins += [whole((taps, conv)), whole((1, conv)), whole((1, 128)), whole((1, 128)), rows(TB, 16), whole((256, di))]
    scratch = [
        pltpu.VMEM((d, wide), bf16),
        pltpu.VMEM((TB + 8, conv), f32),
        pltpu.VMEM((n, di), f32),
        pltpu.VMEM((1, 128), f32),
        pltpu.VMEM((2 * TB + 8 * nb, di), f32),
    ]
    (nrm, xbc, xc, slope, xd, dts, cc, ct, st, dbf, end, tot, nrme, xbce) = call(
        front_kernel(nw, di, conv, heads), (nt,), ins, outs, scratch, 15,
        [ids, u, ue, gain_in] + wx_parts + [cw, cb, dtb, nr2, tok, e2], "front")
    chain = Steps(carried(tot, end, 1, t))
    chain.step(wz_parts[1])
    chain.step()
    chain.step(wo_parts[1])
    incoming = chain.finish()

    crow = pl.BlockSpec((32, TI), lambda i, s: (0, i))
    srow = pl.BlockSpec((1, TI), lambda i, s: (0, i))
    crow2 = pl.BlockSpec((32, CH), lambda i, s: (0, i))
    srow2 = pl.BlockSpec((1, CH), lambda i, s: (0, i))
    bspec, cspec = rows(TI, n, di // n), rows(TI, n, di // n + 1)
    (yin,) = call(
        inner_kernel(heads, di), (t // TI,),
        [bspec, cspec, rows(TI, di), rows(TI, 128), crow, rows(TI, 16), srow],
        [(rows(TI, di), (t, di), bf16)], [], 10,
        [ids, xc, xc, xd, cc, ct, tok, segr], "inner")

    blk = pl.BlockSpec((nb, n, di), lambda i, s: (i, 0, 0))
    outs = [
        (rows(TB, d), (t, d), bf16),
        (rows(TB, di), (t, di), bf16),
        (rows(TB, di), (t, di), bf16),
        (rows(TB, di), (t, di), bf16),
        (rows(TB, di), (t, di), bf16),
        (rows(TB, d), (t, d), bf16),
        (blk, (nc, n, di), bf16),
        (blk, (nc, n, di), bf16),
        (rows(TB, 128), (t, 128), f32),
        (whole((8, 128)), (8, 128), f32),
        (whole((n, di)), (n, di), f32),
    ]
    ins = [rows(TB, d), rows(TB, di), rows(TB, di), rows(TB, n, di // n + 1), rows(TB, 128), rows(TB, 16), blk,
           pl.BlockSpec((nb, 8, 128), lambda i, s: (i, 0, 0)), whole((n, di)), rows(TB, d), rows(TB, d)]
    ins += [whole(v.shape) for v in wz_parts + wo_parts]
    ins += [whole((1, di)), whole((1, di)), whole((256, di))]
    scratch = [pltpu.VMEM((d, di), bf16), pltpu.VMEM((di, d), bf16)]
    scratch += [pltpu.VMEM((TB, di), f32)] * 3
    scratch += [pltpu.VMEM((TB + 8 * nb, di), f32), pltpu.VMEM((TB, di), bf16), pltpu.VMEM((8, di), f32)]
    (mixed, gn, dz, dy, edy, e, sf, dcs, rin, g_skip, reach) = call(
        gate_kernel(nw, di, d), (nt,), ins, outs, scratch, 25,
        [ids, nrm, yin, xc, xc, cc, tok, st, dbf, incoming, u, cot] + wz_parts + wo_parts + [gain_gate, dsk, e2], "gate")
    tn = (((0,), (0,)), ((), ()))

    def outer(a, b):
        return lax.dot_general(a, b, tn, preferred_element_type=f32)

    back_state = Steps(carried(tot, reach, -1, t))
    s1 = back_state.value
    gw_out = outer(after(gn, s1), e).astype(bf16)
    gw_z = outer(nrm, after(dz, s1)).astype(bf16)
    s2 = back_state.step()
    oz_p = Steps(pair_steps([gw_out, gw_z]))
    oz_w = Steps(other_steps(oz_p.step(s2)))
    oz2 = oz_w.value
    hh, hw2 = heads // 2, di // 2

    def at(shape, col):
        return pl.BlockSpec(shape, lambda i, s: (0, col))

    def half_inner(k, dep):
        outs = [
            (rows(CH, hw2), (t, hw2), bf16),
            (rows(CH, n), (t, n), f32),
            (rows(CH, n), (t, n), f32),
            (rows(CH, 128), (t, 128), f32),
        ]
        return call(
            inner_back_kernel(p, hh * k, hh * (k + 1)), (t // CH,),
            [rows(CH, n, di // n), rows(CH, n, di // n + 1), rows(CH, hw2, k), rows(CH, hw2, k), rows(CH, 128), crow2,
             pl.BlockSpec((hh * CH, 128), lambda i, s: (k, 0)), rows(CH, 16), srow2],
            outs, [pltpu.VMEM((128, CH), f32)], 12,
            [ids, xc, xc, xd, after(dy, dep), cc, ct, hot, tok, segr], "inner_back")

    def rev(block, width, col=0):
        return pl.BlockSpec((block, width), lambda i, s: (nt - 1 - i, col))

    def half_back(k, inner, dep, gend, extra):
        gxd, dbi, dci, rk = inner
        last = k == 1
        cols = hw2 + 2 * n if last else hw2
        rblk = pl.BlockSpec((nb, n, hw2), lambda i, s: (nt - 1 - i, 0, k))
        ins = [rev(TB, hw2, k), rev(TB, n, di // n), rev(TB, hw2, k), rev(TB, hw2, k), at((16, hw2), k),
               rev(TB, hw2, k), rev(TB, 256), rev(TB, 128), rev(TB, 16), whole((8, 16)), rev(TB, hw2),
               rev(TB, n), rev(TB, n), rev(TB, 128), rev(TB, 128), rev(TB, hw2, k), rev(TB, hw2, k), rblk, rblk,
               at((n, hw2), k), at((taps, hw2), k), at((1, hw2), k), whole((1, 128)), at((256, hw2), k)]
        args = [ids, xc, xc, slope, xbc, xbce, xd, dts, cc, tok, elink, after(gxd, dep), dbi, dci, rk, rin, dy,
                edy, sf, dcs, gend, cw, dsk, nr, e2]
        outs = [
            (rev(TB, cols + 128 * last), (t, cols + 128 * last), bf16),
            (whole((16, cols)), (16, cols), bf16),
            (whole((8, cols)), (8, cols), f32),
        ]
        if last:
            ins += [rev(TB, 2 * n, di // (2 * n)), rev(TB, 2 * n, di // (2 * n)), at((16, 2 * n), di // (2 * n)),
                    at((taps, 2 * n), di // (2 * n)), rev(TB, n), rev(TB, n), rev(TB, 128), whole((8, 128))]
            args += [slope, xbc, xbce, cw] + list(extra)
        else:
            outs += [(rev(TB, n), (t, n), f32), (rev(TB, n), (t, n), f32), (rev(TB, 128), (t, 128), f32)]
        scratch = [
            pltpu.VMEM((n, hw2), f32),
            pltpu.VMEM((2 * TB + 8 * nb, hw2), f32),
            pltpu.VMEM((TB, hw2), f32),
            pltpu.VMEM((TB + 8, cols), f32),
            pltpu.VMEM((TB, hw2), bf16),
            pltpu.VMEM((TB, hw2), bf16),
            pltpu.VMEM((8 * taps, cols), f32),
            pltpu.VMEM((8, cols), f32),
            pltpu.VMEM((8, 128), f32),
            pltpu.VMEM((8, 128), f32),
        ]
        return call(back_kernel(hw2, n, hh * k, hh * (k + 1), last), (nt,), ins, outs, scratch, 15, args, "back")

    in_a = half_inner(0, (s2, oz2))
    s3 = back_state.step(oz2)
    s3, in_a0 = lax.optimization_barrier((s3, in_a[0]))
    in_b = half_inner(1, (s3, in_a0))
    back_state.step(in_a[0])
    gend = back_state.finish()
    oz_w.step()
    oz_s = Steps(seq_steps(oz_w.finish()))
    oz3 = oz_s.value
    (gpa, edge_a, sum_a, dbp, dcp, ddtp) = half_back(0, in_a, (in_b[0], oz3), gend, None)
    oz4 = oz_s.step(in_b[0])
    gw_xa = (outer(nrm, after(gpa, oz4)) + outer(nrme, edge_a)).astype(bf16)
    xa_p = Steps(pair_steps([gw_xa]))
    xa1 = xa_p.value
    (gpb, edge_b, sum_b) = half_back(1, in_b, (oz4, xa1), gend, (dbp, dcp, ddtp, g_skip))
    oz5 = oz_s.step(gpa)
    oz5, gpb_late = lax.optimization_barrier((oz5, gpb))
    gw_xb = outer(nrm, gpb_late)
    cb2 = conv - hw2
    gw_xb = jnp.concatenate(
        [gw_xb[:, :cb2] + outer(nrme, edge_b), gw_xb[:, cb2 : cb2 + heads]], axis=1).astype(bf16)
    xb_p = Steps(pair_steps([gw_xb]))
    x_w = Steps(other_steps(jnp.concatenate([xa_p.step(), xb_p.step()], axis=2)))
    x2 = x_w.value
    oz7 = oz_s.step(gpb)
    ea_in, eb_in = shift(edge_a, "seq", -1), shift(edge_b, "seq", -1)

    ins = [rows(TB, di), rows(TB, hw2), rows(TB, wide - hw2), whole((16, hw2)), whole((16, cb2)), rows(TB, d), rows(TB, d)]
    ins += [whole(v.shape) for v in wz_parts + wx_parts] + [whole((1, d))]
    outs = [(rows(TB, d), (t, d), bf16)]
    (grad_input,) = call(
        input_kernel(nw, di, conv, heads), (nt,), ins, outs,
        [pltpu.VMEM((d, di), bf16), pltpu.VMEM((d, wide), bf16), pltpu.VMEM((TB, d), f32)], 12,
        [ids, dz, after(gpa, x2), gpb, ea_in, eb_in, u, e] + wz_parts + wx_parts + [gain_in], "input")
    sums = Steps(small_steps(jnp.concatenate([sum_a, sum_b], axis=1)))
    x_s = Steps(seq_steps(x_w.finish()))
    x3 = x_s.value
    sums.step((x3, grad_input))
    x4 = x_s.step((grad_input, oz7))
    sums.step(x4)
    oz_s.step(x4)
    x5 = x_s.step()
    sums.step(x5)
    r_x, r_oz, total = x_s.finish(), oz_s.finish(), sums.finish()
    k = r_oz.shape[1] - di
    r_out = jnp.concatenate([r_oz[:, q * d : (q + 1) * d] for q in range(k // d)], axis=0)
    r_z = r_oz[:, k:]
    w = lax.axis_index("wshard")

    def mine(v):
        width = v.shape[-1] // nw
        return lax.dynamic_slice_in_dim(v, w * width, width, axis=v.ndim - 1)

    by_head = total[5:8, :heads] + total[5:8, hw2 : hw2 + heads]
    by_head = mine(by_head * jnp.concatenate([rate, jnp.ones((2, heads), f32)], axis=0))
    res = [mine(total[:taps]), mine(total[taps]), by_head[0], by_head[2], by_head[1]]
    res.append((jnp.sum(r_z * wz.astype(f32), axis=1) + jnp.sum(r_x * wx.astype(f32), axis=1)) / norm_gain.astype(f32))
    res.append(jnp.sum(r_out * out_proj.astype(f32), axis=1) / gate_gain.astype(f32))
    return (mixed[None], grad_input[None], jnp.concatenate([r_z, r_x], axis=1), r_out) + tuple(res)


def solution(mesh):
    wide = P("wshard", "seq", None)
    mat = P("wshard", None)
    taps = P(None, "wshard")
    vec = P("wshard")
    return jax.shard_map(
        body,
        mesh=mesh,
        in_specs=(wide, wide, mat, mat, mat, taps) + (vec,) * 6,
        out_specs=(wide, wide, mat, mat, taps) + (vec,) * 6,
        check_vma=False,
    )
```

```python
import jax
import jax.numpy as jnp
import numpy as np
from jax import lax
from jax.experimental import pallas as pl
from jax.experimental.pallas import tpu as pltpu
from jax.sharding import PartitionSpec as P

f32 = jnp.float32
bf16 = jnp.bfloat16
EPS = 1e-05
LOG2E = 1.4426950408889634
CH = 128
TB = 256
TI = 256
LONGEST = 4096
HIGH = lax.Precision.HIGHEST
MB = 1024 * 1024
VMEM = 60 * MB


def sigmoid(v):
    return 0.5 * jnp.tanh(0.5 * v) + 0.5


def dot(a, b):
    return jnp.dot(a, b, preferred_element_type=f32)


def dot_nt(a, b):
    return lax.dot_general(a, b, (((1,), (1,)), ((), ())), preferred_element_type=f32)


def two(v):
    hi = v.astype(bf16)
    return hi, (v - hi.astype(f32)).astype(bf16)


def spread(v, e2):
    return dot(jnp.concatenate(two(v), axis=1), e2)


def head_sums(row, e2):
    hi, lo = two(jnp.broadcast_to(row, (8, row.shape[1])))
    return dot_nt(hi, e2[0:128, :]) + dot_nt(lo, e2[0:128, :])


def cost(us):
    return pl.CostEstimate(flops=int(us * 1.1e9), bytes_accessed=1 << 20, transcendentals=0)


def call(kernel, grid, ins, outs, scratch, us, args, name):
    return pl.pallas_call(
        kernel,
        grid_spec=pltpu.PrefetchScalarGridSpec(
            num_scalar_prefetch=1,
            grid=grid,
            in_specs=ins,
            out_specs=[o[0] for o in outs],
            scratch_shapes=scratch,
        ),
        out_shape=[jax.ShapeDtypeStruct(o[1], o[2]) for o in outs],
        compiler_params=pltpu.CompilerParams(
            vmem_limit_bytes=VMEM, dimension_semantics=("arbitrary",)
        ),
        cost_estimate=cost(us),
        name=name,
    )(*args)


def rows(block, cols, col=0):
    return pl.BlockSpec((block, cols), lambda i, s: (i, col))


def whole(shape):
    return pl.BlockSpec(shape, lambda i, s: (0,) * len(shape))


def norm_rows(uf, gain):
    scale = lax.rsqrt(jnp.mean(uf * uf, axis=-1, keepdims=True) + EPS)
    return (uf * scale * gain).astype(bf16)


def place(buf, ids, parts, width):
    for j, part in enumerate(parts):
        n = part.shape[0]
        at = pl.multiple_of(ids[j] * n, 64)
        buf[pl.ds(at, n), :width] = part[...]


def put_pack(ref, decay, state):
    n = state.shape[0]
    hi, lo = two(decay)
    ref[0:n, :] = state.astype(bf16)
    ref[n:, :] = jnp.concatenate([hi.astype(f32), lo.astype(f32)], axis=0).astype(bf16)


def front_kernel(np_, di, conv, heads):
    def kernel(ids, u, ue, gain, *rest):
        parts = rest[:np_]
        (cw, cb, dtb, nr, tok, e2, nrm_o, xbc_o, xc_o, slope_o, xd_o, dts_o, cc_o, ct_o,
         st_o, db_o, end_o, tot_o, pk_o, nrme_o, xbce_o, wbuf, ext, state, kd, sp) = rest[np_:]
        i = pl.program_id(0)
        n = (conv - di) // 2

        @pl.when(i == 0)
        def _():
            wbuf[:, conv:] = jnp.zeros((wbuf.shape[0], wbuf.shape[1] - conv), bf16)
            place(wbuf, ids, parts, conv + heads)
            nrme = norm_rows(ue[...].astype(f32), gain[...])
            nrme_o[...] = nrme
            pe = dot(nrme, wbuf[:, :conv]).astype(bf16)
            xbce_o[...] = pe
            ext[0:8, :] = pe.astype(f32)[8:16]
            state[...] = jnp.zeros_like(state)
            kd[...] = jnp.ones_like(kd)

        nrm = norm_rows(u[...].astype(f32), gain[...])
        nrm_o[...] = nrm
        pd = dot(nrm, wbuf[:, conv:])
        for c0 in range(0, conv, 256):
            px = dot(nrm, wbuf[:, c0 : c0 + 256]).astype(bf16)
            xbc_o[:, c0 : c0 + 256] = px
            ext[8 : 8 + TB, c0 : c0 + 256] = px.astype(f32)
        sh = pd + dtb[...]
        dt = jnp.maximum(sh, 0.0) + jnp.log1p(jnp.exp(-jnp.abs(sh)))
        dts_o[:, :128] = dt
        dts_o[:, 128:] = jax.nn.sigmoid(sh)
        a2 = dt * nr[...]
        ri = lax.broadcasted_iota(jnp.int32, (CH, CH), 0)
        ci = lax.broadcasted_iota(jnp.int32, (CH, CH), 1)
        low = (ri >= ci).astype(f32)
        pieces = [dt]
        leaves = []
        for k in range(TB // CH):
            r = slice(k * CH, (k + 1) * CH)
            c2 = jnp.dot(low, a2[r], precision=HIGH, preferred_element_type=f32)
            cc_o[r, :] = c2
            ct_o[:, r] = c2.T[: ct_o.shape[0], :]
            pieces.append(jnp.exp2(c2[CH - 1 :] - c2) * tok[r, 2:3])
            leaves.append(jnp.exp2(c2[CH - 1 :]) * tok[(k + 1) * CH - 1 : (k + 1) * CH, 1:2])
        lv = jnp.concatenate([jnp.broadcast_to(v, (8, 128)) for v in leaves], axis=0)
        sp[...] = spread(jnp.concatenate(pieces + [lv], axis=0), e2[...])
        for r0 in range(0, TB, 64):
            l0, l1, l2 = tok[r0 : r0 + 64, 3:4], tok[r0 : r0 + 64, 4:5], tok[r0 : r0 + 64, 5:6]
            for c0 in range(0, conv, 256):
                c = slice(c0, c0 + 256)
                pre = cb[:, c] + cw[3:4, c] * ext[8 + r0 : 72 + r0, c]
                pre = pre + cw[2:3, c] * (ext[7 + r0 : 71 + r0, c] * l2)
                pre = pre + cw[1:2, c] * (ext[6 + r0 : 70 + r0, c] * l1)
                pre = pre + cw[0:1, c] * (ext[5 + r0 : 69 + r0, c] * l0)
                sg = sigmoid(pre)
                xc = pre * sg
                xc_o[r0 : r0 + 64, c] = xc.astype(bf16)
                slope_o[r0 : r0 + 64, c] = (sg + xc * (1.0 - sg)).astype(bf16)
                if c0 < di:
                    xd_o[r0 : r0 + 64, c] = (xc * sp[r0 : r0 + 64, c]).astype(bf16)
        ext[0:8, :] = ext[TB : TB + 8, :]
        for k in range(TB // CH):
            r = slice(k * CH, (k + 1) * CH)
            st_o[k] = state[...].astype(bf16)
            db_o[k] = jnp.broadcast_to(kd[...], (8, 128))
            bt = xc_o[r, di : di + n].astype(f32).T.astype(bf16)
            for c0 in range(0, di, 256):
                c = slice(c0, c0 + 256)
                xw = (xd_o[r, c].astype(f32) * sp[TB + k * CH : TB + (k + 1) * CH, c]).astype(bf16)
                lvr = sp[2 * TB + 8 * k : 2 * TB + 8 * k + 1, c]
                state[:, c] = lvr * state[:, c] + dot(bt, xw)
            kd[...] = kd[...] * leaves[k]

        @pl.when(i == pl.num_programs(0) - 1)
        def _():
            end_o[...] = state[...]
            total = spread(jnp.broadcast_to(kd[...], (8, 128)), e2[...])
            tot_o[...] = total
            put_pack(pk_o, total, state[...])

    return kernel


def inner_kernel(heads, di):
    p = di // heads
    per = 128 // p

    def kernel(ids, b, c, xd, cc, ct, tok, segr, y_o):
        ri = lax.broadcasted_iota(jnp.int32, (CH, CH), 0)
        ci = lax.broadcasted_iota(jnp.int32, (CH, CH), 1)
        lanes = lax.broadcasted_iota(jnp.int32, (1, 128), 1) // p
        for k in range(b.shape[0] // CH):
            r = slice(k * CH, (k + 1) * CH)
            s = dot_nt(c[r, :], b[r, :])
            bias = jnp.where((tok[r, 0:1] == segr[:, r]) & (ri >= ci), 0.0, -1e30)
            for j in range(heads // per):
                xp = xd[r, 128 * j : 128 * j + 128]
                ms, xs = [], []
                for q in range(per):
                    h = per * j + q
                    e = jnp.exp2(cc[r, h : h + 1] - ct[h : h + 1, r] + bias)
                    ms.append((s * e).astype(bf16))
                    xs.append(xp * (lanes == q).astype(f32).astype(bf16))
                out = dot(jnp.concatenate(ms, axis=1), jnp.concatenate(xs, axis=0))
                y_o[r, 128 * j : 128 * j + 128] = out.astype(bf16)

    return kernel


def gate_kernel(np_, di, d):
    def kernel(ids, nrm, yin, x, c_in, cc, tok, st, db, inc, tot, u, cot, *rest):
        wz, wo = rest[:np_], rest[np_ : 2 * np_]
        (gain, dsk, e2, mixed_o, gn_o, dz_o, dy_o, edy_o, e_o, sf_o, dc_o, rin_o, gs_o,
         rg_o, pk_o, zbuf, obuf, z, yi, dgn, ee, pr, gs) = rest[2 * np_ :]
        i = pl.program_id(0)

        @pl.when(i == 0)
        def _():
            place(zbuf, ids, wz, di)
            place(obuf, ids, wo, d)
            gs[...] = jnp.zeros_like(gs)
            rg_o[...] = jnp.zeros_like(rg_o)

        keep = tok[:, 6:7]
        ef = cot[...].astype(f32) * keep
        e = ef.astype(bf16)
        e_o[...] = e
        nb = TB // CH
        ents = []
        for k in range(nb):
            r = slice(k * CH, (k + 1) * CH)
            ents.append(jnp.exp2(cc[r, :]) * tok[r, 1:2])
        ee[...] = spread(jnp.concatenate(ents + [db[k] for k in range(nb)], axis=0), e2[...])
        for k in range(nb):
            r = slice(k * CH, (k + 1) * CH)
            for c0 in range(0, di, 256):
                c = slice(c0, c0 + 256)
                dbr = ee[TB + 8 * k : TB + 8 * k + 1, c]
                sf = (st[k, :, c].astype(f32) + dbr * inc[:, c].astype(f32)).astype(bf16)
                sf_o[k, :, c] = sf
                yi[r, c] = dot(c_in[r, :], sf)
        z[...] = dot(nrm[...], zbuf[...])
        dgn[...] = dot_nt(e, obuf[...])

        def strip(r):
            xs = x[r, :].astype(f32)
            eyi = ee[r, :] * yi[r, :]
            y = yin[r, :].astype(f32) + eyi + dsk[...] * xs
            zz = z[r, :]
            sg = sigmoid(zz)
            act = zz * sg
            g = y * act
            scale = lax.rsqrt(jnp.mean(g * g, axis=-1, keepdims=True) + EPS)
            ug = g * scale
            gn_o[r, :] = (ug * gain[...]).astype(bf16)
            dg0 = dgn[r, :]
            dn = dg0 * gain[...]
            m = jnp.mean(dn * ug, axis=-1, keepdims=True)
            dg = scale * (dn - ug * m)
            dy = dg * act
            dz_o[r, :] = (dg * y * (sg + act * (1.0 - sg))).astype(bf16)
            dy_o[r, :] = dy.astype(bf16)
            ps = xs * dy
            gs[...] += ps[0:8] + ps[8:16]
            edy_o[r, :] = (dy * ee[r, :]).astype(bf16)
            pr[r, :] = (dy * eyi).astype(bf16)

        for t in range(TB // 16):
            strip(slice(t * 16, t * 16 + 16))
        rin_o[...] = dot_nt(pr[...], e2[0:128, :])
        mixed_o[...] = (keep * (u[...].astype(f32) + dot(gn_o[...], obuf[...]))).astype(bf16)
        for k in range(nb):
            r = slice(k * CH, (k + 1) * CH)
            ctr = c_in[r, :].astype(f32).T.astype(bf16)
            for c0 in range(0, di, 256):
                c = slice(c0, c0 + 256)
                dcv = dot(ctr, edy_o[r, c])
                dc_o[k, :, c] = dcv.astype(bf16)
                rg_o[:, c] += ee[TB + 8 * k : TB + 8 * k + 1, c] * dcv

        @pl.when(i == pl.num_programs(0) - 1)
        def _():
            gs_o[...] = head_sums(jnp.sum(gs[...], axis=0, keepdims=True), e2)
            put_pack(pk_o, tot[...], rg_o[...])

    return kernel


def inner_back_kernel(p, h0, h1):
    per = 128 // p

    def kernel(ids, b, c, xd, dy, cc, ct, hot, tok, segr, gxd_o, db_o, dc_o, rk_o, rr):
        si = lax.broadcasted_iota(jnp.int32, (CH, CH), 0)
        ti = lax.broadcasted_iota(jnp.int32, (CH, CH), 1)
        lanes = lax.broadcasted_iota(jnp.int32, (1, 128), 1) // p
        rr[...] = jnp.zeros_like(rr)
        for k in range(b.shape[0] // CH):
            r = slice(k * CH, (k + 1) * CH)
            st = dot_nt(b[r, :], c[r, :])
            bias = jnp.where((tok[r, 0:1] == segr[:, r]) & (ti >= si), 0.0, -1e30)
            gsum = jnp.zeros((CH, CH), f32)
            ksum = jnp.zeros((CH, 128), f32)
            for j in range((h1 - h0) // per):
                xp = xd[r, 128 * j : 128 * j + 128]
                dyp = dy[r, 128 * j : 128 * j + 128]
                dys = jnp.concatenate(
                    [dyp * (lanes == q).astype(f32).astype(bf16) for q in range(per)], axis=0
                )
                gm = dot_nt(xp, dys)
                ms, exs = [], []
                for q in range(per):
                    h = h0 + per * j + q
                    e = jnp.exp2(ct[h : h + 1, r] - cc[r, h : h + 1] + bias)
                    ms.append((st * e).astype(bf16))
                    ge = gm[:, q * CH : (q + 1) * CH] * e
                    gsum = gsum + ge
                    ex = (ge * st).astype(bf16)
                    exs.append(ex)
                    rr[h : h + 1, r] = jnp.sum(ex.astype(f32), axis=0, keepdims=True)
                ksum = ksum + dot(jnp.concatenate(exs, axis=1), hot[per * CH * j : per * CH * (j + 1), :])
                out = dot(jnp.concatenate(ms, axis=1), dys)
                gxd_o[r, 128 * j : 128 * j + 128] = out.astype(bf16)
            rk_o[r, :] = rr[:, r].T - ksum
            db_o[r, :] = dot(gsum.astype(bf16), c[r, :])
            dc_o[r, :] = dot(gsum.T.astype(bf16), b[r, :])

    return kernel


def back_kernel(w, n, h0, h1, last_part):
    cols = w + 2 * n if last_part else w

    def kernel(ids, x_in, b_in, slope, xbc, xbce, xd, dts, cc, tok, elink, gxd, dbi, dci, rk, rin,
               dy, edy, sf, dcs, gend, cw, dsk, nr, e2, *rest):
        if last_part:
            slope2, xbc2, xbce2, cw2, dbp, dcp, ddtp, gsk = rest[:8]
            gp_o, edge_o, sum_o = rest[8:11]
        else:
            gp_o, edge_o, sum_o, dbp_o, dcp_o, ddtp_o = rest[:6]
        ds, sp, sr, ext, xq, xe, gw_o, gb_o, ga_o, gdt_o = rest[-10:]
        i = pl.program_id(0)
        nb = TB // CH

        def pick(a, a2, r, c0):
            return a[r, c0 : c0 + 256] if c0 < w else a2[r, c0 - w : c0 - w + 256]

        @pl.when(i == 0)
        def _():
            ds[...] = gend[...].astype(f32)
            ext[TB : TB + 8, :] = jnp.zeros((8, cols), f32)
            gw_o[...] = jnp.zeros_like(gw_o)
            gb_o[...] = jnp.zeros_like(gb_o)
            ga_o[...] = jnp.zeros_like(ga_o)
            gdt_o[...] = jnp.zeros_like(gdt_o)

        if not last_part:
            slope2 = xbc2 = xbce2 = cw2 = None
        dt = dts[:, :128]
        pieces, leaves = [dt], []
        for k in range(nb):
            r = slice(k * CH, (k + 1) * CH)
            c2 = cc[r, :]
            pieces.append(jnp.exp2(c2[CH - 1 :] - c2) * tok[r, 2:3])
            leaves.append(jnp.exp2(c2[CH - 1 :]) * tok[(k + 1) * CH - 1 : (k + 1) * CH, 1:2])
        lv = jnp.concatenate([jnp.broadcast_to(v, (8, 128)) for v in leaves], axis=0)
        sp[...] = spread(jnp.concatenate(pieces + [lv], axis=0), e2[...])
        lsum = [None] * nb
        for k in reversed(range(nb)):
            r = slice(k * CH, (k + 1) * CH)
            lacc = []
            gb = dbi[r, :]
            gc = dci[r, :]
            for c0 in range(0, w, 256):
                c = slice(c0, c0 + 256)
                dsv = ds[:, c]
                dsb = dsv.astype(bf16)
                sfv = sf[k, :, c]
                sr[r, c] = dot(b_in[r, :], dsb)
                xwv = (xd[r, c].astype(f32) * sp[TB + k * CH : TB + (k + 1) * CH, c]).astype(bf16)
                gb = gb + dot_nt(xwv, dsb)
                gc = gc + dot_nt(edy[r, c], sfv)
                lacc.append(jnp.sum(dsv * sfv.astype(f32), axis=0, keepdims=True))
                lvr = sp[2 * TB + 8 * k : 2 * TB + 8 * k + 1, c]
                ds[:, c] = lvr * dsv + dcs[k, :, c].astype(f32)
            lsum[k] = head_sums(jnp.concatenate(lacc, axis=1), e2)[0:1]
            if last_part:
                ext[r, w : w + n] = (gb + dbp[r, :]) * slope2[r, :n].astype(f32)
                ext[r, w + n :] = (gc + dcp[r, :]) * slope2[r, n:].astype(f32)
            else:
                dbp_o[r, :] = gb
                dcp_o[r, :] = gc

        def strip(r, re):
            x = x_in[r, :].astype(f32)
            es = sp[re, :] * sr[r, :]
            q = gxd[r, :].astype(f32) + es
            gx = sp[r, :] * q + dsk[...] * dy[r, :].astype(f32)
            ext[r, 0:w] = gx * slope[r, :].astype(f32)
            xq[r, :] = (x * q).astype(bf16)
            xe[r, :] = (x * es).astype(bf16)

        for t in range(TB // 16):
            strip(slice(t * 16, t * 16 + 16), slice(TB + t * 16, TB + t * 16 + 16))
        gdt = dot_nt(xq[...], e2[0:128, :])
        et = dot_nt(xe[...], e2[0:128, :]) * dt
        ri = lax.broadcasted_iota(jnp.int32, (CH, CH), 0)
        ci = lax.broadcasted_iota(jnp.int32, (CH, CH), 1)
        hl = lax.broadcasted_iota(jnp.int32, (1, 128), 1)
        hm = ((hl >= h0) & (hl < h1)).astype(f32)
        tri = jnp.concatenate([(ci >= ri).astype(f32), (ci < ri).astype(f32)], axis=1)
        for k in range(nb):
            r = slice(k * CH, (k + 1) * CH)
            v = jnp.concatenate([rk[r, :] + rin[r, :] * hm, et[r]], axis=0)
            ga = jnp.dot(tri, v, precision=HIGH, preferred_element_type=f32) + lsum[k] * leaves[k]
            ddt = (gdt[r] + ga * nr[...]) * dts[r, 128:]
            gad = ga * dts[r, :128]
            acc_a, acc_d = gad[0:8], ddt[0:8]
            for q in range(8, CH, 8):
                acc_a = acc_a + gad[q : q + 8]
                acc_d = acc_d + ddt[q : q + 8]
            ga_o[...] += acc_a
            gdt_o[...] += acc_d
            if last_part:
                gp_o[r, cols:] = (ddt + ddtp[r, :]).astype(bf16)
            else:
                ddtp_o[r, :] = ddt
        for r0 in range(0, TB, 64):
            rs = slice(r0, r0 + 64)
            links = [jnp.broadcast_to(tok[rs, 6 + s : 7 + s], (64, 256)) for s in (1, 2, 3)]
            for c0 in range(0, cols, 256):
                c = slice(c0, c0 + 256)
                g0 = ext[rs, c]
                xb = pick(xbc, xbc2, rs, c0).astype(f32)
                gsum = pick(cw, cw2, slice(3, 4), c0) * g0
                ws = [None, None, None, g0 * xb]
                for s in (1, 2, 3):
                    gs = ext[r0 + s : r0 + s + 64, c] * links[s - 1]
                    gsum = gsum + pick(cw, cw2, slice(3 - s, 4 - s), c0) * gs
                    ws[3 - s] = gs * xb
                gp_o[rs, c] = gsum.astype(bf16)
                gb = g0[0:8]
                for q in range(8, 64, 8):
                    gb = gb + g0[q : q + 8]
                gb_o[:, c] += gb
                for o in range(4):
                    v = ws[o][0:8]
                    for q in range(8, 64, 8):
                        v = v + ws[o][q : q + 8]
                    gw_o[8 * o : 8 * o + 8, c] += v
        ext[TB : TB + 8, :] = ext[0:8, :]

        @pl.when(i == pl.num_programs(0) - 1)
        def _():
            zero = jnp.zeros((8, 256), f32)
            for c0 in range(0, cols, 256):
                c = slice(c0, c0 + 256)
                xb = pick(xbce, xbce2, slice(8, 16), c0).astype(f32)
                ext[8:16, c] = ext[TB : TB + 8, c]
                ext[0:8, c] = zero
                gsum = zero
                for s in (1, 2, 3):
                    gs = ext[s : s + 8, c] * elink[:, 6 + s : 7 + s]
                    gsum = gsum + pick(cw, cw2, slice(3 - s, 4 - s), c0) * gs
                    gw_o[8 * (3 - s) : 8 * (3 - s) + 8, c] += gs * xb
                edge_o[:, c] = jnp.concatenate([zero, gsum], axis=0).astype(bf16)
                sums = [jnp.sum(gw_o[8 * o : 8 * o + 8, c], axis=0, keepdims=True) for o in range(4)]
                sums.append(jnp.sum(gb_o[:, c], axis=0, keepdims=True))
                sum_o[:, c] = jnp.concatenate(sums + [zero[0:3]], axis=0)
            sum_o[5:6, 0:128] = jnp.sum(ga_o[...], axis=0, keepdims=True)
            sum_o[6:7, 0:128] = jnp.sum(gdt_o[...], axis=0, keepdims=True)
            if last_part:
                sum_o[7:8, 0:128] = gsk[0:1, :]

    return kernel


def input_kernel(np_, di, conv, heads):
    def kernel(ids, gpz, gpa, gpb, ea, eb, u, e, *rest):
        wz, wx = rest[:np_], rest[np_ : 2 * np_]
        gain, gi_o, zbuf, xbuf, gn = rest[2 * np_ :]
        i = pl.program_id(0)

        @pl.when(i == 0)
        def _():
            xbuf[:, conv:] = jnp.zeros((xbuf.shape[0], xbuf.shape[1] - conv), bf16)
            place(zbuf, ids, wz, di)
            place(xbuf, ids, wx, conv + heads)

        wa = gpa.shape[1]
        wd = u.shape[1]
        last = (i == pl.num_programs(0) - 1).astype(f32)
        for c0 in range(0, wd, 256):
            c = slice(c0, c0 + 256)
            g = dot_nt(gpz[...], zbuf[c, :]) + dot_nt(gpa[...], xbuf[c, :wa]) + dot_nt(gpb[...], xbuf[c, wa:])
            tail = (dot_nt(ea[...], xbuf[c, :wa]) + dot_nt(eb[...], xbuf[c, wa:conv])) * last
            gn[: TB - 16, c] = g[: TB - 16]
            gn[TB - 16 :, c] = g[TB - 16 :] + tail
        for r0 in range(0, TB, 16):
            r = slice(r0, r0 + 16)
            uf = u[r, :].astype(f32)
            scale = lax.rsqrt(jnp.mean(uf * uf, axis=-1, keepdims=True) + EPS)
            unit = uf * scale
            dn = gn[r, :] * gain[...]
            m = jnp.mean(dn * unit, axis=-1, keepdims=True)
            gi_o[r, :] = (e[r, :].astype(f32) + scale * (dn - unit * m)).astype(bf16)

    return kernel


def swap(v, axis, bit):
    return lax.ppermute(v, axis, [(k, k ^ bit) for k in range(lax.axis_size(axis))])


def shift(v, axis, steps):
    n = lax.axis_size(axis)
    return lax.ppermute(v, axis, [(k, k + steps) for k in range(n) if 0 <= k + steps < n])


def bits_of(n):
    return [1 << k for k in reversed(range((n - 1).bit_length()))]


def after(v, dep):
    if dep is None:
        return v
    return lax.optimization_barrier((v, dep))[0]


def gather_parts(v, axis):
    parts = [v]
    for bit in bits_of(lax.axis_size(axis)):
        parts = parts + [swap(p, axis, bit) for p in parts]
    return parts


def in_order(parts, axis):
    at = lax.axis_index(axis)
    n = lax.axis_size(axis)
    v = jnp.stack(parts)
    rest = v.shape[1:]
    bits = bits_of(n)
    v = v.reshape((2,) * len(bits) + rest)
    for k, bit in enumerate(reversed(bits)):
        v = jnp.where((at // bit) % 2 == 0, v, jnp.flip(v, k))
    order = tuple(reversed(range(len(bits))))
    return v.transpose(order + tuple(range(len(bits), v.ndim))).reshape((n,) + rest)


def part_ids(axis):
    ids = [lax.axis_index(axis)]
    for bit in bits_of(lax.axis_size(axis)):
        ids = ids + [k ^ bit for k in ids]
    return ids


def add(a, b):
    return (a.astype(f32) + b.astype(f32)).astype(bf16)


def pair_steps(gs):
    nw = lax.axis_size("wshard")
    w = lax.axis_index("wshard")
    n = min(g.shape[0] for g in gs) // nw

    def pick(at):
        out = []
        for g in gs:
            v = g.reshape(nw // 2, 2, -1, g.shape[-1])
            v = lax.dynamic_index_in_dim(v, at, 1, keepdims=False)
            k = v.shape[1] // n
            out += [v[:, q * n : (q + 1) * n] for q in range(k)]
        return jnp.concatenate(out, axis=2) if len(out) > 1 else out[0]

    send, keep = pick(1 - w % 2), pick(w % 2)
    dep = yield send
    yield add(keep, swap(after(send, dep), "wshard", 1))


def other_steps(v):
    nw = lax.axis_size("wshard")
    w = lax.axis_index("wshard")
    n = v.shape[1]
    for bit in [1 << k for k in range(1, (nw - 1).bit_length())]:
        at = (w // bit) % 2
        v = v.reshape(-1, 2, n, v.shape[-1]).swapaxes(0, 1)
        send = lax.dynamic_index_in_dim(v, 1 - at, 0, keepdims=False)
        keep = lax.dynamic_index_in_dim(v, at, 0, keepdims=False)
        dep = yield send
        v = add(keep, swap(after(send, dep), "wshard", bit))
    yield v.reshape(n, -1)


def pairs_of(n):
    bits = [1 << k for k in range((n - 1).bit_length())]
    return [bits[k : k + 2] for k in range(0, len(bits), 2)]


def swap_all(parts, axis, bits):
    got = parts[:1]
    for m in range(1, 1 << len(bits)):
        got.append(swap(parts[m], axis, sum(bit for k, bit in enumerate(bits) if (m >> k) & 1)))
    return got


def by_index(got, at, bits):
    for k, bit in enumerate(bits):
        here = (at // bit) % 2 == 1
        got = [jnp.where(here, got[m ^ (1 << k)], got[m]) for m in range(len(got))]
    return got


def seq_steps(v):
    groups = pairs_of(lax.axis_size("seq"))
    s = lax.axis_index("seq")
    single = groups.pop() if len(groups[-1]) == 1 else None
    for bits in groups:
        n = 1 << len(bits)
        at = (s // bits[0]) % n
        v = v.reshape(n, -1, v.shape[-1])
        send = [lax.dynamic_index_in_dim(v, at ^ m, 0, keepdims=False) for m in range(n)]
        dep = yield tuple(send)
        got = swap_all(after(send, dep), "seq", bits)
        v = sum(g.astype(f32) for g in got).astype(bf16)
    if single:
        dep = yield v
        v = add(v, swap(after(v, dep), "seq", single[0]))
    for bits in reversed(groups):
        dep = yield v
        v = after(v, dep)
        got = swap_all([v] * (1 << len(bits)), "seq", bits)
        dep = yield tuple(got[1:])
        v = jnp.concatenate(by_index(after(tuple(got), dep), s, bits), axis=0)
    yield v.astype(f32)


def small_steps(v):
    for axis in ("wshard", "seq"):
        at = lax.axis_index(axis)
        for bits in pairs_of(lax.axis_size(axis)):
            dep = yield v
            v = after(v, dep)
            v = sum(by_index(swap_all([v] * (1 << len(bits)), axis, bits), at, bits))
    yield v


def pack_state(decay, state):
    hi, lo = two(decay)
    return jnp.concatenate([state.astype(bf16), hi, lo], axis=0)


def unpack_state(v, n):
    return v[n : n + 8].astype(f32)[:1] + v[n + 8 : n + 16].astype(f32)[:1], v[:n].astype(f32)


def carried(send, decay, state, sign, tokens):
    n = state.shape[0]
    span = 1
    while span < -(-LONGEST // tokens):
        if span > 1:
            send = pack_state(decay, state)
        dep = yield send
        d, s = unpack_state(shift(after(send, dep), "seq", sign * span), n)
        state = state + decay[:1] * s
        decay = decay * d
        span *= 2
    send = state.astype(bf16)
    dep = yield send
    yield shift(after(send, dep), "seq", sign)


class Steps:
    def __init__(self, gen):
        self.gen = gen
        self.value = next(gen)

    def step(self, dep=None):
        try:
            self.value = self.gen.send(dep)
        except StopIteration:
            pass
        return self.value

    def finish(self):
        for self.value in self.gen:
            pass
        return self.value


def body(inputs, cotangent, lengths, in_proj, out_proj, conv_weight, conv_bias, a_log, d_skip,
         dt_bias, norm_gain, gate_gain):
    t, d = inputs.shape[1:]
    nw = lax.axis_size("wshard")
    di = out_proj.shape[0] * nw
    heads = a_log.shape[0] * nw
    conv = conv_bias.shape[0] * nw
    taps = conv_weight.shape[0]
    n = (conv - di) // 2
    p = di // heads
    docs = lengths.shape[1]
    nt, nc, nb = t // TB, t // CH, TB // CH
    wide = conv + 128
    wx, wz = in_proj[:, di:], in_proj[:, :di]
    pc = conv // nw
    width = -(-max(pc, di // nw, 384) // 128) * 128


    def line(*vs):
        vs = [v if v.ndim == 2 else v[None] for v in vs]
        vs = [jnp.pad(v, ((0, 0), (0, (width if k == len(vs) - 1 else 128 * (k + 1)) - 128 * k - v.shape[1])))
              for k, v in enumerate(vs)]
        return jnp.concatenate(vs, axis=1)

    small = jnp.concatenate(
        [line(conv_weight), line(conv_bias), line(gate_gain), line(norm_gain), line(a_log, d_skip, dt_bias)], axis=0)
    wx_parts = gather_parts(wx, "wshard")
    small = in_order(gather_parts(after(small, wx_parts[nw // 2]), "wshard"), "wshard").astype(f32)
    wz_parts = gather_parts(after(wz, wx_parts[1]), "wshard")
    wo_parts = gather_parts(after(out_proj, wx_parts[1]), "wshard")
    ids = jnp.stack(part_ids("wshard")).astype(jnp.int32)
    hw = heads // nw
    cw = small[:, :taps, :pc].swapaxes(0, 1).reshape(taps, conv)
    cb = small[:, taps, :pc].reshape(1, conv)
    gain_gate = small[:, taps + 1, : di // nw].reshape(1, di)
    gain_in = small[:, taps + 2, : d // nw].reshape(1, d)
    log_rate, skip, dtb = [small[:, taps + 3, 128 * k : 128 * k + hw].reshape(1, heads) for k in range(3)]
    rate = -jnp.exp(log_rate)
    pad = ((0, 0), (0, 128 - heads))
    nr = jnp.pad(rate, pad)
    nr2 = nr * LOG2E
    dtb = jnp.pad(dtb, pad)
    dsk = jnp.repeat(skip, p, axis=1)
    e1 = np.arange(128)[:, None] == np.arange(di)[None] // p
    e2 = jnp.asarray(np.concatenate([e1, e1], axis=0), bf16)
    hot = jnp.asarray(np.arange(heads * CH)[:, None] // CH == np.arange(128)[None], bf16)
    first = lax.axis_index("seq") * t
    pos = first - 8 + jnp.arange(t + 16, dtype=jnp.int32)
    ends = jnp.cumsum(lengths[0], dtype=jnp.int32)
    seg = jnp.sum((pos[:, None] >= ends[None]).astype(jnp.int32), axis=1)
    seg = jnp.where(pos < 0, -1, seg)
    here = seg[: t + 8]
    own = seg[8 : t + 8]
    entering = jnp.repeat(seg[7 : t + 7 : CH], CH)
    leaving = jnp.repeat(seg[7 + CH : t + 8 : CH], CH)
    zero8 = jnp.zeros((8,), jnp.int32)
    back = [jnp.concatenate([zero8, (seg[8 - k : t + 8 - k] == own).astype(jnp.int32)]) for k in (3, 2, 1)]
    ahead = [(seg[k : t + 8 + k] == here).astype(jnp.int32) for k in (1, 2, 3)]
    cols = [here, jnp.concatenate([zero8, (entering == own).astype(jnp.int32)]),
            jnp.concatenate([zero8, (leaving == own).astype(jnp.int32)])]
    cols = cols + back + [(here < docs).astype(jnp.int32)] + ahead + [jnp.zeros_like(here)] * 6
    tok_all = jnp.stack(cols, axis=1).astype(f32)
    tok, elink = tok_all[8:], tok_all[:8]
    segr = own.astype(f32)[None]
    u, cot = inputs[0], cotangent[0]
    ue = shift(u[t - 16 :], "seq", 1)

    outs = [
        (rows(TB, d), (t, d), bf16),
        (rows(TB, conv), (t, conv), bf16),
        (rows(TB, conv), (t, conv), bf16),
        (rows(TB, conv), (t, conv), bf16),
        (rows(TB, di), (t, di), bf16),
        (rows(TB, 256), (t, 256), f32),
        (rows(TB, 128), (t, 128), f32),
        (pl.BlockSpec((32, TB), lambda i, s: (0, i)), (32, t), f32),
        (pl.BlockSpec((nb, n, di), lambda i, s: (i, 0, 0)), (nc, n, di), bf16),
        (pl.BlockSpec((nb, 8, 128), lambda i, s: (i, 0, 0)), (nc, 8, 128), f32),
        (whole((n, di)), (n, di), f32),
        (whole((8, di)), (8, di), f32),
        (whole((n + 16, di)), (n + 16, di), bf16),
        (whole((16, d)), (16, d), bf16),
        (whole((16, conv)), (16, conv), bf16),
    ]
    ins = [rows(TB, d), whole((16, d)), whole((1, d))] + [whole(v.shape) for v in wx_parts]
    ins += [whole((taps, conv)), whole((1, conv)), whole((1, 128)), whole((1, 128)), rows(TB, 16), whole((256, di))]
    scratch = [
        pltpu.VMEM((d, wide), bf16),
        pltpu.VMEM((TB + 8, conv), f32),
        pltpu.VMEM((n, di), f32),
        pltpu.VMEM((1, 128), f32),
        pltpu.VMEM((2 * TB + 8 * nb, di), f32),
    ]
    (nrm, xbc, xc, slope, xd, dts, cc, ct, st, dbf, end, tot, pack, nrme, xbce) = call(
        front_kernel(nw, di, conv, heads), (nt,), ins, outs, scratch, 15,
        [ids, u, ue, gain_in] + wx_parts + [cw, cb, dtb, nr2, tok, e2], "front")
    chain = Steps(carried(pack, tot, end, 1, t))
    chain.step(wz_parts[1])
    chain.step()
    chain.step(wo_parts[1])
    incoming = chain.finish()

    crow = pl.BlockSpec((32, TI), lambda i, s: (0, i))
    srow = pl.BlockSpec((1, TI), lambda i, s: (0, i))
    crow2 = pl.BlockSpec((32, CH), lambda i, s: (0, i))
    srow2 = pl.BlockSpec((1, CH), lambda i, s: (0, i))
    bspec, cspec = rows(TI, n, di // n), rows(TI, n, di // n + 1)
    (yin,) = call(
        inner_kernel(heads, di), (t // TI,),
        [bspec, cspec, rows(TI, di), rows(TI, 128), crow, rows(TI, 16), srow],
        [(rows(TI, di), (t, di), bf16)], [], 10,
        [ids, xc, xc, xd, cc, ct, tok, segr], "inner")

    blk = pl.BlockSpec((nb, n, di), lambda i, s: (i, 0, 0))
    outs = [
        (rows(TB, d), (t, d), bf16),
        (rows(TB, di), (t, di), bf16),
        (rows(TB, di), (t, di), bf16),
        (rows(TB, di), (t, di), bf16),
        (rows(TB, di), (t, di), bf16),
        (rows(TB, d), (t, d), bf16),
        (blk, (nc, n, di), bf16),
        (blk, (nc, n, di), bf16),
        (rows(TB, 128), (t, 128), f32),
        (whole((8, 128)), (8, 128), f32),
        (whole((n, di)), (n, di), f32),
        (whole((n + 16, di)), (n + 16, di), bf16),
    ]
    ins = [rows(TB, d), rows(TB, di), rows(TB, di), rows(TB, n, di // n + 1), rows(TB, 128), rows(TB, 16), blk,
           pl.BlockSpec((nb, 8, 128), lambda i, s: (i, 0, 0)), whole((n, di)), whole((8, di)), rows(TB, d), rows(TB, d)]
    ins += [whole(v.shape) for v in wz_parts + wo_parts]
    ins += [whole((1, di)), whole((1, di)), whole((256, di))]
    scratch = [pltpu.VMEM((d, di), bf16), pltpu.VMEM((di, d), bf16)]
    scratch += [pltpu.VMEM((TB, di), f32)] * 3
    scratch += [pltpu.VMEM((TB + 8 * nb, di), f32), pltpu.VMEM((TB, di), bf16), pltpu.VMEM((8, di), f32)]
    (mixed, gn, dz, dy, edy, e, sf, dcs, rin, g_skip, reach, reach_pack) = call(
        gate_kernel(nw, di, d), (nt,), ins, outs, scratch, 25,
        [ids, nrm, yin, xc, xc, cc, tok, st, dbf, incoming, tot, u, cot] + wz_parts + wo_parts + [gain_gate, dsk, e2], "gate")
    tn = (((0,), (0,)), ((), ()))

    def outer(a, b):
        return lax.dot_general(a, b, tn, preferred_element_type=f32)

    back_state = Steps(carried(reach_pack, tot, reach, -1, t))
    s1 = back_state.value
    gw_out = outer(after(gn, s1), e).astype(bf16)
    gw_z = outer(nrm, after(dz, s1)).astype(bf16)
    s2 = back_state.step()
    oz_p = Steps(pair_steps([gw_out, gw_z]))
    oz_w = Steps(other_steps(oz_p.step(s2)))
    oz2 = oz_w.value
    hh, hw2 = heads // 2, di // 2

    def at(shape, col):
        return pl.BlockSpec(shape, lambda i, s: (0, col))

    def half_inner(k, dep):
        outs = [
            (rows(CH, hw2), (t, hw2), bf16),
            (rows(CH, n), (t, n), f32),
            (rows(CH, n), (t, n), f32),
            (rows(CH, 128), (t, 128), f32),
        ]
        return call(
            inner_back_kernel(p, hh * k, hh * (k + 1)), (t // CH,),
            [rows(CH, n, di // n), rows(CH, n, di // n + 1), rows(CH, hw2, k), rows(CH, hw2, k), rows(CH, 128), crow2,
             pl.BlockSpec((hh * CH, 128), lambda i, s: (k, 0)), rows(CH, 16), srow2],
            outs, [pltpu.VMEM((128, CH), f32)], 12,
            [ids, xc, xc, xd, after(dy, dep), cc, ct, hot, tok, segr], "inner_back")

    def rev(block, width, col=0):
        return pl.BlockSpec((block, width), lambda i, s: (nt - 1 - i, col))

    def half_back(k, inner, dep, gend, extra):
        gxd, dbi, dci, rk = inner
        last = k == 1
        cols = hw2 + 2 * n if last else hw2
        rblk = pl.BlockSpec((nb, n, hw2), lambda i, s: (nt - 1 - i, 0, k))
        ins = [rev(TB, hw2, k), rev(TB, n, di // n), rev(TB, hw2, k), rev(TB, hw2, k), at((16, hw2), k),
               rev(TB, hw2, k), rev(TB, 256), rev(TB, 128), rev(TB, 16), whole((8, 16)), rev(TB, hw2),
               rev(TB, n), rev(TB, n), rev(TB, 128), rev(TB, 128), rev(TB, hw2, k), rev(TB, hw2, k), rblk, rblk,
               at((n, hw2), k), at((taps, hw2), k), at((1, hw2), k), whole((1, 128)), at((256, hw2), k)]
        args = [ids, xc, xc, slope, xbc, xbce, xd, dts, cc, tok, elink, after(gxd, dep), dbi, dci, rk, rin, dy,
                edy, sf, dcs, gend, cw, dsk, nr, e2]
        outs = [
            (rev(TB, cols + 128 * last), (t, cols + 128 * last), bf16),
            (whole((16, cols)), (16, cols), bf16),
            (whole((8, cols)), (8, cols), f32),
        ]
        if last:
            ins += [rev(TB, 2 * n, di // (2 * n)), rev(TB, 2 * n, di // (2 * n)), at((16, 2 * n), di // (2 * n)),
                    at((taps, 2 * n), di // (2 * n)), rev(TB, n), rev(TB, n), rev(TB, 128), whole((8, 128))]
            args += [slope, xbc, xbce, cw] + list(extra)
        else:
            outs += [(rev(TB, n), (t, n), f32), (rev(TB, n), (t, n), f32), (rev(TB, 128), (t, 128), f32)]
        scratch = [
            pltpu.VMEM((n, hw2), f32),
            pltpu.VMEM((2 * TB + 8 * nb, hw2), f32),
            pltpu.VMEM((TB, hw2), f32),
            pltpu.VMEM((TB + 8, cols), f32),
            pltpu.VMEM((TB, hw2), bf16),
            pltpu.VMEM((TB, hw2), bf16),
            pltpu.VMEM((8 * taps, cols), f32),
            pltpu.VMEM((8, cols), f32),
            pltpu.VMEM((8, 128), f32),
            pltpu.VMEM((8, 128), f32),
        ]
        return call(back_kernel(hw2, n, hh * k, hh * (k + 1), last), (nt,), ins, outs, scratch, 15, args, "back")

    in_a = half_inner(0, (s2, oz2))
    s3 = back_state.step(oz2)
    s3, in_a0 = lax.optimization_barrier((s3, in_a[0]))
    in_b = half_inner(1, (s3, in_a0))
    back_state.step(in_a[0])
    gend = back_state.finish()
    oz_w.step()
    oz_s = Steps(seq_steps(oz_w.finish()))
    oz3 = oz_s.value
    (gpa, edge_a, sum_a, dbp, dcp, ddtp) = half_back(0, in_a, (in_b[0], oz3), gend, None)
    oz4 = oz_s.step(in_b[0])
    gw_xa = (outer(nrm, after(gpa, oz4)) + outer(nrme, edge_a)).astype(bf16)
    xa_p = Steps(pair_steps([gw_xa]))
    xa1 = xa_p.value
    (gpb, edge_b, sum_b) = half_back(1, in_b, (oz4, xa1), gend, (dbp, dcp, ddtp, g_skip))
    oz5 = oz_s.step(gpa)
    oz5, gpb_late = lax.optimization_barrier((oz5, gpb))
    gw_xb = outer(nrm, gpb_late)
    cb2 = conv - hw2
    gw_xb = jnp.concatenate(
        [gw_xb[:, :cb2] + outer(nrme, edge_b), gw_xb[:, cb2 : cb2 + heads]], axis=1).astype(bf16)
    xb_p = Steps(pair_steps([gw_xb]))
    x_w = Steps(other_steps(jnp.concatenate([xa_p.step(), xb_p.step()], axis=2)))
    x2 = x_w.value
    ea_in, eb_in = shift(edge_a, "seq", -1), shift(edge_b, "seq", -1)
    oz7 = oz_s.step((x2, ea_in))

    ins = [rows(TB, di), rows(TB, hw2), rows(TB, wide - hw2), whole((16, hw2)), whole((16, cb2)), rows(TB, d), rows(TB, d)]
    ins += [whole(v.shape) for v in wz_parts + wx_parts] + [whole((1, d))]
    outs = [(rows(TB, d), (t, d), bf16)]
    (grad_input,) = call(
        input_kernel(nw, di, conv, heads), (nt,), ins, outs,
        [pltpu.VMEM((d, di), bf16), pltpu.VMEM((d, wide), bf16), pltpu.VMEM((TB, d), f32)], 12,
        [ids, dz, after(gpa, x2), gpb, ea_in, eb_in, u, e] + wz_parts + wx_parts + [gain_in], "input")
    sums = Steps(small_steps(jnp.concatenate([sum_a, sum_b], axis=1)))
    x_s = Steps(seq_steps(x_w.finish()))
    x3 = x_s.value
    sums.step((x3, grad_input))
    x4 = x_s.step((grad_input, oz7))
    sums.step(x4)
    oz_s.step(x4)
    x5 = x_s.step()
    sums.step(x5)
    r_x, r_oz, total = x_s.finish(), oz_s.finish(), sums.finish()
    k = r_oz.shape[1] - di
    r_out = jnp.concatenate([r_oz[:, q * d : (q + 1) * d] for q in range(k // d)], axis=0)
    r_z = r_oz[:, k:]
    w = lax.axis_index("wshard")

    def mine(v):
        width = v.shape[-1] // nw
        return lax.dynamic_slice_in_dim(v, w * width, width, axis=v.ndim - 1)

    by_head = total[5:8, :heads] + total[5:8, hw2 : hw2 + heads]
    by_head = mine(by_head * jnp.concatenate([rate, jnp.ones((2, heads), f32)], axis=0))
    res = [mine(total[:taps]), mine(total[taps]), by_head[0], by_head[2], by_head[1]]
    res.append((jnp.sum(r_z * wz.astype(f32), axis=1) + jnp.sum(r_x * wx.astype(f32), axis=1)) / norm_gain.astype(f32))
    res.append(jnp.sum(r_out * out_proj.astype(f32), axis=1) / gate_gain.astype(f32))
    return (mixed[None], grad_input[None], jnp.concatenate([r_z, r_x], axis=1), r_out) + tuple(res)


def solution(mesh):
    wide = P("wshard", "seq", None)
    mat = P("wshard", None)
    taps = P(None, "wshard")
    vec = P("wshard")
    return jax.shard_map(
        body,
        mesh=mesh,
        in_specs=(wide, wide, mat, mat, mat, taps) + (vec,) * 6,
        out_specs=(wide, wide, mat, mat, taps) + (vec,) * 6,
        check_vma=False,
    )
```

```python
import jax
import jax.numpy as jnp
import numpy as np
from jax import lax
from jax.experimental import pallas as pl
from jax.experimental.pallas import tpu as pltpu
from jax.sharding import PartitionSpec as P

f32 = jnp.float32
bf16 = jnp.bfloat16
EPS = 1e-05
LOG2E = 1.4426950408889634
CH = 128
TB = 256
TI = 256
LONGEST = 4096
HIGH = lax.Precision.HIGHEST
MB = 1024 * 1024
VMEM = 60 * MB


def sigmoid(v):
    return 0.5 * jnp.tanh(0.5 * v) + 0.5


def dot(a, b):
    return jnp.dot(a, b, preferred_element_type=f32)


def dot_nt(a, b):
    return lax.dot_general(a, b, (((1,), (1,)), ((), ())), preferred_element_type=f32)


def two(v):
    hi = v.astype(bf16)
    return hi, (v - hi.astype(f32)).astype(bf16)


def spread(v, e2):
    return dot(jnp.concatenate(two(v), axis=1), e2)


def head_sums(row, e2):
    hi, lo = two(jnp.broadcast_to(row, (8, row.shape[1])))
    return dot_nt(hi, e2[0:128, :]) + dot_nt(lo, e2[0:128, :])


def cost(us):
    return pl.CostEstimate(flops=int(us * 1.1e9), bytes_accessed=1 << 20, transcendentals=0)


def call(kernel, grid, ins, outs, scratch, us, args, name):
    return pl.pallas_call(
        kernel,
        grid_spec=pltpu.PrefetchScalarGridSpec(
            num_scalar_prefetch=1,
            grid=grid,
            in_specs=ins,
            out_specs=[o[0] for o in outs],
            scratch_shapes=scratch,
        ),
        out_shape=[jax.ShapeDtypeStruct(o[1], o[2]) for o in outs],
        compiler_params=pltpu.CompilerParams(
            vmem_limit_bytes=VMEM, dimension_semantics=("arbitrary",)
        ),
        cost_estimate=cost(us),
        name=name,
    )(*args)


def rows(block, cols, col=0):
    return pl.BlockSpec((block, cols), lambda i, s: (i, col))


def whole(shape):
    return pl.BlockSpec(shape, lambda i, s: (0,) * len(shape))


def norm_rows(uf, gain):
    scale = lax.rsqrt(jnp.mean(uf * uf, axis=-1, keepdims=True) + EPS)
    return (uf * scale * gain).astype(bf16)


def place(buf, ids, parts, width):
    for j, part in enumerate(parts):
        n = part.shape[0]
        at = pl.multiple_of(ids[j] * n, 64)
        buf[pl.ds(at, n), :width] = part[...]


def put_pack(ref, decay, state):
    n = state.shape[0]
    hi, lo = two(decay)
    ref[0:n, :] = state.astype(bf16)
    ref[n:, :] = jnp.concatenate([hi.astype(f32), lo.astype(f32)], axis=0).astype(bf16)


def front_kernel(np_, di, conv, heads):
    def kernel(ids, u, ue, gain, *rest):
        parts = rest[:np_]
        (cw, cb, dtb, nr, tok, e2, nrm_o, xbc_o, xc_o, slope_o, xd_o, dts_o, cc_o, ct_o,
         st_o, db_o, end_o, tot_o, pk_o, nrme_o, xbce_o, wbuf, ext, state, kd, sp) = rest[np_:]
        i = pl.program_id(0)
        n = (conv - di) // 2

        @pl.when(i == 0)
        def _():
            wbuf[:, conv:] = jnp.zeros((wbuf.shape[0], wbuf.shape[1] - conv), bf16)
            place(wbuf, ids, parts, conv + heads)
            nrme = norm_rows(ue[...].astype(f32), gain[...])
            nrme_o[...] = nrme
            pe = dot(nrme, wbuf[:, :conv]).astype(bf16)
            xbce_o[...] = pe
            ext[0:8, :] = pe.astype(f32)[8:16]
            state[...] = jnp.zeros_like(state)
            kd[...] = jnp.ones_like(kd)

        nrm = norm_rows(u[...].astype(f32), gain[...])
        nrm_o[...] = nrm
        pd = dot(nrm, wbuf[:, conv:])
        for c0 in range(0, conv, 256):
            px = dot(nrm, wbuf[:, c0 : c0 + 256]).astype(bf16)
            xbc_o[:, c0 : c0 + 256] = px
            ext[8 : 8 + TB, c0 : c0 + 256] = px.astype(f32)
        sh = pd + dtb[...]
        dt = jnp.maximum(sh, 0.0) + jnp.log1p(jnp.exp(-jnp.abs(sh)))
        dts_o[:, :128] = dt
        dts_o[:, 128:] = jax.nn.sigmoid(sh)
        a2 = dt * nr[...]
        ri = lax.broadcasted_iota(jnp.int32, (CH, CH), 0)
        ci = lax.broadcasted_iota(jnp.int32, (CH, CH), 1)
        low = (ri >= ci).astype(f32)
        pieces = [dt]
        leaves = []
        for k in range(TB // CH):
            r = slice(k * CH, (k + 1) * CH)
            c2 = jnp.dot(low, a2[r], precision=HIGH, preferred_element_type=f32)
            cc_o[r, :] = c2
            ct_o[:, r] = c2.T[: ct_o.shape[0], :]
            pieces.append(jnp.exp2(c2[CH - 1 :] - c2) * tok[r, 2:3])
            leaves.append(jnp.exp2(c2[CH - 1 :]) * tok[(k + 1) * CH - 1 : (k + 1) * CH, 1:2])
        lv = jnp.concatenate([jnp.broadcast_to(v, (8, 128)) for v in leaves], axis=0)
        sp[...] = spread(jnp.concatenate(pieces + [lv], axis=0), e2[...])
        for r0 in range(0, TB, 64):
            l0, l1, l2 = tok[r0 : r0 + 64, 3:4], tok[r0 : r0 + 64, 4:5], tok[r0 : r0 + 64, 5:6]
            for c0 in range(0, conv, 256):
                c = slice(c0, c0 + 256)
                pre = cb[:, c] + cw[3:4, c] * ext[8 + r0 : 72 + r0, c]
                pre = pre + cw[2:3, c] * (ext[7 + r0 : 71 + r0, c] * l2)
                pre = pre + cw[1:2, c] * (ext[6 + r0 : 70 + r0, c] * l1)
                pre = pre + cw[0:1, c] * (ext[5 + r0 : 69 + r0, c] * l0)
                sg = sigmoid(pre)
                xc = pre * sg
                xc_o[r0 : r0 + 64, c] = xc.astype(bf16)
                slope_o[r0 : r0 + 64, c] = (sg + xc * (1.0 - sg)).astype(bf16)
                if c0 < di:
                    xd_o[r0 : r0 + 64, c] = (xc * sp[r0 : r0 + 64, c]).astype(bf16)
        ext[0:8, :] = ext[TB : TB + 8, :]
        for k in range(TB // CH):
            r = slice(k * CH, (k + 1) * CH)
            st_o[k] = state[...].astype(bf16)
            db_o[k] = jnp.broadcast_to(kd[...], (8, 128))
            bt = xc_o[r, di : di + n].astype(f32).T.astype(bf16)
            for c0 in range(0, di, 256):
                c = slice(c0, c0 + 256)
                xw = (xd_o[r, c].astype(f32) * sp[TB + k * CH : TB + (k + 1) * CH, c]).astype(bf16)
                lvr = sp[2 * TB + 8 * k : 2 * TB + 8 * k + 1, c]
                state[:, c] = lvr * state[:, c] + dot(bt, xw)
            kd[...] = kd[...] * leaves[k]

        @pl.when(i == pl.num_programs(0) - 1)
        def _():
            end_o[...] = state[...]
            total = spread(jnp.broadcast_to(kd[...], (8, 128)), e2[...])
            tot_o[...] = total
            put_pack(pk_o, total, state[...])

    return kernel


def inner_kernel(heads, di):
    p = di // heads
    per = 128 // p

    def kernel(ids, b, c, xd, cc, ct, tok, segr, y_o):
        ri = lax.broadcasted_iota(jnp.int32, (CH, CH), 0)
        ci = lax.broadcasted_iota(jnp.int32, (CH, CH), 1)
        lanes = lax.broadcasted_iota(jnp.int32, (1, 128), 1) // p
        for k in range(b.shape[0] // CH):
            r = slice(k * CH, (k + 1) * CH)
            s = dot_nt(c[r, :], b[r, :])
            bias = jnp.where((tok[r, 0:1] == segr[:, r]) & (ri >= ci), 0.0, -1e30)
            for j in range(heads // per):
                xp = xd[r, 128 * j : 128 * j + 128]
                ms, xs = [], []
                for q in range(per):
                    h = per * j + q
                    e = jnp.exp2(cc[r, h : h + 1] - ct[h : h + 1, r] + bias)
                    ms.append((s * e).astype(bf16))
                    xs.append(xp * (lanes == q).astype(f32).astype(bf16))
                out = dot(jnp.concatenate(ms, axis=1), jnp.concatenate(xs, axis=0))
                y_o[r, 128 * j : 128 * j + 128] = out.astype(bf16)

    return kernel


def gate_kernel(np_, di, d):
    def kernel(ids, nrm, yin, x, c_in, cc, tok, st, db, inc, tot, u, cot, *rest):
        wz, wo = rest[:np_], rest[np_ : 2 * np_]
        (gain, dsk, e2, mixed_o, gn_o, dz_o, dy_o, edy_o, e_o, sf_o, dc_o, rin_o, gs_o,
         rg_o, pk_o, zbuf, obuf, z, yi, dgn, ee, pr, gs) = rest[2 * np_ :]
        i = pl.program_id(0)

        @pl.when(i == 0)
        def _():
            place(zbuf, ids, wz, di)
            place(obuf, ids, wo, d)
            gs[...] = jnp.zeros_like(gs)
            rg_o[...] = jnp.zeros_like(rg_o)

        keep = tok[:, 6:7]
        ef = cot[...].astype(f32) * keep
        e = ef.astype(bf16)
        e_o[...] = e
        nb = TB // CH
        ents = []
        for k in range(nb):
            r = slice(k * CH, (k + 1) * CH)
            ents.append(jnp.exp2(cc[r, :]) * tok[r, 1:2])
        ee[...] = spread(jnp.concatenate(ents + [db[k] for k in range(nb)], axis=0), e2[...])
        for k in range(nb):
            r = slice(k * CH, (k + 1) * CH)
            for c0 in range(0, di, 256):
                c = slice(c0, c0 + 256)
                dbr = ee[TB + 8 * k : TB + 8 * k + 1, c]
                sf = (st[k, :, c].astype(f32) + dbr * inc[:, c].astype(f32)).astype(bf16)
                sf_o[k, :, c] = sf
                yi[r, c] = dot(c_in[r, :], sf)
        z[...] = dot(nrm[...], zbuf[...])
        dgn[...] = dot_nt(e, obuf[...])

        def strip(r):
            xs = x[r, :].astype(f32)
            eyi = ee[r, :] * yi[r, :]
            y = yin[r, :].astype(f32) + eyi + dsk[...] * xs
            zz = z[r, :]
            sg = sigmoid(zz)
            act = zz * sg
            g = y * act
            scale = lax.rsqrt(jnp.mean(g * g, axis=-1, keepdims=True) + EPS)
            ug = g * scale
            gn_o[r, :] = (ug * gain[...]).astype(bf16)
            dg0 = dgn[r, :]
            dn = dg0 * gain[...]
            m = jnp.mean(dn * ug, axis=-1, keepdims=True)
            dg = scale * (dn - ug * m)
            dy = dg * act
            dz_o[r, :] = (dg * y * (sg + act * (1.0 - sg))).astype(bf16)
            dy_o[r, :] = dy.astype(bf16)
            ps = xs * dy
            gs[...] += ps[0:8] + ps[8:16]
            edy_o[r, :] = (dy * ee[r, :]).astype(bf16)
            pr[r, :] = (dy * eyi).astype(bf16)

        for t in range(TB // 16):
            strip(slice(t * 16, t * 16 + 16))
        rin_o[...] = dot_nt(pr[...], e2[0:128, :])
        mixed_o[...] = (keep * (u[...].astype(f32) + dot(gn_o[...], obuf[...]))).astype(bf16)
        for k in range(nb):
            r = slice(k * CH, (k + 1) * CH)
            ctr = c_in[r, :].astype(f32).T.astype(bf16)
            for c0 in range(0, di, 256):
                c = slice(c0, c0 + 256)
                dcv = dot(ctr, edy_o[r, c])
                dc_o[k, :, c] = dcv.astype(bf16)
                rg_o[:, c] += ee[TB + 8 * k : TB + 8 * k + 1, c] * dcv

        @pl.when(i == pl.num_programs(0) - 1)
        def _():
            gs_o[...] = head_sums(jnp.sum(gs[...], axis=0, keepdims=True), e2)
            put_pack(pk_o, tot[...], rg_o[...])

    return kernel


def inner_back_kernel(p, h0, h1):
    per = 128 // p

    def kernel(ids, b, c, xd, dy, cc, ct, hot, tok, segr, gxd_o, db_o, dc_o, rk_o, rr):
        si = lax.broadcasted_iota(jnp.int32, (CH, CH), 0)
        ti = lax.broadcasted_iota(jnp.int32, (CH, CH), 1)
        lanes = lax.broadcasted_iota(jnp.int32, (1, 128), 1) // p
        rr[...] = jnp.zeros_like(rr)
        for k in range(b.shape[0] // CH):
            r = slice(k * CH, (k + 1) * CH)
            st = dot_nt(b[r, :], c[r, :])
            bias = jnp.where((tok[r, 0:1] == segr[:, r]) & (ti >= si), 0.0, -1e30)
            gsum = jnp.zeros((CH, CH), f32)
            ksum = jnp.zeros((CH, 128), f32)
            for j in range((h1 - h0) // per):
                xp = xd[r, 128 * j : 128 * j + 128]
                dyp = dy[r, 128 * j : 128 * j + 128]
                dys = jnp.concatenate(
                    [dyp * (lanes == q).astype(f32).astype(bf16) for q in range(per)], axis=0
                )
                gm = dot_nt(xp, dys)
                ms, exs = [], []
                for q in range(per):
                    h = h0 + per * j + q
                    e = jnp.exp2(ct[h : h + 1, r] - cc[r, h : h + 1] + bias)
                    ms.append((st * e).astype(bf16))
                    ge = gm[:, q * CH : (q + 1) * CH] * e
                    gsum = gsum + ge
                    ex = (ge * st).astype(bf16)
                    exs.append(ex)
                    rr[h : h + 1, r] = jnp.sum(ex.astype(f32), axis=0, keepdims=True)
                ksum = ksum + dot(jnp.concatenate(exs, axis=1), hot[per * CH * j : per * CH * (j + 1), :])
                out = dot(jnp.concatenate(ms, axis=1), dys)
                gxd_o[r, 128 * j : 128 * j + 128] = out.astype(bf16)
            rk_o[r, :] = rr[:, r].T - ksum
            db_o[r, :] = dot(gsum.astype(bf16), c[r, :])
            dc_o[r, :] = dot(gsum.T.astype(bf16), b[r, :])

    return kernel


def back_kernel(w, n, h0, h1, last_part):
    cols = w + 2 * n if last_part else w

    def kernel(ids, x_in, b_in, slope, xbc, xbce, xd, dts, cc, tok, elink, gxd, dbi, dci, rk, rin,
               dy, edy, sf, dcs, gend, cw, dsk, nr, e2, *rest):
        if last_part:
            slope2, xbc2, xbce2, cw2, dbp, dcp, ddtp, gsk = rest[:8]
            gp_o, edge_o, sum_o = rest[8:11]
        else:
            gp_o, edge_o, sum_o, dbp_o, dcp_o, ddtp_o = rest[:6]
        ds, sp, sr, ext, xq, xe, gw_o, gb_o, ga_o, gdt_o = rest[-10:]
        i = pl.program_id(0)
        nb = TB // CH

        def pick(a, a2, r, c0):
            return a[r, c0 : c0 + 256] if c0 < w else a2[r, c0 - w : c0 - w + 256]

        @pl.when(i == 0)
        def _():
            ds[...] = gend[...].astype(f32)
            ext[TB : TB + 8, :] = jnp.zeros((8, cols), f32)
            gw_o[...] = jnp.zeros_like(gw_o)
            gb_o[...] = jnp.zeros_like(gb_o)
            ga_o[...] = jnp.zeros_like(ga_o)
            gdt_o[...] = jnp.zeros_like(gdt_o)

        if not last_part:
            slope2 = xbc2 = xbce2 = cw2 = None
        dt = dts[:, :128]
        pieces, leaves = [dt], []
        for k in range(nb):
            r = slice(k * CH, (k + 1) * CH)
            c2 = cc[r, :]
            pieces.append(jnp.exp2(c2[CH - 1 :] - c2) * tok[r, 2:3])
            leaves.append(jnp.exp2(c2[CH - 1 :]) * tok[(k + 1) * CH - 1 : (k + 1) * CH, 1:2])
        lv = jnp.concatenate([jnp.broadcast_to(v, (8, 128)) for v in leaves], axis=0)
        sp[...] = spread(jnp.concatenate(pieces + [lv], axis=0), e2[...])
        lsum = [None] * nb
        for k in reversed(range(nb)):
            r = slice(k * CH, (k + 1) * CH)
            lacc = []
            gb = dbi[r, :]
            gc = dci[r, :]
            for c0 in range(0, w, 256):
                c = slice(c0, c0 + 256)
                dsv = ds[:, c]
                dsb = dsv.astype(bf16)
                sfv = sf[k, :, c]
                sr[r, c] = dot(b_in[r, :], dsb)
                xwv = (xd[r, c].astype(f32) * sp[TB + k * CH : TB + (k + 1) * CH, c]).astype(bf16)
                gb = gb + dot_nt(xwv, dsb)
                gc = gc + dot_nt(edy[r, c], sfv)
                lacc.append(jnp.sum(dsv * sfv.astype(f32), axis=0, keepdims=True))
                lvr = sp[2 * TB + 8 * k : 2 * TB + 8 * k + 1, c]
                ds[:, c] = lvr * dsv + dcs[k, :, c].astype(f32)
            lsum[k] = head_sums(jnp.concatenate(lacc, axis=1), e2)[0:1]
            if last_part:
                ext[r, w : w + n] = (gb + dbp[r, :]) * slope2[r, :n].astype(f32)
                ext[r, w + n :] = (gc + dcp[r, :]) * slope2[r, n:].astype(f32)
            else:
                dbp_o[r, :] = gb
                dcp_o[r, :] = gc

        def strip(r, re):
            x = x_in[r, :].astype(f32)
            es = sp[re, :] * sr[r, :]
            q = gxd[r, :].astype(f32) + es
            gx = sp[r, :] * q + dsk[...] * dy[r, :].astype(f32)
            ext[r, 0:w] = gx * slope[r, :].astype(f32)
            xq[r, :] = (x * q).astype(bf16)
            xe[r, :] = (x * es).astype(bf16)

        for t in range(TB // 16):
            strip(slice(t * 16, t * 16 + 16), slice(TB + t * 16, TB + t * 16 + 16))
        gdt = dot_nt(xq[...], e2[0:128, :])
        et = dot_nt(xe[...], e2[0:128, :]) * dt
        ri = lax.broadcasted_iota(jnp.int32, (CH, CH), 0)
        ci = lax.broadcasted_iota(jnp.int32, (CH, CH), 1)
        hl = lax.broadcasted_iota(jnp.int32, (1, 128), 1)
        hm = ((hl >= h0) & (hl < h1)).astype(f32)
        tri = jnp.concatenate([(ci >= ri).astype(f32), (ci < ri).astype(f32)], axis=1)
        for k in range(nb):
            r = slice(k * CH, (k + 1) * CH)
            v = jnp.concatenate([rk[r, :] + rin[r, :] * hm, et[r]], axis=0)
            ga = jnp.dot(tri, v, precision=HIGH, preferred_element_type=f32) + lsum[k] * leaves[k]
            ddt = (gdt[r] + ga * nr[...]) * dts[r, 128:]
            gad = ga * dts[r, :128]
            acc_a, acc_d = gad[0:8], ddt[0:8]
            for q in range(8, CH, 8):
                acc_a = acc_a + gad[q : q + 8]
                acc_d = acc_d + ddt[q : q + 8]
            ga_o[...] += acc_a
            gdt_o[...] += acc_d
            if last_part:
                gp_o[r, cols:] = (ddt + ddtp[r, :]).astype(bf16)
            else:
                ddtp_o[r, :] = ddt
        for r0 in range(0, TB, 64):
            rs = slice(r0, r0 + 64)
            links = [jnp.broadcast_to(tok[rs, 6 + s : 7 + s], (64, 256)) for s in (1, 2, 3)]
            for c0 in range(0, cols, 256):
                c = slice(c0, c0 + 256)
                g0 = ext[rs, c]
                xb = pick(xbc, xbc2, rs, c0).astype(f32)
                gsum = pick(cw, cw2, slice(3, 4), c0) * g0
                ws = [None, None, None, g0 * xb]
                for s in (1, 2, 3):
                    gs = ext[r0 + s : r0 + s + 64, c] * links[s - 1]
                    gsum = gsum + pick(cw, cw2, slice(3 - s, 4 - s), c0) * gs
                    ws[3 - s] = gs * xb
                gp_o[rs, c] = gsum.astype(bf16)
                gb = g0[0:8]
                for q in range(8, 64, 8):
                    gb = gb + g0[q : q + 8]
                gb_o[:, c] += gb
                for o in range(4):
                    v = ws[o][0:8]
                    for q in range(8, 64, 8):
                        v = v + ws[o][q : q + 8]
                    gw_o[8 * o : 8 * o + 8, c] += v
        ext[TB : TB + 8, :] = ext[0:8, :]

        @pl.when(i == pl.num_programs(0) - 1)
        def _():
            zero = jnp.zeros((8, 256), f32)
            for c0 in range(0, cols, 256):
                c = slice(c0, c0 + 256)
                xb = pick(xbce, xbce2, slice(8, 16), c0).astype(f32)
                ext[8:16, c] = ext[TB : TB + 8, c]
                ext[0:8, c] = zero
                gsum = zero
                for s in (1, 2, 3):
                    gs = ext[s : s + 8, c] * elink[:, 6 + s : 7 + s]
                    gsum = gsum + pick(cw, cw2, slice(3 - s, 4 - s), c0) * gs
                    gw_o[8 * (3 - s) : 8 * (3 - s) + 8, c] += gs * xb
                edge_o[:, c] = jnp.concatenate([zero, gsum], axis=0).astype(bf16)
                sums = [jnp.sum(gw_o[8 * o : 8 * o + 8, c], axis=0, keepdims=True) for o in range(4)]
                sums.append(jnp.sum(gb_o[:, c], axis=0, keepdims=True))
                sum_o[:, c] = jnp.concatenate(sums + [zero[0:3]], axis=0)
            sum_o[5:6, 0:128] = jnp.sum(ga_o[...], axis=0, keepdims=True)
            sum_o[6:7, 0:128] = jnp.sum(gdt_o[...], axis=0, keepdims=True)
            if last_part:
                sum_o[7:8, 0:128] = gsk[0:1, :]

    return kernel


def input_kernel(np_, di, conv, heads):
    def kernel(ids, gpz, gpa, gpb, ea, eb, u, e, *rest):
        wz, wx = rest[:np_], rest[np_ : 2 * np_]
        gain, gi_o, zbuf, xbuf, gn = rest[2 * np_ :]
        i = pl.program_id(0)

        @pl.when(i == 0)
        def _():
            xbuf[:, conv:] = jnp.zeros((xbuf.shape[0], xbuf.shape[1] - conv), bf16)
            place(zbuf, ids, wz, di)
            place(xbuf, ids, wx, conv + heads)

        wa = gpa.shape[1]
        wd = u.shape[1]
        last = (i == pl.num_programs(0) - 1).astype(f32)
        for c0 in range(0, wd, 256):
            c = slice(c0, c0 + 256)
            g = dot_nt(gpz[...], zbuf[c, :]) + dot_nt(gpa[...], xbuf[c, :wa]) + dot_nt(gpb[...], xbuf[c, wa:])
            tail = (dot_nt(ea[...], xbuf[c, :wa]) + dot_nt(eb[...], xbuf[c, wa:conv])) * last
            gn[: TB - 16, c] = g[: TB - 16]
            gn[TB - 16 :, c] = g[TB - 16 :] + tail
        for r0 in range(0, TB, 16):
            r = slice(r0, r0 + 16)
            uf = u[r, :].astype(f32)
            scale = lax.rsqrt(jnp.mean(uf * uf, axis=-1, keepdims=True) + EPS)
            unit = uf * scale
            dn = gn[r, :] * gain[...]
            m = jnp.mean(dn * unit, axis=-1, keepdims=True)
            gi_o[r, :] = (e[r, :].astype(f32) + scale * (dn - unit * m)).astype(bf16)

    return kernel


def swap(v, axis, bit):
    return lax.ppermute(v, axis, [(k, k ^ bit) for k in range(lax.axis_size(axis))])


def shift(v, axis, steps):
    n = lax.axis_size(axis)
    return lax.ppermute(v, axis, [(k, k + steps) for k in range(n) if 0 <= k + steps < n])


def bits_of(n):
    return [1 << k for k in reversed(range((n - 1).bit_length()))]


def after(v, dep):
    if dep is None:
        return v
    return lax.optimization_barrier((v, dep))[0]


def gather_parts(v, axis):
    parts = [v]
    for bit in bits_of(lax.axis_size(axis)):
        parts = parts + [swap(p, axis, bit) for p in parts]
    return parts


def in_order(parts, axis):
    at = lax.axis_index(axis)
    n = lax.axis_size(axis)
    v = jnp.stack(parts)
    rest = v.shape[1:]
    bits = bits_of(n)
    v = v.reshape((2,) * len(bits) + rest)
    for k, bit in enumerate(reversed(bits)):
        v = jnp.where((at // bit) % 2 == 0, v, jnp.flip(v, k))
    order = tuple(reversed(range(len(bits))))
    return v.transpose(order + tuple(range(len(bits), v.ndim))).reshape((n,) + rest)


def part_ids(axis):
    ids = [lax.axis_index(axis)]
    for bit in bits_of(lax.axis_size(axis)):
        ids = ids + [k ^ bit for k in ids]
    return ids


def add(a, b):
    return (a.astype(f32) + b.astype(f32)).astype(bf16)


def pair_steps(gs):
    nw = lax.axis_size("wshard")
    w = lax.axis_index("wshard")
    n = min(g.shape[0] for g in gs) // nw

    def pick(at):
        out = []
        for g in gs:
            v = g.reshape(nw // 2, 2, -1, g.shape[-1])
            v = lax.dynamic_index_in_dim(v, at, 1, keepdims=False)
            k = v.shape[1] // n
            out += [v[:, q * n : (q + 1) * n] for q in range(k)]
        return jnp.concatenate(out, axis=2) if len(out) > 1 else out[0]

    send, keep = pick(1 - w % 2), pick(w % 2)
    dep = yield send
    yield add(keep, swap(after(send, dep), "wshard", 1))


def other_steps(v):
    nw = lax.axis_size("wshard")
    w = lax.axis_index("wshard")
    n = v.shape[1]
    for bit in [1 << k for k in range(1, (nw - 1).bit_length())]:
        at = (w // bit) % 2
        v = v.reshape(-1, 2, n, v.shape[-1]).swapaxes(0, 1)
        send = lax.dynamic_index_in_dim(v, 1 - at, 0, keepdims=False)
        keep = lax.dynamic_index_in_dim(v, at, 0, keepdims=False)
        dep = yield send
        v = add(keep, swap(after(send, dep), "wshard", bit))
    yield v.reshape(n, -1)


def pairs_of(n):
    bits = [1 << k for k in range((n - 1).bit_length())]
    return [bits[k : k + 2] for k in range(0, len(bits), 2)]


def swap_all(parts, axis, bits):
    got = parts[:1]
    for m in range(1, 1 << len(bits)):
        got.append(swap(parts[m], axis, sum(bit for k, bit in enumerate(bits) if (m >> k) & 1)))
    return got


def by_index(got, at, bits):
    for k, bit in enumerate(bits):
        here = (at // bit) % 2 == 1
        got = [jnp.where(here, got[m ^ (1 << k)], got[m]) for m in range(len(got))]
    return got


def seq_steps(v):
    groups = pairs_of(lax.axis_size("seq"))
    s = lax.axis_index("seq")
    single = groups.pop() if len(groups[-1]) == 1 else None
    for bits in groups:
        n = 1 << len(bits)
        at = (s // bits[0]) % n
        v = v.reshape(n, -1, v.shape[-1])
        send = [lax.dynamic_index_in_dim(v, at ^ m, 0, keepdims=False) for m in range(n)]
        dep = yield tuple(send)
        got = swap_all(after(send, dep), "seq", bits)
        v = sum(g.astype(f32) for g in got).astype(bf16)
    if single:
        dep = yield v
        v = add(v, swap(after(v, dep), "seq", single[0]))
    for bits in reversed(groups):
        dep = yield v
        v = after(v, dep)
        got = swap_all([v] * (1 << len(bits)), "seq", bits)
        dep = yield tuple(got[1:])
        v = jnp.concatenate(by_index(after(tuple(got), dep), s, bits), axis=0)
    yield v.astype(f32)


def small_steps(v):
    for axis in ("wshard", "seq"):
        at = lax.axis_index(axis)
        for bits in pairs_of(lax.axis_size(axis)):
            dep = yield v
            v = after(v, dep)
            v = sum(by_index(swap_all([v] * (1 << len(bits)), axis, bits), at, bits))
    yield v


def pack_state(decay, state):
    hi, lo = two(decay)
    return jnp.concatenate([state.astype(bf16), hi, lo], axis=0)


def unpack_state(v, n):
    return v[n : n + 8].astype(f32)[:1] + v[n + 8 : n + 16].astype(f32)[:1], v[:n].astype(f32)


def carried(send, decay, state, sign, tokens):
    n = state.shape[0]
    span = 1
    while span < -(-LONGEST // tokens):
        if span > 1:
            send = pack_state(decay, state)
        dep = yield send
        d, s = unpack_state(shift(after(send, dep), "seq", sign * span), n)
        state = state + decay[:1] * s
        decay = decay * d
        span *= 2
    send = state.astype(bf16)
    dep = yield send
    yield shift(after(send, dep), "seq", sign)


class Steps:
    def __init__(self, gen):
        self.gen = gen
        self.value = next(gen)

    def step(self, dep=None):
        try:
            self.value = self.gen.send(dep)
        except StopIteration:
            pass
        return self.value

    def finish(self):
        for self.value in self.gen:
            pass
        return self.value


def body(inputs, cotangent, lengths, in_proj, out_proj, conv_weight, conv_bias, a_log, d_skip,
         dt_bias, norm_gain, gate_gain):
    t, d = inputs.shape[1:]
    nw = lax.axis_size("wshard")
    di = out_proj.shape[0] * nw
    heads = a_log.shape[0] * nw
    conv = conv_bias.shape[0] * nw
    taps = conv_weight.shape[0]
    n = (conv - di) // 2
    p = di // heads
    docs = lengths.shape[1]
    nt, nc, nb = t // TB, t // CH, TB // CH
    wide = conv + 128
    first = lax.axis_index("seq") * t
    pos = first - 8 + jnp.arange(t + 16, dtype=jnp.int32)
    ends = jnp.cumsum(lengths[0], dtype=jnp.int32)
    seg = jnp.sum((pos[:, None] >= ends[None]).astype(jnp.int32), axis=1)
    seg = jnp.where(pos < 0, -1, seg)
    here = seg[: t + 8]
    own = seg[8 : t + 8]
    entering = jnp.repeat(seg[7 : t + 7 : CH], CH)
    leaving = jnp.repeat(seg[7 + CH : t + 8 : CH], CH)
    zero8 = jnp.zeros((8,), jnp.int32)
    back = [jnp.concatenate([zero8, (seg[8 - k : t + 8 - k] == own).astype(jnp.int32)]) for k in (3, 2, 1)]
    ahead = [(seg[k : t + 8 + k] == here).astype(jnp.int32) for k in (1, 2, 3)]
    cols = [here, jnp.concatenate([zero8, (entering == own).astype(jnp.int32)]),
            jnp.concatenate([zero8, (leaving == own).astype(jnp.int32)])]
    cols = cols + back + [(here < docs).astype(jnp.int32)] + ahead + [jnp.zeros_like(here)] * 6
    tok_all = jnp.stack(cols, axis=1).astype(f32)
    tok, elink = tok_all[8:], tok_all[:8]
    segr = own.astype(f32)[None]
    ids = jnp.stack(part_ids("wshard")).astype(jnp.int32)
    u, cot = inputs[0], cotangent[0]
    ue = shift(u[t - 16 :], "seq", 1)
    wx, wz = in_proj[:, di:], in_proj[:, :di]
    pc = conv // nw
    width = -(-max(pc, di // nw, 384) // 128) * 128


    def line(*vs):
        vs = [v if v.ndim == 2 else v[None] for v in vs]
        vs = [jnp.pad(v, ((0, 0), (0, (width if k == len(vs) - 1 else 128 * (k + 1)) - 128 * k - v.shape[1])))
              for k, v in enumerate(vs)]
        return jnp.concatenate(vs, axis=1)

    small = jnp.concatenate(
        [line(conv_weight), line(conv_bias), line(gate_gain), line(norm_gain), line(a_log, d_skip, dt_bias)], axis=0)
    wx_parts = gather_parts(wx, "wshard")
    small = in_order(gather_parts(after(small, (wx_parts[nw // 2], wz, tok, ids, ue)), "wshard"), "wshard").astype(f32)
    wz_parts = gather_parts(after(wz, wx_parts[-1]), "wshard")
    wo_parts = gather_parts(after(out_proj, wx_parts[-1]), "wshard")
    hw = heads // nw
    cw = small[:, :taps, :pc].swapaxes(0, 1).reshape(taps, conv)
    cb = small[:, taps, :pc].reshape(1, conv)
    gain_gate = small[:, taps + 1, : di // nw].reshape(1, di)
    gain_in = small[:, taps + 2, : d // nw].reshape(1, d)
    log_rate, skip, dtb = [small[:, taps + 3, 128 * k : 128 * k + hw].reshape(1, heads) for k in range(3)]
    rate = -jnp.exp(log_rate)
    pad = ((0, 0), (0, 128 - heads))
    nr = jnp.pad(rate, pad)
    nr2 = nr * LOG2E
    dtb = jnp.pad(dtb, pad)
    dsk = jnp.repeat(skip, p, axis=1)
    e1 = np.arange(128)[:, None] == np.arange(di)[None] // p
    e2 = jnp.asarray(np.concatenate([e1, e1], axis=0), bf16)
    hot = jnp.asarray(np.arange(heads * CH)[:, None] // CH == np.arange(128)[None], bf16)

    outs = [
        (rows(TB, d), (t, d), bf16),
        (rows(TB, conv), (t, conv), bf16),
        (rows(TB, conv), (t, conv), bf16),
        (rows(TB, conv), (t, conv), bf16),
        (rows(TB, di), (t, di), bf16),
        (rows(TB, 256), (t, 256), f32),
        (rows(TB, 128), (t, 128), f32),
        (pl.BlockSpec((32, TB), lambda i, s: (0, i)), (32, t), f32),
        (pl.BlockSpec((nb, n, di), lambda i, s: (i, 0, 0)), (nc, n, di), bf16),
        (pl.BlockSpec((nb, 8, 128), lambda i, s: (i, 0, 0)), (nc, 8, 128), f32),
        (whole((n, di)), (n, di), f32),
        (whole((8, di)), (8, di), f32),
        (whole((n + 16, di)), (n + 16, di), bf16),
        (whole((16, d)), (16, d), bf16),
        (whole((16, conv)), (16, conv), bf16),
    ]
    ins = [rows(TB, d), whole((16, d)), whole((1, d))] + [whole(v.shape) for v in wx_parts]
    ins += [whole((taps, conv)), whole((1, conv)), whole((1, 128)), whole((1, 128)), rows(TB, 16), whole((256, di))]
    scratch = [
        pltpu.VMEM((d, wide), bf16),
        pltpu.VMEM((TB + 8, conv), f32),
        pltpu.VMEM((n, di), f32),
        pltpu.VMEM((1, 128), f32),
        pltpu.VMEM((2 * TB + 8 * nb, di), f32),
    ]
    (nrm, xbc, xc, slope, xd, dts, cc, ct, st, dbf, end, tot, pack, nrme, xbce) = call(
        front_kernel(nw, di, conv, heads), (nt,), ins, outs, scratch, 15,
        [ids, u, ue, gain_in] + wx_parts + [cw, cb, dtb, nr2, tok, e2], "front")
    chain = Steps(carried(pack, tot, end, 1, t))
    chain.step(wz_parts[1])
    chain.step()
    chain.step(wo_parts[1])
    incoming = chain.finish()

    crow = pl.BlockSpec((32, TI), lambda i, s: (0, i))
    srow = pl.BlockSpec((1, TI), lambda i, s: (0, i))
    crow2 = pl.BlockSpec((32, CH), lambda i, s: (0, i))
    srow2 = pl.BlockSpec((1, CH), lambda i, s: (0, i))
    bspec, cspec = rows(TI, n, di // n), rows(TI, n, di // n + 1)
    (yin,) = call(
        inner_kernel(heads, di), (t // TI,),
        [bspec, cspec, rows(TI, di), rows(TI, 128), crow, rows(TI, 16), srow],
        [(rows(TI, di), (t, di), bf16)], [], 10,
        [ids, xc, xc, xd, cc, ct, tok, segr], "inner")

    blk = pl.BlockSpec((nb, n, di), lambda i, s: (i, 0, 0))
    outs = [
        (rows(TB, d), (t, d), bf16),
        (rows(TB, di), (t, di), bf16),
        (rows(TB, di), (t, di), bf16),
        (rows(TB, di), (t, di), bf16),
        (rows(TB, di), (t, di), bf16),
        (rows(TB, d), (t, d), bf16),
        (blk, (nc, n, di), bf16),
        (blk, (nc, n, di), bf16),
        (rows(TB, 128), (t, 128), f32),
        (whole((8, 128)), (8, 128), f32),
        (whole((n, di)), (n, di), f32),
        (whole((n + 16, di)), (n + 16, di), bf16),
    ]
    ins = [rows(TB, d), rows(TB, di), rows(TB, di), rows(TB, n, di // n + 1), rows(TB, 128), rows(TB, 16), blk,
           pl.BlockSpec((nb, 8, 128), lambda i, s: (i, 0, 0)), whole((n, di)), whole((8, di)), rows(TB, d), rows(TB, d)]
    ins += [whole(v.shape) for v in wz_parts + wo_parts]
    ins += [whole((1, di)), whole((1, di)), whole((256, di))]
    scratch = [pltpu.VMEM((d, di), bf16), pltpu.VMEM((di, d), bf16)]
    scratch += [pltpu.VMEM((TB, di), f32)] * 3
    scratch += [pltpu.VMEM((TB + 8 * nb, di), f32), pltpu.VMEM((TB, di), bf16), pltpu.VMEM((8, di), f32)]
    (mixed, gn, dz, dy, edy, e, sf, dcs, rin, g_skip, reach, reach_pack) = call(
        gate_kernel(nw, di, d), (nt,), ins, outs, scratch, 25,
        [ids, nrm, yin, xc, xc, cc, tok, st, dbf, incoming, tot, u, cot] + wz_parts + wo_parts + [gain_gate, dsk, e2], "gate")
    tn = (((0,), (0,)), ((), ()))

    def outer(a, b):
        return lax.dot_general(a, b, tn, preferred_element_type=f32)

    back_state = Steps(carried(reach_pack, tot, reach, -1, t))
    s1 = back_state.value
    gw_out = outer(after(gn, s1), e).astype(bf16)
    gw_z = outer(nrm, after(dz, s1)).astype(bf16)
    s2 = back_state.step()
    oz_p = Steps(pair_steps([gw_out, gw_z]))
    oz_w = Steps(other_steps(oz_p.step(s2)))
    oz2 = oz_w.value
    hh, hw2 = heads // 2, di // 2

    def at(shape, col):
        return pl.BlockSpec(shape, lambda i, s: (0, col))

    def half_inner(k, dep):
        outs = [
            (rows(CH, hw2), (t, hw2), bf16),
            (rows(CH, n), (t, n), f32),
            (rows(CH, n), (t, n), f32),
            (rows(CH, 128), (t, 128), f32),
        ]
        return call(
            inner_back_kernel(p, hh * k, hh * (k + 1)), (t // CH,),
            [rows(CH, n, di // n), rows(CH, n, di // n + 1), rows(CH, hw2, k), rows(CH, hw2, k), rows(CH, 128), crow2,
             pl.BlockSpec((hh * CH, 128), lambda i, s: (k, 0)), rows(CH, 16), srow2],
            outs, [pltpu.VMEM((128, CH), f32)], 12,
            [ids, xc, xc, xd, after(dy, dep), cc, ct, hot, tok, segr], "inner_back")

    def rev(block, width, col=0):
        return pl.BlockSpec((block, width), lambda i, s: (nt - 1 - i, col))

    def half_back(k, inner, dep, gend, extra):
        gxd, dbi, dci, rk = inner
        last = k == 1
        cols = hw2 + 2 * n if last else hw2
        rblk = pl.BlockSpec((nb, n, hw2), lambda i, s: (nt - 1 - i, 0, k))
        ins = [rev(TB, hw2, k), rev(TB, n, di // n), rev(TB, hw2, k), rev(TB, hw2, k), at((16, hw2), k),
               rev(TB, hw2, k), rev(TB, 256), rev(TB, 128), rev(TB, 16), whole((8, 16)), rev(TB, hw2),
               rev(TB, n), rev(TB, n), rev(TB, 128), rev(TB, 128), rev(TB, hw2, k), rev(TB, hw2, k), rblk, rblk,
               at((n, hw2), k), at((taps, hw2), k), at((1, hw2), k), whole((1, 128)), at((256, hw2), k)]
        args = [ids, xc, xc, slope, xbc, xbce, xd, dts, cc, tok, elink, after(gxd, dep), dbi, dci, rk, rin, dy,
                edy, sf, dcs, gend, cw, dsk, nr, e2]
        outs = [
            (rev(TB, cols + 128 * last), (t, cols + 128 * last), bf16),
            (whole((16, cols)), (16, cols), bf16),
            (whole((8, cols)), (8, cols), f32),
        ]
        if last:
            ins += [rev(TB, 2 * n, di // (2 * n)), rev(TB, 2 * n, di // (2 * n)), at((16, 2 * n), di // (2 * n)),
                    at((taps, 2 * n), di // (2 * n)), rev(TB, n), rev(TB, n), rev(TB, 128), whole((8, 128))]
            args += [slope, xbc, xbce, cw] + list(extra)
        else:
            outs += [(rev(TB, n), (t, n), f32), (rev(TB, n), (t, n), f32), (rev(TB, 128), (t, 128), f32)]
        scratch = [
            pltpu.VMEM((n, hw2), f32),
            pltpu.VMEM((2 * TB + 8 * nb, hw2), f32),
            pltpu.VMEM((TB, hw2), f32),
            pltpu.VMEM((TB + 8, cols), f32),
            pltpu.VMEM((TB, hw2), bf16),
            pltpu.VMEM((TB, hw2), bf16),
            pltpu.VMEM((8 * taps, cols), f32),
            pltpu.VMEM((8, cols), f32),
            pltpu.VMEM((8, 128), f32),
            pltpu.VMEM((8, 128), f32),
        ]
        return call(back_kernel(hw2, n, hh * k, hh * (k + 1), last), (nt,), ins, outs, scratch, 15, args, "back")

    in_a = half_inner(0, (s2, oz2))
    s3 = back_state.step(oz2)
    s3, in_a0 = lax.optimization_barrier((s3, in_a[0]))
    in_b = half_inner(1, (s3, in_a0))
    back_state.step(in_a[0])
    gend = back_state.finish()
    oz_w.step()
    oz_s = Steps(seq_steps(oz_w.finish()))
    oz3 = oz_s.value
    (gpa, edge_a, sum_a, dbp, dcp, ddtp) = half_back(0, in_a, (in_b[0], oz3), gend, None)
    oz4 = oz_s.step(in_b[0])
    gw_xa = (outer(nrm, after(gpa, oz4)) + outer(nrme, edge_a)).astype(bf16)
    xa_p = Steps(pair_steps([gw_xa]))
    xa1 = xa_p.value
    (gpb, edge_b, sum_b) = half_back(1, in_b, (oz4, xa1), gend, (dbp, dcp, ddtp, g_skip))
    oz5 = oz_s.step(gpa)
    oz5, gpb_late = lax.optimization_barrier((oz5, gpb))
    gw_xb = outer(nrm, gpb_late)
    cb2 = conv - hw2
    gw_xb = jnp.concatenate(
        [gw_xb[:, :cb2] + outer(nrme, edge_b), gw_xb[:, cb2 : cb2 + heads]], axis=1).astype(bf16)
    xb_p = Steps(pair_steps([gw_xb]))
    x_w = Steps(other_steps(jnp.concatenate([xa_p.step(), xb_p.step()], axis=2)))
    x2 = x_w.value
    ea_in, eb_in = shift(edge_a, "seq", -1), shift(edge_b, "seq", -1)
    oz7 = oz_s.step((x2, ea_in))

    ins = [rows(TB, di), rows(TB, hw2), rows(TB, wide - hw2), whole((16, hw2)), whole((16, cb2)), rows(TB, d), rows(TB, d)]
    ins += [whole(v.shape) for v in wz_parts + wx_parts] + [whole((1, d))]
    outs = [(rows(TB, d), (t, d), bf16)]
    (grad_input,) = call(
        input_kernel(nw, di, conv, heads), (nt,), ins, outs,
        [pltpu.VMEM((d, di), bf16), pltpu.VMEM((d, wide), bf16), pltpu.VMEM((TB, d), f32)], 12,
        [ids, dz, after(gpa, x2), gpb, ea_in, eb_in, u, e] + wz_parts + wx_parts + [gain_in], "input")
    sums = Steps(small_steps(jnp.concatenate([sum_a, sum_b], axis=1)))
    x_s = Steps(seq_steps(x_w.finish()))
    x3 = x_s.value
    sums.step((x3, grad_input))
    x4 = x_s.step((grad_input, oz7))
    sums.step(x4)
    oz_s.step(x4)
    x5 = x_s.step()
    sums.step(x5)
    r_x, r_oz, total = x_s.finish(), oz_s.finish(), sums.finish()
    k = r_oz.shape[1] - di
    r_out = jnp.concatenate([r_oz[:, q * d : (q + 1) * d] for q in range(k // d)], axis=0)
    r_z = r_oz[:, k:]
    w = lax.axis_index("wshard")

    def mine(v):
        width = v.shape[-1] // nw
        return lax.dynamic_slice_in_dim(v, w * width, width, axis=v.ndim - 1)

    by_head = total[5:8, :heads] + total[5:8, hw2 : hw2 + heads]
    by_head = mine(by_head * jnp.concatenate([rate, jnp.ones((2, heads), f32)], axis=0))
    res = [mine(total[:taps]), mine(total[taps]), by_head[0], by_head[2], by_head[1]]
    res.append((jnp.sum(r_z * wz.astype(f32), axis=1) + jnp.sum(r_x * wx.astype(f32), axis=1)) / norm_gain.astype(f32))
    res.append(jnp.sum(r_out * out_proj.astype(f32), axis=1) / gate_gain.astype(f32))
    return (mixed[None], grad_input[None], jnp.concatenate([r_z, r_x], axis=1), r_out) + tuple(res)


def solution(mesh):
    wide = P("wshard", "seq", None)
    mat = P("wshard", None)
    taps = P(None, "wshard")
    vec = P("wshard")
    return jax.shard_map(
        body,
        mesh=mesh,
        in_specs=(wide, wide, mat, mat, mat, taps) + (vec,) * 6,
        out_specs=(wide, wide, mat, mat, taps) + (vec,) * 6,
        check_vma=False,
    )
```

```python
import jax
import jax.numpy as jnp
import numpy as np
from jax import lax
from jax.experimental import pallas as pl
from jax.experimental.pallas import tpu as pltpu
from jax.sharding import PartitionSpec as P

f32 = jnp.float32
bf16 = jnp.bfloat16
EPS = 1e-05
LOG2E = 1.4426950408889634
CH = 128
TB = 256
TI = 256
LONGEST = 4096
HIGH = lax.Precision.HIGHEST
MB = 1024 * 1024
VMEM = 53 * MB


def sigmoid(v):
    return 0.5 * jnp.tanh(0.5 * v) + 0.5


def dot(a, b):
    return jnp.dot(a, b, preferred_element_type=f32)


def dot_nt(a, b):
    return lax.dot_general(a, b, (((1,), (1,)), ((), ())), preferred_element_type=f32)


def two(v):
    hi = v.astype(bf16)
    return hi, (v - hi.astype(f32)).astype(bf16)


def spread(v, e2):
    return dot(jnp.concatenate(two(v), axis=1), e2)


def head_sums(row, e2):
    hi, lo = two(jnp.broadcast_to(row, (8, row.shape[1])))
    return dot_nt(hi, e2[0:128, :]) + dot_nt(lo, e2[0:128, :])


def cost(us):
    return pl.CostEstimate(flops=int(us * 1.1e9), bytes_accessed=1 << 20, transcendentals=0)


def call(kernel, grid, ins, outs, scratch, us, args, name):
    return pl.pallas_call(
        kernel,
        grid_spec=pltpu.PrefetchScalarGridSpec(
            num_scalar_prefetch=1,
            grid=grid,
            in_specs=ins,
            out_specs=[o[0] for o in outs],
            scratch_shapes=scratch,
        ),
        out_shape=[jax.ShapeDtypeStruct(o[1], o[2]) for o in outs],
        compiler_params=pltpu.CompilerParams(
            vmem_limit_bytes=VMEM, dimension_semantics=("arbitrary",)
        ),
        cost_estimate=cost(us),
        name=name,
    )(*args)


def rows(block, cols, col=0):
    return pl.BlockSpec((block, cols), lambda i, s: (i, col))


def whole(shape):
    return pl.BlockSpec(shape, lambda i, s: (0,) * len(shape))


def norm_rows(uf, gain):
    scale = lax.rsqrt(jnp.mean(uf * uf, axis=-1, keepdims=True) + EPS)
    return (uf * scale * gain).astype(bf16)


def place(buf, ids, parts, width):
    for j, part in enumerate(parts):
        n = part.shape[0]
        at = pl.multiple_of(ids[j] * n, 64)
        buf[pl.ds(at, n), :width] = part[...]


def put_pack(ref, decay, state):
    n = state.shape[0]
    hi, lo = two(decay)
    ref[0:n, :] = state.astype(bf16)
    ref[n:, :] = jnp.concatenate([hi.astype(f32), lo.astype(f32)], axis=0).astype(bf16)


def front_kernel(np_, di, conv, heads):
    def kernel(ids, u, ue, gain, *rest):
        parts = rest[:np_]
        (cw, cb, dtb, nr, tok, e2, nrm_o, xbc_o, xc_o, slope_o, xd_o, dts_o, cc_o, ct_o,
         st_o, db_o, end_o, tot_o, pk_o, nrme_o, xbce_o, wbuf, ext, state, kd, sp) = rest[np_:]
        i = pl.program_id(0)
        n = (conv - di) // 2

        @pl.when(i == 0)
        def _():
            wbuf[:, conv:] = jnp.zeros((wbuf.shape[0], wbuf.shape[1] - conv), bf16)
            place(wbuf, ids, parts, conv + heads)
            nrme = norm_rows(ue[...].astype(f32), gain[...])
            nrme_o[...] = nrme
            pe = dot(nrme, wbuf[:, :conv]).astype(bf16)
            xbce_o[...] = pe
            ext[0:8, :] = pe.astype(f32)[8:16]
            state[...] = jnp.zeros_like(state)
            kd[...] = jnp.ones_like(kd)

        nrm = norm_rows(u[...].astype(f32), gain[...])
        nrm_o[...] = nrm
        pd = dot(nrm, wbuf[:, conv:])
        for c0 in range(0, conv, 256):
            px = dot(nrm, wbuf[:, c0 : c0 + 256]).astype(bf16)
            xbc_o[:, c0 : c0 + 256] = px
            ext[8 : 8 + TB, c0 : c0 + 256] = px.astype(f32)
        sh = pd + dtb[...]
        dt = jnp.maximum(sh, 0.0) + jnp.log1p(jnp.exp(-jnp.abs(sh)))
        dts_o[:, :128] = dt
        dts_o[:, 128:] = jax.nn.sigmoid(sh)
        a2 = dt * nr[...]
        ri = lax.broadcasted_iota(jnp.int32, (CH, CH), 0)
        ci = lax.broadcasted_iota(jnp.int32, (CH, CH), 1)
        low = (ri >= ci).astype(f32)
        pieces = [dt]
        leaves = []
        for k in range(TB // CH):
            r = slice(k * CH, (k + 1) * CH)
            c2 = jnp.dot(low, a2[r], precision=HIGH, preferred_element_type=f32)
            cc_o[r, :] = c2
            ct_o[:, r] = c2.T[: ct_o.shape[0], :]
            pieces.append(jnp.exp2(c2[CH - 1 :] - c2) * tok[r, 2:3])
            leaves.append(jnp.exp2(c2[CH - 1 :]) * tok[(k + 1) * CH - 1 : (k + 1) * CH, 1:2])
        lv = jnp.concatenate([jnp.broadcast_to(v, (8, 128)) for v in leaves], axis=0)
        sp[...] = spread(jnp.concatenate(pieces + [lv], axis=0), e2[...])
        for r0 in range(0, TB, 64):
            l0, l1, l2 = tok[r0 : r0 + 64, 3:4], tok[r0 : r0 + 64, 4:5], tok[r0 : r0 + 64, 5:6]
            for c0 in range(0, conv, 256):
                c = slice(c0, c0 + 256)
                pre = cb[:, c] + cw[3:4, c] * ext[8 + r0 : 72 + r0, c]
                pre = pre + cw[2:3, c] * (ext[7 + r0 : 71 + r0, c] * l2)
                pre = pre + cw[1:2, c] * (ext[6 + r0 : 70 + r0, c] * l1)
                pre = pre + cw[0:1, c] * (ext[5 + r0 : 69 + r0, c] * l0)
                sg = sigmoid(pre)
                xc = pre * sg
                xc_o[r0 : r0 + 64, c] = xc.astype(bf16)
                slope_o[r0 : r0 + 64, c] = (sg + xc * (1.0 - sg)).astype(bf16)
                if c0 < di:
                    xd_o[r0 : r0 + 64, c] = (xc * sp[r0 : r0 + 64, c]).astype(bf16)
        ext[0:8, :] = ext[TB : TB + 8, :]
        for k in range(TB // CH):
            r = slice(k * CH, (k + 1) * CH)
            st_o[k] = state[...].astype(bf16)
            db_o[k] = jnp.broadcast_to(kd[...], (8, 128))
            bt = xc_o[r, di : di + n].astype(f32).T.astype(bf16)
            for c0 in range(0, di, 256):
                c = slice(c0, c0 + 256)
                xw = (xd_o[r, c].astype(f32) * sp[TB + k * CH : TB + (k + 1) * CH, c]).astype(bf16)
                lvr = sp[2 * TB + 8 * k : 2 * TB + 8 * k + 1, c]
                state[:, c] = lvr * state[:, c] + dot(bt, xw)
            kd[...] = kd[...] * leaves[k]

        @pl.when(i == pl.num_programs(0) - 1)
        def _():
            end_o[...] = state[...]
            total = spread(jnp.broadcast_to(kd[...], (8, 128)), e2[...])
            tot_o[...] = total
            put_pack(pk_o, total, state[...])

    return kernel


def inner_kernel(heads, di):
    p = di // heads
    per = 128 // p

    def kernel(ids, b, c, xd, cc, ct, tok, segr, y_o):
        ri = lax.broadcasted_iota(jnp.int32, (CH, CH), 0)
        ci = lax.broadcasted_iota(jnp.int32, (CH, CH), 1)
        lanes = lax.broadcasted_iota(jnp.int32, (1, 128), 1) // p
        for k in range(b.shape[0] // CH):
            r = slice(k * CH, (k + 1) * CH)
            s = dot_nt(c[r, :], b[r, :])
            bias = jnp.where((tok[r, 0:1] == segr[:, r]) & (ri >= ci), 0.0, -1e30)
            for j in range(heads // per):
                xp = xd[r, 128 * j : 128 * j + 128]
                ms, xs = [], []
                for q in range(per):
                    h = per * j + q
                    e = jnp.exp2(cc[r, h : h + 1] - ct[h : h + 1, r] + bias)
                    ms.append((s * e).astype(bf16))
                    xs.append(xp * (lanes == q).astype(f32).astype(bf16))
                out = dot(jnp.concatenate(ms, axis=1), jnp.concatenate(xs, axis=0))
                y_o[r, 128 * j : 128 * j + 128] = out.astype(bf16)

    return kernel


def gate_kernel(np_, di, d):
    def kernel(ids, nrm, yin, x, c_in, cc, tok, st, db, inc, tot, u, cot, *rest):
        wz, wo = rest[:np_], rest[np_ : 2 * np_]
        (gain, dsk, e2, mixed_o, gn_o, dz_o, dy_o, edy_o, e_o, sf_o, dc_o, rin_o, gs_o,
         rg_o, pk_o, zbuf, obuf, z, yi, dgn, ee, pr, gs) = rest[2 * np_ :]
        i = pl.program_id(0)

        @pl.when(i == 0)
        def _():
            place(zbuf, ids, wz, di)
            place(obuf, ids, wo, d)
            gs[...] = jnp.zeros_like(gs)
            rg_o[...] = jnp.zeros_like(rg_o)

        keep = tok[:, 6:7]
        ef = cot[...].astype(f32) * keep
        e = ef.astype(bf16)
        e_o[...] = e
        nb = TB // CH
        ents = []
        for k in range(nb):
            r = slice(k * CH, (k + 1) * CH)
            ents.append(jnp.exp2(cc[r, :]) * tok[r, 1:2])
        ee[...] = spread(jnp.concatenate(ents + [db[k] for k in range(nb)], axis=0), e2[...])
        for k in range(nb):
            r = slice(k * CH, (k + 1) * CH)
            for c0 in range(0, di, 256):
                c = slice(c0, c0 + 256)
                dbr = ee[TB + 8 * k : TB + 8 * k + 1, c]
                sf = (st[k, :, c].astype(f32) + dbr * inc[:, c].astype(f32)).astype(bf16)
                sf_o[k, :, c] = sf
                yi[r, c] = dot(c_in[r, :], sf)
        z[...] = dot(nrm[...], zbuf[...])
        dgn[...] = dot_nt(e, obuf[...])

        def strip(r):
            xs = x[r, :].astype(f32)
            eyi = ee[r, :] * yi[r, :]
            y = yin[r, :].astype(f32) + eyi + dsk[...] * xs
            zz = z[r, :]
            sg = sigmoid(zz)
            act = zz * sg
            g = y * act
            scale = lax.rsqrt(jnp.mean(g * g, axis=-1, keepdims=True) + EPS)
            ug = g * scale
            gn_o[r, :] = (ug * gain[...]).astype(bf16)
            dg0 = dgn[r, :]
            dn = dg0 * gain[...]
            m = jnp.mean(dn * ug, axis=-1, keepdims=True)
            dg = scale * (dn - ug * m)
            dy = dg * act
            dz_o[r, :] = (dg * y * (sg + act * (1.0 - sg))).astype(bf16)
            dy_o[r, :] = dy.astype(bf16)
            ps = xs * dy
            gs[...] += ps[0:8] + ps[8:16]
            edy_o[r, :] = (dy * ee[r, :]).astype(bf16)
            pr[r, :] = (dy * eyi).astype(bf16)

        for t in range(TB // 16):
            strip(slice(t * 16, t * 16 + 16))
        rin_o[...] = dot_nt(pr[...], e2[0:128, :])
        mixed_o[...] = (keep * (u[...].astype(f32) + dot(gn_o[...], obuf[...]))).astype(bf16)
        for k in range(nb):
            r = slice(k * CH, (k + 1) * CH)
            ctr = c_in[r, :].astype(f32).T.astype(bf16)
            for c0 in range(0, di, 256):
                c = slice(c0, c0 + 256)
                dcv = dot(ctr, edy_o[r, c])
                dc_o[k, :, c] = dcv.astype(bf16)
                rg_o[:, c] += ee[TB + 8 * k : TB + 8 * k + 1, c] * dcv

        @pl.when(i == pl.num_programs(0) - 1)
        def _():
            gs_o[...] = head_sums(jnp.sum(gs[...], axis=0, keepdims=True), e2)
            put_pack(pk_o, tot[...], rg_o[...])

    return kernel


def inner_back_kernel(p, h0, h1):
    per = 128 // p

    def kernel(ids, b, c, xd, dy, cc, ct, hot, tok, segr, gxd_o, db_o, dc_o, rk_o, rr):
        si = lax.broadcasted_iota(jnp.int32, (CH, CH), 0)
        ti = lax.broadcasted_iota(jnp.int32, (CH, CH), 1)
        lanes = lax.broadcasted_iota(jnp.int32, (1, 128), 1) // p
        rr[...] = jnp.zeros_like(rr)
        for k in range(b.shape[0] // CH):
            r = slice(k * CH, (k + 1) * CH)
            st = dot_nt(b[r, :], c[r, :])
            bias = jnp.where((tok[r, 0:1] == segr[:, r]) & (ti >= si), 0.0, -1e30)
            gsum = jnp.zeros((CH, CH), f32)
            ksum = jnp.zeros((CH, 128), f32)
            for j in range((h1 - h0) // per):
                xp = xd[r, 128 * j : 128 * j + 128]
                dyp = dy[r, 128 * j : 128 * j + 128]
                dys = jnp.concatenate(
                    [dyp * (lanes == q).astype(f32).astype(bf16) for q in range(per)], axis=0
                )
                gm = dot_nt(xp, dys)
                ms, exs = [], []
                for q in range(per):
                    h = h0 + per * j + q
                    e = jnp.exp2(ct[h : h + 1, r] - cc[r, h : h + 1] + bias)
                    ms.append((st * e).astype(bf16))
                    ge = gm[:, q * CH : (q + 1) * CH] * e
                    gsum = gsum + ge
                    ex = (ge * st).astype(bf16)
                    exs.append(ex)
                    rr[h : h + 1, r] = jnp.sum(ex.astype(f32), axis=0, keepdims=True)
                ksum = ksum + dot(jnp.concatenate(exs, axis=1), hot[per * CH * j : per * CH * (j + 1), :])
                out = dot(jnp.concatenate(ms, axis=1), dys)
                gxd_o[r, 128 * j : 128 * j + 128] = out.astype(bf16)
            rk_o[r, :] = rr[:, r].T - ksum
            db_o[r, :] = dot(gsum.astype(bf16), c[r, :])
            dc_o[r, :] = dot(gsum.T.astype(bf16), b[r, :])

    return kernel


def back_kernel(w, n, h0, h1, last_part):
    cols = w + 2 * n if last_part else w

    def kernel(ids, x_in, b_in, slope, xbc, xbce, xd, dts, cc, tok, elink, gxd, dbi, dci, rk, rin,
               dy, edy, sf, dcs, gend, cw, dsk, nr, e2, *rest):
        if last_part:
            slope2, xbc2, xbce2, cw2, dbp, dcp, ddtp, gsk = rest[:8]
            gp_o, edge_o, sum_o = rest[8:11]
        else:
            gp_o, edge_o, sum_o, dbp_o, dcp_o, ddtp_o = rest[:6]
        ds, sp, sr, ext, xq, xe, gw_o, gb_o, ga_o, gdt_o = rest[-10:]
        i = pl.program_id(0)
        nb = TB // CH

        def pick(a, a2, r, c0):
            return a[r, c0 : c0 + 256] if c0 < w else a2[r, c0 - w : c0 - w + 256]

        @pl.when(i == 0)
        def _():
            ds[...] = gend[...].astype(f32)
            ext[TB : TB + 8, :] = jnp.zeros((8, cols), f32)
            gw_o[...] = jnp.zeros_like(gw_o)
            gb_o[...] = jnp.zeros_like(gb_o)
            ga_o[...] = jnp.zeros_like(ga_o)
            gdt_o[...] = jnp.zeros_like(gdt_o)

        if not last_part:
            slope2 = xbc2 = xbce2 = cw2 = None
        dt = dts[:, :128]
        pieces, leaves = [dt], []
        for k in range(nb):
            r = slice(k * CH, (k + 1) * CH)
            c2 = cc[r, :]
            pieces.append(jnp.exp2(c2[CH - 1 :] - c2) * tok[r, 2:3])
            leaves.append(jnp.exp2(c2[CH - 1 :]) * tok[(k + 1) * CH - 1 : (k + 1) * CH, 1:2])
        lv = jnp.concatenate([jnp.broadcast_to(v, (8, 128)) for v in leaves], axis=0)
        sp[...] = spread(jnp.concatenate(pieces + [lv], axis=0), e2[...])
        lsum = [None] * nb
        for k in reversed(range(nb)):
            r = slice(k * CH, (k + 1) * CH)
            lacc = []
            gb = dbi[r, :]
            gc = dci[r, :]
            for c0 in range(0, w, 256):
                c = slice(c0, c0 + 256)
                dsv = ds[:, c]
                dsb = dsv.astype(bf16)
                sfv = sf[k, :, c]
                sr[r, c] = dot(b_in[r, :], dsb)
                xwv = (xd[r, c].astype(f32) * sp[TB + k * CH : TB + (k + 1) * CH, c]).astype(bf16)
                gb = gb + dot_nt(xwv, dsb)
                gc = gc + dot_nt(edy[r, c], sfv)
                lacc.append(jnp.sum(dsv * sfv.astype(f32), axis=0, keepdims=True))
                lvr = sp[2 * TB + 8 * k : 2 * TB + 8 * k + 1, c]
                ds[:, c] = lvr * dsv + dcs[k, :, c].astype(f32)
            lsum[k] = head_sums(jnp.concatenate(lacc, axis=1), e2)[0:1]
            if last_part:
                ext[r, w : w + n] = (gb + dbp[r, :]) * slope2[r, :n].astype(f32)
                ext[r, w + n :] = (gc + dcp[r, :]) * slope2[r, n:].astype(f32)
            else:
                dbp_o[r, :] = gb
                dcp_o[r, :] = gc

        def strip(r, re):
            x = x_in[r, :].astype(f32)
            es = sp[re, :] * sr[r, :]
            q = gxd[r, :].astype(f32) + es
            gx = sp[r, :] * q + dsk[...] * dy[r, :].astype(f32)
            ext[r, 0:w] = gx * slope[r, :].astype(f32)
            xq[r, :] = (x * q).astype(bf16)
            xe[r, :] = (x * es).astype(bf16)

        for t in range(TB // 16):
            strip(slice(t * 16, t * 16 + 16), slice(TB + t * 16, TB + t * 16 + 16))
        gdt = dot_nt(xq[...], e2[0:128, :])
        et = dot_nt(xe[...], e2[0:128, :]) * dt
        ri = lax.broadcasted_iota(jnp.int32, (CH, CH), 0)
        ci = lax.broadcasted_iota(jnp.int32, (CH, CH), 1)
        hl = lax.broadcasted_iota(jnp.int32, (1, 128), 1)
        hm = ((hl >= h0) & (hl < h1)).astype(f32)
        tri = jnp.concatenate([(ci >= ri).astype(f32), (ci < ri).astype(f32)], axis=1)
        for k in range(nb):
            r = slice(k * CH, (k + 1) * CH)
            v = jnp.concatenate([rk[r, :] + rin[r, :] * hm, et[r]], axis=0)
            ga = jnp.dot(tri, v, precision=HIGH, preferred_element_type=f32) + lsum[k] * leaves[k]
            ddt = (gdt[r] + ga * nr[...]) * dts[r, 128:]
            gad = ga * dts[r, :128]
            acc_a, acc_d = gad[0:8], ddt[0:8]
            for q in range(8, CH, 8):
                acc_a = acc_a + gad[q : q + 8]
                acc_d = acc_d + ddt[q : q + 8]
            ga_o[...] += acc_a
            gdt_o[...] += acc_d
            if last_part:
                gp_o[r, cols:] = (ddt + ddtp[r, :]).astype(bf16)
            else:
                ddtp_o[r, :] = ddt
        for r0 in range(0, TB, 64):
            rs = slice(r0, r0 + 64)
            links = [jnp.broadcast_to(tok[rs, 6 + s : 7 + s], (64, 256)) for s in (1, 2, 3)]
            for c0 in range(0, cols, 256):
                c = slice(c0, c0 + 256)
                g0 = ext[rs, c]
                xb = pick(xbc, xbc2, rs, c0).astype(f32)
                gsum = pick(cw, cw2, slice(3, 4), c0) * g0
                ws = [None, None, None, g0 * xb]
                for s in (1, 2, 3):
                    gs = ext[r0 + s : r0 + s + 64, c] * links[s - 1]
                    gsum = gsum + pick(cw, cw2, slice(3 - s, 4 - s), c0) * gs
                    ws[3 - s] = gs * xb
                gp_o[rs, c] = gsum.astype(bf16)
                gb = g0[0:8]
                for q in range(8, 64, 8):
                    gb = gb + g0[q : q + 8]
                gb_o[:, c] += gb
                for o in range(4):
                    v = ws[o][0:8]
                    for q in range(8, 64, 8):
                        v = v + ws[o][q : q + 8]
                    gw_o[8 * o : 8 * o + 8, c] += v
        ext[TB : TB + 8, :] = ext[0:8, :]

        @pl.when(i == pl.num_programs(0) - 1)
        def _():
            zero = jnp.zeros((8, 256), f32)
            for c0 in range(0, cols, 256):
                c = slice(c0, c0 + 256)
                xb = pick(xbce, xbce2, slice(8, 16), c0).astype(f32)
                ext[8:16, c] = ext[TB : TB + 8, c]
                ext[0:8, c] = zero
                gsum = zero
                for s in (1, 2, 3):
                    gs = ext[s : s + 8, c] * elink[:, 6 + s : 7 + s]
                    gsum = gsum + pick(cw, cw2, slice(3 - s, 4 - s), c0) * gs
                    gw_o[8 * (3 - s) : 8 * (3 - s) + 8, c] += gs * xb
                edge_o[:, c] = jnp.concatenate([zero, gsum], axis=0).astype(bf16)
                sums = [jnp.sum(gw_o[8 * o : 8 * o + 8, c], axis=0, keepdims=True) for o in range(4)]
                sums.append(jnp.sum(gb_o[:, c], axis=0, keepdims=True))
                sum_o[:, c] = jnp.concatenate(sums + [zero[0:3]], axis=0)
            sum_o[5:6, 0:128] = jnp.sum(ga_o[...], axis=0, keepdims=True)
            sum_o[6:7, 0:128] = jnp.sum(gdt_o[...], axis=0, keepdims=True)
            if last_part:
                sum_o[7:8, 0:128] = gsk[0:1, :]

    return kernel


def input_kernel(np_, di, conv, heads):
    def kernel(ids, gpz, gpa, gpb, ea, eb, u, e, *rest):
        wz, wx = rest[:np_], rest[np_ : 2 * np_]
        gain, gi_o, zbuf, xbuf, gn = rest[2 * np_ :]
        i = pl.program_id(0)

        @pl.when(i == 0)
        def _():
            xbuf[:, conv:] = jnp.zeros((xbuf.shape[0], xbuf.shape[1] - conv), bf16)
            place(zbuf, ids, wz, di)
            place(xbuf, ids, wx, conv + heads)

        wa = gpa.shape[1]
        wd = u.shape[1]
        last = (i == pl.num_programs(0) - 1).astype(f32)
        for c0 in range(0, wd, 256):
            c = slice(c0, c0 + 256)
            g = dot_nt(gpz[...], zbuf[c, :]) + dot_nt(gpa[...], xbuf[c, :wa]) + dot_nt(gpb[...], xbuf[c, wa:])
            tail = (dot_nt(ea[...], xbuf[c, :wa]) + dot_nt(eb[...], xbuf[c, wa:conv])) * last
            gn[: TB - 16, c] = g[: TB - 16]
            gn[TB - 16 :, c] = g[TB - 16 :] + tail
        for r0 in range(0, TB, 16):
            r = slice(r0, r0 + 16)
            uf = u[r, :].astype(f32)
            scale = lax.rsqrt(jnp.mean(uf * uf, axis=-1, keepdims=True) + EPS)
            unit = uf * scale
            dn = gn[r, :] * gain[...]
            m = jnp.mean(dn * unit, axis=-1, keepdims=True)
            gi_o[r, :] = (e[r, :].astype(f32) + scale * (dn - unit * m)).astype(bf16)

    return kernel


def swap(v, axis, bit):
    return lax.ppermute(v, axis, [(k, k ^ bit) for k in range(lax.axis_size(axis))])


def shift(v, axis, steps):
    n = lax.axis_size(axis)
    return lax.ppermute(v, axis, [(k, k + steps) for k in range(n) if 0 <= k + steps < n])


def bits_of(n):
    return [1 << k for k in reversed(range((n - 1).bit_length()))]


def after(v, dep):
    if dep is None:
        return v
    return lax.optimization_barrier((v, dep))[0]


def gather_parts(v, axis):
    parts = [v]
    for bit in bits_of(lax.axis_size(axis)):
        parts = parts + [swap(p, axis, bit) for p in parts]
    return parts


def in_order(parts, axis):
    at = lax.axis_index(axis)
    n = lax.axis_size(axis)
    v = jnp.stack(parts)
    rest = v.shape[1:]
    bits = bits_of(n)
    v = v.reshape((2,) * len(bits) + rest)
    for k, bit in enumerate(reversed(bits)):
        v = jnp.where((at // bit) % 2 == 0, v, jnp.flip(v, k))
    order = tuple(reversed(range(len(bits))))
    return v.transpose(order + tuple(range(len(bits), v.ndim))).reshape((n,) + rest)


def part_ids(axis):
    ids = [lax.axis_index(axis)]
    for bit in bits_of(lax.axis_size(axis)):
        ids = ids + [k ^ bit for k in ids]
    return ids


def add(a, b):
    return (a.astype(f32) + b.astype(f32)).astype(bf16)


def pair_steps(gs):
    nw = lax.axis_size("wshard")
    w = lax.axis_index("wshard")
    n = min(g.shape[0] for g in gs) // nw

    def pick(at):
        out = []
        for g in gs:
            v = g.reshape(nw // 2, 2, -1, g.shape[-1])
            v = lax.dynamic_index_in_dim(v, at, 1, keepdims=False)
            k = v.shape[1] // n
            out += [v[:, q * n : (q + 1) * n] for q in range(k)]
        return jnp.concatenate(out, axis=2) if len(out) > 1 else out[0]

    send, keep = pick(1 - w % 2), pick(w % 2)
    dep = yield send
    yield add(keep, swap(after(send, dep), "wshard", 1))


def other_steps(v):
    nw = lax.axis_size("wshard")
    w = lax.axis_index("wshard")
    n = v.shape[1]
    for bit in [1 << k for k in range(1, (nw - 1).bit_length())]:
        at = (w // bit) % 2
        v = v.reshape(-1, 2, n, v.shape[-1]).swapaxes(0, 1)
        send = lax.dynamic_index_in_dim(v, 1 - at, 0, keepdims=False)
        keep = lax.dynamic_index_in_dim(v, at, 0, keepdims=False)
        dep = yield send
        v = add(keep, swap(after(send, dep), "wshard", bit))
    yield v.reshape(n, -1)


def pairs_of(n):
    bits = [1 << k for k in range((n - 1).bit_length())]
    return [bits[k : k + 2] for k in range(0, len(bits), 2)]


def swap_all(parts, axis, bits):
    got = parts[:1]
    for m in range(1, 1 << len(bits)):
        got.append(swap(parts[m], axis, sum(bit for k, bit in enumerate(bits) if (m >> k) & 1)))
    return got


def by_index(got, at, bits):
    for k, bit in enumerate(bits):
        here = (at // bit) % 2 == 1
        got = [jnp.where(here, got[m ^ (1 << k)], got[m]) for m in range(len(got))]
    return got


def seq_steps(v):
    groups = pairs_of(lax.axis_size("seq"))
    s = lax.axis_index("seq")
    single = groups.pop() if len(groups[-1]) == 1 else None
    for bits in groups:
        n = 1 << len(bits)
        at = (s // bits[0]) % n
        v = v.reshape(n, -1, v.shape[-1])
        send = [lax.dynamic_index_in_dim(v, at ^ m, 0, keepdims=False) for m in range(n)]
        dep = yield tuple(send)
        got = swap_all(after(send, dep), "seq", bits)
        v = sum(g.astype(f32) for g in got).astype(bf16)
    if single:
        dep = yield v
        v = add(v, swap(after(v, dep), "seq", single[0]))
    for bits in reversed(groups):
        dep = yield v
        v = after(v, dep)
        got = swap_all([v] * (1 << len(bits)), "seq", bits)
        dep = yield tuple(got[1:])
        v = jnp.concatenate(by_index(after(tuple(got), dep), s, bits), axis=0)
    yield v.astype(f32)


def small_steps(v):
    for axis in ("wshard", "seq"):
        at = lax.axis_index(axis)
        for bits in pairs_of(lax.axis_size(axis)):
            dep = yield v
            v = after(v, dep)
            v = sum(by_index(swap_all([v] * (1 << len(bits)), axis, bits), at, bits))
    yield v


def pack_state(decay, state):
    hi, lo = two(decay)
    return jnp.concatenate([state.astype(bf16), hi, lo], axis=0)


def unpack_state(v, n):
    return v[n : n + 8].astype(f32)[:1] + v[n + 8 : n + 16].astype(f32)[:1], v[:n].astype(f32)


def carried(send, decay, state, sign, tokens):
    n = state.shape[0]
    span = 1
    while span < -(-LONGEST // tokens):
        if span > 1:
            send = pack_state(decay, state)
        dep = yield send
        d, s = unpack_state(shift(after(send, dep), "seq", sign * span), n)
        state = state + decay[:1] * s
        decay = decay * d
        span *= 2
    send = state.astype(bf16)
    dep = yield send
    yield shift(after(send, dep), "seq", sign)


class Steps:
    def __init__(self, gen):
        self.gen = gen
        self.value = next(gen)

    def step(self, dep=None):
        try:
            self.value = self.gen.send(dep)
        except StopIteration:
            pass
        return self.value

    def finish(self):
        for self.value in self.gen:
            pass
        return self.value


def body(inputs, cotangent, lengths, in_proj, out_proj, conv_weight, conv_bias, a_log, d_skip,
         dt_bias, norm_gain, gate_gain):
    t, d = inputs.shape[1:]
    nw = lax.axis_size("wshard")
    di = out_proj.shape[0] * nw
    heads = a_log.shape[0] * nw
    conv = conv_bias.shape[0] * nw
    taps = conv_weight.shape[0]
    n = (conv - di) // 2
    p = di // heads
    docs = lengths.shape[1]
    nt, nc, nb = t // TB, t // CH, TB // CH
    wide = conv + 128
    first = lax.axis_index("seq") * t
    pos = first - 8 + jnp.arange(t + 16, dtype=jnp.int32)
    ends = jnp.cumsum(lengths[0], dtype=jnp.int32)
    seg = jnp.sum((pos[:, None] >= ends[None]).astype(jnp.int32), axis=1)
    seg = jnp.where(pos < 0, -1, seg)
    here = seg[: t + 8]
    own = seg[8 : t + 8]
    entering = jnp.repeat(seg[7 : t + 7 : CH], CH)
    leaving = jnp.repeat(seg[7 + CH : t + 8 : CH], CH)
    zero8 = jnp.zeros((8,), jnp.int32)
    back = [jnp.concatenate([zero8, (seg[8 - k : t + 8 - k] == own).astype(jnp.int32)]) for k in (3, 2, 1)]
    ahead = [(seg[k : t + 8 + k] == here).astype(jnp.int32) for k in (1, 2, 3)]
    cols = [here, jnp.concatenate([zero8, (entering == own).astype(jnp.int32)]),
            jnp.concatenate([zero8, (leaving == own).astype(jnp.int32)])]
    cols = cols + back + [(here < docs).astype(jnp.int32)] + ahead + [jnp.zeros_like(here)] * 6
    tok_all = jnp.stack(cols, axis=1).astype(f32)
    tok, elink = tok_all[8:], tok_all[:8]
    segr = own.astype(f32)[None]
    ids = jnp.stack(part_ids("wshard")).astype(jnp.int32)
    u, cot = inputs[0], cotangent[0]
    ue = shift(u[t - 16 :], "seq", 1)
    wx, wz = in_proj[:, di:], in_proj[:, :di]
    pc = conv // nw
    width = -(-max(pc, di // nw, 384) // 128) * 128


    def line(*vs):
        vs = [v if v.ndim == 2 else v[None] for v in vs]
        vs = [jnp.pad(v, ((0, 0), (0, (width if k == len(vs) - 1 else 128 * (k + 1)) - 128 * k - v.shape[1])))
              for k, v in enumerate(vs)]
        return jnp.concatenate(vs, axis=1)

    small = jnp.concatenate(
        [line(conv_weight), line(conv_bias), line(gate_gain), line(norm_gain), line(a_log, d_skip, dt_bias)], axis=0)
    wx_parts = gather_parts(wx, "wshard")
    small = in_order(gather_parts(after(small, (wx_parts[nw // 2], wz, tok, ids, ue)), "wshard"), "wshard").astype(f32)
    wz_parts = gather_parts(after(wz, wx_parts[-1]), "wshard")
    wo_parts = gather_parts(after(out_proj, wx_parts[-1]), "wshard")
    hw = heads // nw
    cw = small[:, :taps, :pc].swapaxes(0, 1).reshape(taps, conv)
    cb = small[:, taps, :pc].reshape(1, conv)
    gain_gate = small[:, taps + 1, : di // nw].reshape(1, di)
    gain_in = small[:, taps + 2, : d // nw].reshape(1, d)
    log_rate, skip, dtb = [small[:, taps + 3, 128 * k : 128 * k + hw].reshape(1, heads) for k in range(3)]
    rate = -jnp.exp(log_rate)
    pad = ((0, 0), (0, 128 - heads))
    nr = jnp.pad(rate, pad)
    nr2 = nr * LOG2E
    dtb = jnp.pad(dtb, pad)
    dsk = jnp.repeat(skip, p, axis=1)
    e1 = np.arange(128)[:, None] == np.arange(di)[None] // p
    e2 = jnp.asarray(np.concatenate([e1, e1], axis=0), bf16)
    hot = jnp.asarray(np.arange(heads * CH)[:, None] // CH == np.arange(128)[None], bf16)

    outs = [
        (rows(TB, d), (t, d), bf16),
        (rows(TB, conv), (t, conv), bf16),
        (rows(TB, conv), (t, conv), bf16),
        (rows(TB, conv), (t, conv), bf16),
        (rows(TB, di), (t, di), bf16),
        (rows(TB, 256), (t, 256), f32),
        (rows(TB, 128), (t, 128), f32),
        (pl.BlockSpec((32, TB), lambda i, s: (0, i)), (32, t), f32),
        (pl.BlockSpec((nb, n, di), lambda i, s: (i, 0, 0)), (nc, n, di), bf16),
        (pl.BlockSpec((nb, 8, 128), lambda i, s: (i, 0, 0)), (nc, 8, 128), f32),
        (whole((n, di)), (n, di), f32),
        (whole((8, di)), (8, di), f32),
        (whole((n + 16, di)), (n + 16, di), bf16),
        (whole((16, d)), (16, d), bf16),
        (whole((16, conv)), (16, conv), bf16),
    ]
    ins = [rows(TB, d), whole((16, d)), whole((1, d))] + [whole(v.shape) for v in wx_parts]
    ins += [whole((taps, conv)), whole((1, conv)), whole((1, 128)), whole((1, 128)), rows(TB, 16), whole((256, di))]
    scratch = [
        pltpu.VMEM((d, wide), bf16),
        pltpu.VMEM((TB + 8, conv), f32),
        pltpu.VMEM((n, di), f32),
        pltpu.VMEM((1, 128), f32),
        pltpu.VMEM((2 * TB + 8 * nb, di), f32),
    ]
    (nrm, xbc, xc, slope, xd, dts, cc, ct, st, dbf, end, tot, pack, nrme, xbce) = call(
        front_kernel(nw, di, conv, heads), (nt,), ins, outs, scratch, 15,
        [ids, u, ue, gain_in] + wx_parts + [cw, cb, dtb, nr2, tok, e2], "front")
    chain = Steps(carried(pack, tot, end, 1, t))
    chain.step(wz_parts[1])
    chain.step()
    chain.step(wo_parts[1])
    incoming = chain.finish()

    crow = pl.BlockSpec((32, TI), lambda i, s: (0, i))
    srow = pl.BlockSpec((1, TI), lambda i, s: (0, i))
    crow2 = pl.BlockSpec((32, CH), lambda i, s: (0, i))
    srow2 = pl.BlockSpec((1, CH), lambda i, s: (0, i))
    bspec, cspec = rows(TI, n, di // n), rows(TI, n, di // n + 1)
    (yin,) = call(
        inner_kernel(heads, di), (t // TI,),
        [bspec, cspec, rows(TI, di), rows(TI, 128), crow, rows(TI, 16), srow],
        [(rows(TI, di), (t, di), bf16)], [], 10,
        [ids, xc, xc, xd, cc, ct, tok, segr], "inner")

    blk = pl.BlockSpec((nb, n, di), lambda i, s: (i, 0, 0))
    outs = [
        (rows(TB, d), (t, d), bf16),
        (rows(TB, di), (t, di), bf16),
        (rows(TB, di), (t, di), bf16),
        (rows(TB, di), (t, di), bf16),
        (rows(TB, di), (t, di), bf16),
        (rows(TB, d), (t, d), bf16),
        (blk, (nc, n, di), bf16),
        (blk, (nc, n, di), bf16),
        (rows(TB, 128), (t, 128), f32),
        (whole((8, 128)), (8, 128), f32),
        (whole((n, di)), (n, di), f32),
        (whole((n + 16, di)), (n + 16, di), bf16),
    ]
    ins = [rows(TB, d), rows(TB, di), rows(TB, di), rows(TB, n, di // n + 1), rows(TB, 128), rows(TB, 16), blk,
           pl.BlockSpec((nb, 8, 128), lambda i, s: (i, 0, 0)), whole((n, di)), whole((8, di)), rows(TB, d), rows(TB, d)]
    ins += [whole(v.shape) for v in wz_parts + wo_parts]
    ins += [whole((1, di)), whole((1, di)), whole((256, di))]
    scratch = [pltpu.VMEM((d, di), bf16), pltpu.VMEM((di, d), bf16)]
    scratch += [pltpu.VMEM((TB, di), f32)] * 3
    scratch += [pltpu.VMEM((TB + 8 * nb, di), f32), pltpu.VMEM((TB, di), bf16), pltpu.VMEM((8, di), f32)]
    (mixed, gn, dz, dy, edy, e, sf, dcs, rin, g_skip, reach, reach_pack) = call(
        gate_kernel(nw, di, d), (nt,), ins, outs, scratch, 25,
        [ids, nrm, yin, xc, xc, cc, tok, st, dbf, incoming, tot, u, cot] + wz_parts + wo_parts + [gain_gate, dsk, e2], "gate")
    tn = (((0,), (0,)), ((), ()))

    def outer(a, b):
        return lax.dot_general(a, b, tn, preferred_element_type=f32)

    back_state = Steps(carried(reach_pack, tot, reach, -1, t))
    s1 = back_state.value
    gw_out = outer(after(gn, s1), e).astype(bf16)
    gw_z = outer(nrm, after(dz, s1)).astype(bf16)
    s2 = back_state.step()
    oz_p = Steps(pair_steps([gw_out, gw_z]))
    oz_w = Steps(other_steps(oz_p.step(s2)))
    oz2 = oz_w.value
    hh, hw2 = heads // 2, di // 2

    def at(shape, col):
        return pl.BlockSpec(shape, lambda i, s: (0, col))

    def half_inner(k, dep):
        outs = [
            (rows(CH, hw2), (t, hw2), bf16),
            (rows(CH, n), (t, n), f32),
            (rows(CH, n), (t, n), f32),
            (rows(CH, 128), (t, 128), f32),
        ]
        return call(
            inner_back_kernel(p, hh * k, hh * (k + 1)), (t // CH,),
            [rows(CH, n, di // n), rows(CH, n, di // n + 1), rows(CH, hw2, k), rows(CH, hw2, k), rows(CH, 128), crow2,
             pl.BlockSpec((hh * CH, 128), lambda i, s: (k, 0)), rows(CH, 16), srow2],
            outs, [pltpu.VMEM((128, CH), f32)], 12,
            [ids, xc, xc, xd, after(dy, dep), cc, ct, hot, tok, segr], "inner_back")

    def rev(block, width, col=0):
        return pl.BlockSpec((block, width), lambda i, s: (nt - 1 - i, col))

    def half_back(k, inner, dep, gend, extra):
        gxd, dbi, dci, rk = inner
        last = k == 1
        cols = hw2 + 2 * n if last else hw2
        rblk = pl.BlockSpec((nb, n, hw2), lambda i, s: (nt - 1 - i, 0, k))
        ins = [rev(TB, hw2, k), rev(TB, n, di // n), rev(TB, hw2, k), rev(TB, hw2, k), at((16, hw2), k),
               rev(TB, hw2, k), rev(TB, 256), rev(TB, 128), rev(TB, 16), whole((8, 16)), rev(TB, hw2),
               rev(TB, n), rev(TB, n), rev(TB, 128), rev(TB, 128), rev(TB, hw2, k), rev(TB, hw2, k), rblk, rblk,
               at((n, hw2), k), at((taps, hw2), k), at((1, hw2), k), whole((1, 128)), at((256, hw2), k)]
        args = [ids, xc, xc, slope, xbc, xbce, xd, dts, cc, tok, elink, after(gxd, dep), dbi, dci, rk, rin, dy,
                edy, sf, dcs, gend, cw, dsk, nr, e2]
        outs = [
            (rev(TB, cols + 128 * last), (t, cols + 128 * last), bf16),
            (whole((16, cols)), (16, cols), bf16),
            (whole((8, cols)), (8, cols), f32),
        ]
        if last:
            ins += [rev(TB, 2 * n, di // (2 * n)), rev(TB, 2 * n, di // (2 * n)), at((16, 2 * n), di // (2 * n)),
                    at((taps, 2 * n), di // (2 * n)), rev(TB, n), rev(TB, n), rev(TB, 128), whole((8, 128))]
            args += [slope, xbc, xbce, cw] + list(extra)
        else:
            outs += [(rev(TB, n), (t, n), f32), (rev(TB, n), (t, n), f32), (rev(TB, 128), (t, 128), f32)]
        scratch = [
            pltpu.VMEM((n, hw2), f32),
            pltpu.VMEM((2 * TB + 8 * nb, hw2), f32),
            pltpu.VMEM((TB, hw2), f32),
            pltpu.VMEM((TB + 8, cols), f32),
            pltpu.VMEM((TB, hw2), bf16),
            pltpu.VMEM((TB, hw2), bf16),
            pltpu.VMEM((8 * taps, cols), f32),
            pltpu.VMEM((8, cols), f32),
            pltpu.VMEM((8, 128), f32),
            pltpu.VMEM((8, 128), f32),
        ]
        return call(back_kernel(hw2, n, hh * k, hh * (k + 1), last), (nt,), ins, outs, scratch, 15, args, "back")

    in_a = half_inner(0, (s2, oz2))
    s3 = back_state.step(oz2)
    s3, in_a0 = lax.optimization_barrier((s3, in_a[0]))
    in_b = half_inner(1, (s3, in_a0))
    back_state.step(in_a[0])
    gend = back_state.finish()
    oz_w.step()
    oz_s = Steps(seq_steps(oz_w.finish()))
    oz3 = oz_s.value
    (gpa, edge_a, sum_a, dbp, dcp, ddtp) = half_back(0, in_a, (in_b[0], oz3), gend, None)
    oz4 = oz_s.step(in_b[0])
    gw_xa = (outer(nrm, after(gpa, oz4)) + outer(nrme, edge_a)).astype(bf16)
    xa_p = Steps(pair_steps([gw_xa]))
    xa1 = xa_p.value
    (gpb, edge_b, sum_b) = half_back(1, in_b, (oz4, xa1), gend, (dbp, dcp, ddtp, g_skip))
    oz5 = oz_s.step(gpa)
    oz5, gpb_late = lax.optimization_barrier((oz5, gpb))
    gw_xb = outer(nrm, gpb_late)
    cb2 = conv - hw2
    gw_xb = jnp.concatenate(
        [gw_xb[:, :cb2] + outer(nrme, edge_b), gw_xb[:, cb2 : cb2 + heads]], axis=1).astype(bf16)
    xb_p = Steps(pair_steps([gw_xb]))
    x_w = Steps(other_steps(jnp.concatenate([xa_p.step(), xb_p.step()], axis=2)))
    x2 = x_w.value
    ea_in, eb_in = shift(edge_a, "seq", -1), shift(edge_b, "seq", -1)
    oz7 = oz_s.step((x2, ea_in))

    ins = [rows(TB, di), rows(TB, hw2), rows(TB, wide - hw2), whole((16, hw2)), whole((16, cb2)), rows(TB, d), rows(TB, d)]
    ins += [whole(v.shape) for v in wz_parts + wx_parts] + [whole((1, d))]
    outs = [(rows(TB, d), (t, d), bf16)]
    (grad_input,) = call(
        input_kernel(nw, di, conv, heads), (nt,), ins, outs,
        [pltpu.VMEM((d, di), bf16), pltpu.VMEM((d, wide), bf16), pltpu.VMEM((TB, d), f32)], 12,
        [ids, dz, after(gpa, x2), gpb, ea_in, eb_in, u, e] + wz_parts + wx_parts + [gain_in], "input")
    sums = Steps(small_steps(jnp.concatenate([sum_a, sum_b], axis=1)))
    x_s = Steps(seq_steps(x_w.finish()))
    x3 = x_s.value
    sums.step((x3, grad_input))
    x4 = x_s.step((grad_input, oz7))
    sums.step(x4)
    oz_s.step(x4)
    x5 = x_s.step()
    sums.step(x5)
    r_x, r_oz, total = x_s.finish(), oz_s.finish(), sums.finish()
    k = r_oz.shape[1] - di
    r_out = jnp.concatenate([r_oz[:, q * d : (q + 1) * d] for q in range(k // d)], axis=0)
    r_z = r_oz[:, k:]
    w = lax.axis_index("wshard")

    def mine(v):
        width = v.shape[-1] // nw
        return lax.dynamic_slice_in_dim(v, w * width, width, axis=v.ndim - 1)

    by_head = total[5:8, :heads] + total[5:8, hw2 : hw2 + heads]
    by_head = mine(by_head * jnp.concatenate([rate, jnp.ones((2, heads), f32)], axis=0))
    res = [mine(total[:taps]), mine(total[taps]), by_head[0], by_head[2], by_head[1]]
    res.append((jnp.sum(r_z * wz.astype(f32), axis=1) + jnp.sum(r_x * wx.astype(f32), axis=1)) / norm_gain.astype(f32))
    res.append(jnp.sum(r_out * out_proj.astype(f32), axis=1) / gate_gain.astype(f32))
    return (mixed[None], grad_input[None], jnp.concatenate([r_z, r_x], axis=1), r_out) + tuple(res)


def solution(mesh):
    wide = P("wshard", "seq", None)
    mat = P("wshard", None)
    taps = P(None, "wshard")
    vec = P("wshard")
    return jax.shard_map(
        body,
        mesh=mesh,
        in_specs=(wide, wide, mat, mat, mat, taps) + (vec,) * 6,
        out_specs=(wide, wide, mat, mat, taps) + (vec,) * 6,
        check_vma=False,
    )
```

```python
import jax
import jax.numpy as jnp
import numpy as np
from jax import lax
from jax.experimental import pallas as pl
from jax.experimental.pallas import tpu as pltpu
from jax.sharding import PartitionSpec as P

f32 = jnp.float32
bf16 = jnp.bfloat16
EPS = 1e-05
LOG2E = 1.4426950408889634
CH = 128
TB = 256
TI = 256
LONGEST = 4096
HIGH = lax.Precision.HIGHEST
MB = 1024 * 1024
VMEM = 53 * MB


def sigmoid(v):
    return 0.5 * jnp.tanh(0.5 * v) + 0.5


def dot(a, b):
    return jnp.dot(a, b, preferred_element_type=f32)


def dot_nt(a, b):
    return lax.dot_general(a, b, (((1,), (1,)), ((), ())), preferred_element_type=f32)


def two(v):
    hi = v.astype(bf16)
    return hi, (v - hi.astype(f32)).astype(bf16)


def spread(v, e2):
    return dot(jnp.concatenate(two(v), axis=1), e2)


def head_sums(row, e2):
    hi, lo = two(jnp.broadcast_to(row, (8, row.shape[1])))
    return dot_nt(hi, e2[0:128, :]) + dot_nt(lo, e2[0:128, :])


def cost(us):
    return pl.CostEstimate(flops=int(us * 1.1e9), bytes_accessed=1 << 20, transcendentals=0)


def call(kernel, grid, ins, outs, scratch, us, args, name):
    return pl.pallas_call(
        kernel,
        grid_spec=pltpu.PrefetchScalarGridSpec(
            num_scalar_prefetch=1,
            grid=grid,
            in_specs=ins,
            out_specs=[o[0] for o in outs],
            scratch_shapes=scratch,
        ),
        out_shape=[jax.ShapeDtypeStruct(o[1], o[2]) for o in outs],
        compiler_params=pltpu.CompilerParams(
            vmem_limit_bytes=VMEM, dimension_semantics=("arbitrary",)
        ),
        cost_estimate=cost(us),
        name=name,
    )(*args)


def rows(block, cols, col=0):
    return pl.BlockSpec((block, cols), lambda i, s: (i, col))


def whole(shape):
    return pl.BlockSpec(shape, lambda i, s: (0,) * len(shape))


def norm_rows(uf, gain):
    scale = lax.rsqrt(jnp.mean(uf * uf, axis=-1, keepdims=True) + EPS)
    return (uf * scale * gain).astype(bf16)


def place(buf, ids, parts, width):
    for j, part in enumerate(parts):
        n = part.shape[0]
        at = pl.multiple_of(ids[j] * n, 64)
        buf[pl.ds(at, n), :width] = part[...]


def put_pack(ref, decay, state):
    n = state.shape[0]
    hi, lo = two(decay)
    ref[0:n, :] = state.astype(bf16)
    ref[n:, :] = jnp.concatenate([hi.astype(f32), lo.astype(f32)], axis=0).astype(bf16)


def front_kernel(np_, di, conv, heads):
    def kernel(ids, u, ue, gain, *rest):
        parts = rest[:np_]
        (cw, cb, dtb, nr, tok, e2, nrm_o, xbc_o, xc_o, slope_o, xd_o, dts_o, cc_o, ct_o,
         st_o, db_o, end_o, tot_o, pk_o, nrme_o, xbce_o, wbuf, ext, state, kd, sp) = rest[np_:]
        i = pl.program_id(0)
        n = (conv - di) // 2

        @pl.when(i == 0)
        def _():
            wbuf[:, conv:] = jnp.zeros((wbuf.shape[0], wbuf.shape[1] - conv), bf16)
            place(wbuf, ids, parts, conv + heads)
            nrme = norm_rows(ue[...].astype(f32), gain[...])
            nrme_o[...] = nrme
            pe = dot(nrme, wbuf[:, :conv]).astype(bf16)
            xbce_o[...] = pe
            ext[0:8, :] = pe.astype(f32)[8:16]
            state[...] = jnp.zeros_like(state)
            kd[...] = jnp.ones_like(kd)

        nrm = norm_rows(u[...].astype(f32), gain[...])
        nrm_o[...] = nrm
        pd = dot(nrm, wbuf[:, conv:])
        for c0 in range(0, conv, 256):
            px = dot(nrm, wbuf[:, c0 : c0 + 256]).astype(bf16)
            xbc_o[:, c0 : c0 + 256] = px
            ext[8 : 8 + TB, c0 : c0 + 256] = px.astype(f32)
        sh = pd + dtb[...]
        dt = jnp.maximum(sh, 0.0) + jnp.log1p(jnp.exp(-jnp.abs(sh)))
        dts_o[:, :128] = dt
        dts_o[:, 128:] = jax.nn.sigmoid(sh)
        a2 = dt * nr[...]
        ri = lax.broadcasted_iota(jnp.int32, (CH, CH), 0)
        ci = lax.broadcasted_iota(jnp.int32, (CH, CH), 1)
        low = (ri >= ci).astype(f32)
        pieces = [dt]
        leaves = []
        for k in range(TB // CH):
            r = slice(k * CH, (k + 1) * CH)
            c2 = jnp.dot(low, a2[r], precision=HIGH, preferred_element_type=f32)
            cc_o[r, :] = c2
            ct_o[:, r] = c2.T[: ct_o.shape[0], :]
            pieces.append(jnp.exp2(c2[CH - 1 :] - c2) * tok[r, 2:3])
            leaves.append(jnp.exp2(c2[CH - 1 :]) * tok[(k + 1) * CH - 1 : (k + 1) * CH, 1:2])
        lv = jnp.concatenate([jnp.broadcast_to(v, (8, 128)) for v in leaves], axis=0)
        sp[...] = spread(jnp.concatenate(pieces + [lv], axis=0), e2[...])
        for r0 in range(0, TB, 64):
            l0, l1, l2 = tok[r0 : r0 + 64, 3:4], tok[r0 : r0 + 64, 4:5], tok[r0 : r0 + 64, 5:6]
            for c0 in range(0, conv, 256):
                c = slice(c0, c0 + 256)
                pre = cb[:, c] + cw[3:4, c] * ext[8 + r0 : 72 + r0, c]
                pre = pre + cw[2:3, c] * (ext[7 + r0 : 71 + r0, c] * l2)
                pre = pre + cw[1:2, c] * (ext[6 + r0 : 70 + r0, c] * l1)
                pre = pre + cw[0:1, c] * (ext[5 + r0 : 69 + r0, c] * l0)
                sg = sigmoid(pre)
                xc = pre * sg
                xc_o[r0 : r0 + 64, c] = xc.astype(bf16)
                slope_o[r0 : r0 + 64, c] = (sg + xc * (1.0 - sg)).astype(bf16)
                if c0 < di:
                    xd_o[r0 : r0 + 64, c] = (xc * sp[r0 : r0 + 64, c]).astype(bf16)
        ext[0:8, :] = ext[TB : TB + 8, :]
        for k in range(TB // CH):
            r = slice(k * CH, (k + 1) * CH)
            st_o[k] = state[...].astype(bf16)
            db_o[k] = jnp.broadcast_to(kd[...], (8, 128))
            bt = xc_o[r, di : di + n].astype(f32).T.astype(bf16)
            for c0 in range(0, di, 256):
                c = slice(c0, c0 + 256)
                xw = (xd_o[r, c].astype(f32) * sp[TB + k * CH : TB + (k + 1) * CH, c]).astype(bf16)
                lvr = sp[2 * TB + 8 * k : 2 * TB + 8 * k + 1, c]
                state[:, c] = lvr * state[:, c] + dot(bt, xw)
            kd[...] = kd[...] * leaves[k]

        @pl.when(i == pl.num_programs(0) - 1)
        def _():
            end_o[...] = state[...]
            total = spread(jnp.broadcast_to(kd[...], (8, 128)), e2[...])
            tot_o[...] = total
            put_pack(pk_o, total, state[...])

    return kernel


def inner_kernel(heads, di):
    p = di // heads
    per = 128 // p

    def kernel(ids, b, c, xd, cc, ct, tok, segr, y_o):
        ri = lax.broadcasted_iota(jnp.int32, (CH, CH), 0)
        ci = lax.broadcasted_iota(jnp.int32, (CH, CH), 1)
        lanes = lax.broadcasted_iota(jnp.int32, (1, 128), 1) // p
        for k in range(b.shape[0] // CH):
            r = slice(k * CH, (k + 1) * CH)
            s = dot_nt(c[r, :], b[r, :])
            bias = jnp.where((tok[r, 0:1] == segr[:, r]) & (ri >= ci), 0.0, -1e30)
            for j in range(heads // per):
                xp = xd[r, 128 * j : 128 * j + 128]
                ms, xs = [], []
                for q in range(per):
                    h = per * j + q
                    e = jnp.exp2(cc[r, h : h + 1] - ct[h : h + 1, r] + bias)
                    ms.append((s * e).astype(bf16))
                    xs.append(xp * (lanes == q).astype(f32).astype(bf16))
                out = dot(jnp.concatenate(ms, axis=1), jnp.concatenate(xs, axis=0))
                y_o[r, 128 * j : 128 * j + 128] = out.astype(bf16)

    return kernel


def gate_kernel(np_, di, d):
    def kernel(ids, nrm, yin, x, c_in, cc, tok, st, db, inc, tot, u, cot, *rest):
        wz, wo = rest[:np_], rest[np_ : 2 * np_]
        (gain, dsk, e2, mixed_o, gn_o, dz_o, dy_o, edy_o, e_o, sf_o, dc_o, rin_o, gs_o,
         rg_o, pk_o, zbuf, obuf, z, yi, dgn, ee, pr, gs) = rest[2 * np_ :]
        i = pl.program_id(0)

        @pl.when(i == 0)
        def _():
            place(zbuf, ids, wz, di)
            place(obuf, ids, wo, d)
            gs[...] = jnp.zeros_like(gs)
            rg_o[...] = jnp.zeros_like(rg_o)

        keep = tok[:, 6:7]
        ef = cot[...].astype(f32) * keep
        e = ef.astype(bf16)
        e_o[...] = e
        nb = TB // CH
        ents = []
        for k in range(nb):
            r = slice(k * CH, (k + 1) * CH)
            ents.append(jnp.exp2(cc[r, :]) * tok[r, 1:2])
        ee[...] = spread(jnp.concatenate(ents + [db[k] for k in range(nb)], axis=0), e2[...])
        for k in range(nb):
            r = slice(k * CH, (k + 1) * CH)
            for c0 in range(0, di, 256):
                c = slice(c0, c0 + 256)
                dbr = ee[TB + 8 * k : TB + 8 * k + 1, c]
                sf = (st[k, :, c].astype(f32) + dbr * inc[:, c].astype(f32)).astype(bf16)
                sf_o[k, :, c] = sf
                yi[r, c] = dot(c_in[r, :], sf)
        z[...] = dot(nrm[...], zbuf[...])
        dgn[...] = dot_nt(e, obuf[...])

        def strip(r):
            xs = x[r, :].astype(f32)
            eyi = ee[r, :] * yi[r, :]
            y = yin[r, :].astype(f32) + eyi + dsk[...] * xs
            zz = z[r, :]
            sg = sigmoid(zz)
            act = zz * sg
            g = y * act
            scale = lax.rsqrt(jnp.mean(g * g, axis=-1, keepdims=True) + EPS)
            ug = g * scale
            gn_o[r, :] = (ug * gain[...]).astype(bf16)
            dg0 = dgn[r, :]
            dn = dg0 * gain[...]
            m = jnp.mean(dn * ug, axis=-1, keepdims=True)
            dg = scale * (dn - ug * m)
            dy = dg * act
            dz_o[r, :] = (dg * y * (sg + act * (1.0 - sg))).astype(bf16)
            dy_o[r, :] = dy.astype(bf16)
            ps = xs * dy
            gs[...] += ps[0:8] + ps[8:16]
            edy_o[r, :] = (dy * ee[r, :]).astype(bf16)
            pr[r, :] = (dy * eyi).astype(bf16)

        for t in range(TB // 16):
            strip(slice(t * 16, t * 16 + 16))
        rin_o[...] = dot_nt(pr[...], e2[0:128, :])
        mixed_o[...] = (keep * (u[...].astype(f32) + dot(gn_o[...], obuf[...]))).astype(bf16)
        for k in range(nb):
            r = slice(k * CH, (k + 1) * CH)
            ctr = c_in[r, :].astype(f32).T.astype(bf16)
            for c0 in range(0, di, 256):
                c = slice(c0, c0 + 256)
                dcv = dot(ctr, edy_o[r, c])
                dc_o[k, :, c] = dcv.astype(bf16)
                rg_o[:, c] += ee[TB + 8 * k : TB + 8 * k + 1, c] * dcv

        @pl.when(i == pl.num_programs(0) - 1)
        def _():
            gs_o[...] = head_sums(jnp.sum(gs[...], axis=0, keepdims=True), e2)
            put_pack(pk_o, tot[...], rg_o[...])

    return kernel


def inner_back_kernel(p, h0, h1):
    per = 128 // p

    def kernel(ids, b, c, xd, dy, cc, ct, hot, tok, segr, gxd_o, db_o, dc_o, rk_o, rr):
        si = lax.broadcasted_iota(jnp.int32, (CH, CH), 0)
        ti = lax.broadcasted_iota(jnp.int32, (CH, CH), 1)
        lanes = lax.broadcasted_iota(jnp.int32, (1, 128), 1) // p
        rr[...] = jnp.zeros_like(rr)
        for k in range(b.shape[0] // CH):
            r = slice(k * CH, (k + 1) * CH)
            st = dot_nt(b[r, :], c[r, :])
            bias = jnp.where((tok[r, 0:1] == segr[:, r]) & (ti >= si), 0.0, -1e30)
            gsum = jnp.zeros((CH, CH), f32)
            ksum = jnp.zeros((CH, 128), f32)
            for j in range((h1 - h0) // per):
                xp = xd[r, 128 * j : 128 * j + 128]
                dyp = dy[r, 128 * j : 128 * j + 128]
                dys = jnp.concatenate(
                    [dyp * (lanes == q).astype(f32).astype(bf16) for q in range(per)], axis=0
                )
                gm = dot_nt(xp, dys)
                ms, exs = [], []
                for q in range(per):
                    h = h0 + per * j + q
                    e = jnp.exp2(ct[h : h + 1, r] - cc[r, h : h + 1] + bias)
                    ms.append((st * e).astype(bf16))
                    ge = gm[:, q * CH : (q + 1) * CH] * e
                    gsum = gsum + ge
                    ex = (ge * st).astype(bf16)
                    exs.append(ex)
                    rr[h : h + 1, r] = jnp.sum(ex.astype(f32), axis=0, keepdims=True)
                ksum = ksum + dot(jnp.concatenate(exs, axis=1), hot[per * CH * j : per * CH * (j + 1), :])
                out = dot(jnp.concatenate(ms, axis=1), dys)
                gxd_o[r, 128 * j : 128 * j + 128] = out.astype(bf16)
            rk_o[r, :] = rr[:, r].T - ksum
            db_o[r, :] = dot(gsum.astype(bf16), c[r, :])
            dc_o[r, :] = dot(gsum.T.astype(bf16), b[r, :])

    return kernel


def back_kernel(w, n, h0, h1, last_part):
    cols = w + 2 * n if last_part else w

    def kernel(ids, x_in, b_in, slope, xbc, xbce, xd, dts, cc, tok, elink, gxd, dbi, dci, rk, rin,
               dy, edy, sf, dcs, gend, cw, dsk, nr, e2, *rest):
        if last_part:
            slope2, xbc2, xbce2, cw2, dbp, dcp, ddtp, gsk = rest[:8]
            gp_o, edge_o, sum_o = rest[8:11]
        else:
            gp_o, edge_o, sum_o, dbp_o, dcp_o, ddtp_o = rest[:6]
        ds, sp, sr, ext, xq, xe, gw_o, gb_o, ga_o, gdt_o = rest[-10:]
        i = pl.program_id(0)
        nb = TB // CH

        def pick(a, a2, r, c0):
            return a[r, c0 : c0 + 256] if c0 < w else a2[r, c0 - w : c0 - w + 256]

        @pl.when(i == 0)
        def _():
            ds[...] = gend[...].astype(f32)
            ext[TB : TB + 8, :] = jnp.zeros((8, cols), f32)
            gw_o[...] = jnp.zeros_like(gw_o)
            gb_o[...] = jnp.zeros_like(gb_o)
            ga_o[...] = jnp.zeros_like(ga_o)
            gdt_o[...] = jnp.zeros_like(gdt_o)

        if not last_part:
            slope2 = xbc2 = xbce2 = cw2 = None
        dt = dts[:, :128]
        pieces, leaves = [dt], []
        for k in range(nb):
            r = slice(k * CH, (k + 1) * CH)
            c2 = cc[r, :]
            pieces.append(jnp.exp2(c2[CH - 1 :] - c2) * tok[r, 2:3])
            leaves.append(jnp.exp2(c2[CH - 1 :]) * tok[(k + 1) * CH - 1 : (k + 1) * CH, 1:2])
        lv = jnp.concatenate([jnp.broadcast_to(v, (8, 128)) for v in leaves], axis=0)
        sp[...] = spread(jnp.concatenate(pieces + [lv], axis=0), e2[...])
        lsum = [None] * nb
        for k in reversed(range(nb)):
            r = slice(k * CH, (k + 1) * CH)
            lacc = []
            gb = dbi[r, :]
            gc = dci[r, :]
            for c0 in range(0, w, 256):
                c = slice(c0, c0 + 256)
                dsv = ds[:, c]
                dsb = dsv.astype(bf16)
                sfv = sf[k, :, c]
                sr[r, c] = dot(b_in[r, :], dsb)
                xwv = (xd[r, c].astype(f32) * sp[TB + k * CH : TB + (k + 1) * CH, c]).astype(bf16)
                gb = gb + dot_nt(xwv, dsb)
                gc = gc + dot_nt(edy[r, c], sfv)
                lacc.append(jnp.sum(dsv * sfv.astype(f32), axis=0, keepdims=True))
                lvr = sp[2 * TB + 8 * k : 2 * TB + 8 * k + 1, c]
                ds[:, c] = lvr * dsv + dcs[k, :, c].astype(f32)
            lsum[k] = head_sums(jnp.concatenate(lacc, axis=1), e2)[0:1]
            if last_part:
                ext[r, w : w + n] = (gb + dbp[r, :]) * slope2[r, :n].astype(f32)
                ext[r, w + n :] = (gc + dcp[r, :]) * slope2[r, n:].astype(f32)
            else:
                dbp_o[r, :] = gb
                dcp_o[r, :] = gc

        def strip(r, re):
            x = x_in[r, :].astype(f32)
            es = sp[re, :] * sr[r, :]
            q = gxd[r, :].astype(f32) + es
            gx = sp[r, :] * q + dsk[...] * dy[r, :].astype(f32)
            ext[r, 0:w] = gx * slope[r, :].astype(f32)
            xq[r, :] = (x * q).astype(bf16)
            xe[r, :] = (x * es).astype(bf16)

        for t in range(TB // 16):
            strip(slice(t * 16, t * 16 + 16), slice(TB + t * 16, TB + t * 16 + 16))
        gdt = dot_nt(xq[...], e2[0:128, :])
        et = dot_nt(xe[...], e2[0:128, :]) * dt
        ri = lax.broadcasted_iota(jnp.int32, (CH, CH), 0)
        ci = lax.broadcasted_iota(jnp.int32, (CH, CH), 1)
        hl = lax.broadcasted_iota(jnp.int32, (1, 128), 1)
        hm = ((hl >= h0) & (hl < h1)).astype(f32)
        tri = jnp.concatenate([(ci >= ri).astype(f32), (ci < ri).astype(f32)], axis=1)
        for k in range(nb):
            r = slice(k * CH, (k + 1) * CH)
            v = jnp.concatenate([rk[r, :] + rin[r, :] * hm, et[r]], axis=0)
            ga = jnp.dot(tri, v, precision=HIGH, preferred_element_type=f32) + lsum[k] * leaves[k]
            ddt = (gdt[r] + ga * nr[...]) * dts[r, 128:]
            gad = ga * dts[r, :128]
            acc_a, acc_d = gad[0:8], ddt[0:8]
            for q in range(8, CH, 8):
                acc_a = acc_a + gad[q : q + 8]
                acc_d = acc_d + ddt[q : q + 8]
            ga_o[...] += acc_a
            gdt_o[...] += acc_d
            if last_part:
                gp_o[r, cols:] = (ddt + ddtp[r, :]).astype(bf16)
            else:
                ddtp_o[r, :] = ddt
        for r0 in range(0, TB, 64):
            rs = slice(r0, r0 + 64)
            links = [jnp.broadcast_to(tok[rs, 6 + s : 7 + s], (64, 256)) for s in (1, 2, 3)]
            for c0 in range(0, cols, 256):
                c = slice(c0, c0 + 256)
                g0 = ext[rs, c]
                xb = pick(xbc, xbc2, rs, c0).astype(f32)
                gsum = pick(cw, cw2, slice(3, 4), c0) * g0
                ws = [None, None, None, g0 * xb]
                for s in (1, 2, 3):
                    gs = ext[r0 + s : r0 + s + 64, c] * links[s - 1]
                    gsum = gsum + pick(cw, cw2, slice(3 - s, 4 - s), c0) * gs
                    ws[3 - s] = gs * xb
                gp_o[rs, c] = gsum.astype(bf16)
                gb = g0[0:8]
                for q in range(8, 64, 8):
                    gb = gb + g0[q : q + 8]
                gb_o[:, c] += gb
                for o in range(4):
                    v = ws[o][0:8]
                    for q in range(8, 64, 8):
                        v = v + ws[o][q : q + 8]
                    gw_o[8 * o : 8 * o + 8, c] += v
        ext[TB : TB + 8, :] = ext[0:8, :]

        @pl.when(i == pl.num_programs(0) - 1)
        def _():
            zero = jnp.zeros((8, 256), f32)
            for c0 in range(0, cols, 256):
                c = slice(c0, c0 + 256)
                xb = pick(xbce, xbce2, slice(8, 16), c0).astype(f32)
                ext[8:16, c] = ext[TB : TB + 8, c]
                ext[0:8, c] = zero
                gsum = zero
                for s in (1, 2, 3):
                    gs = ext[s : s + 8, c] * elink[:, 6 + s : 7 + s]
                    gsum = gsum + pick(cw, cw2, slice(3 - s, 4 - s), c0) * gs
                    gw_o[8 * (3 - s) : 8 * (3 - s) + 8, c] += gs * xb
                edge_o[:, c] = jnp.concatenate([zero, gsum], axis=0).astype(bf16)
                sums = [jnp.sum(gw_o[8 * o : 8 * o + 8, c], axis=0, keepdims=True) for o in range(4)]
                sums.append(jnp.sum(gb_o[:, c], axis=0, keepdims=True))
                sum_o[:, c] = jnp.concatenate(sums + [zero[0:3]], axis=0)
            sum_o[5:6, 0:128] = jnp.sum(ga_o[...], axis=0, keepdims=True)
            sum_o[6:7, 0:128] = jnp.sum(gdt_o[...], axis=0, keepdims=True)
            if last_part:
                sum_o[7:8, 0:128] = gsk[0:1, :]

    return kernel


def input_kernel(np_, di, conv, heads):
    def kernel(ids, gpz, gpa, gpb, edge, u, e, *rest):
        wz, wx = rest[:np_], rest[np_ : 2 * np_]
        gain, gi_o, zbuf, xbuf, gn = rest[2 * np_ :]
        i = pl.program_id(0)

        @pl.when(i == 0)
        def _():
            xbuf[:, conv:] = jnp.zeros((xbuf.shape[0], xbuf.shape[1] - conv), bf16)
            place(zbuf, ids, wz, di)
            place(xbuf, ids, wx, conv + heads)

        wa = gpa.shape[1]
        wd = u.shape[1]
        last = (i == pl.num_programs(0) - 1).astype(f32)
        for c0 in range(0, wd, 256):
            c = slice(c0, c0 + 256)
            g = dot_nt(gpz[...], zbuf[c, :]) + dot_nt(gpa[...], xbuf[c, :wa]) + dot_nt(gpb[...], xbuf[c, wa:])
            tail = dot_nt(edge[...], xbuf[c, :conv]) * last
            gn[: TB - 16, c] = g[: TB - 16]
            gn[TB - 16 :, c] = g[TB - 16 :] + tail
        for r0 in range(0, TB, 16):
            r = slice(r0, r0 + 16)
            uf = u[r, :].astype(f32)
            scale = lax.rsqrt(jnp.mean(uf * uf, axis=-1, keepdims=True) + EPS)
            unit = uf * scale
            dn = gn[r, :] * gain[...]
            m = jnp.mean(dn * unit, axis=-1, keepdims=True)
            gi_o[r, :] = (e[r, :].astype(f32) + scale * (dn - unit * m)).astype(bf16)

    return kernel


def swap(v, axis, bit):
    return lax.ppermute(v, axis, [(k, k ^ bit) for k in range(lax.axis_size(axis))])


def shift(v, axis, steps):
    n = lax.axis_size(axis)
    return lax.ppermute(v, axis, [(k, k + steps) for k in range(n) if 0 <= k + steps < n])


def bits_of(n):
    return [1 << k for k in reversed(range((n - 1).bit_length()))]


def after(v, dep):
    if dep is None:
        return v
    return lax.optimization_barrier((v, dep))[0]


def gather_parts(v, axis):
    parts = [v]
    for bit in bits_of(lax.axis_size(axis)):
        parts = parts + [swap(p, axis, bit) for p in parts]
    return parts


def in_order(parts, axis):
    at = lax.axis_index(axis)
    n = lax.axis_size(axis)
    v = jnp.stack(parts)
    rest = v.shape[1:]
    bits = bits_of(n)
    v = v.reshape((2,) * len(bits) + rest)
    for k, bit in enumerate(reversed(bits)):
        v = jnp.where((at // bit) % 2 == 0, v, jnp.flip(v, k))
    order = tuple(reversed(range(len(bits))))
    return v.transpose(order + tuple(range(len(bits), v.ndim))).reshape((n,) + rest)


def part_ids(axis):
    ids = [lax.axis_index(axis)]
    for bit in bits_of(lax.axis_size(axis)):
        ids = ids + [k ^ bit for k in ids]
    return ids


def add(a, b):
    return (a.astype(f32) + b.astype(f32)).astype(bf16)


def pair_steps(gs):
    nw = lax.axis_size("wshard")
    w = lax.axis_index("wshard")
    n = min(g.shape[0] for g in gs) // nw

    def pick(at):
        out = []
        for g in gs:
            v = g.reshape(nw // 2, 2, -1, g.shape[-1])
            v = lax.dynamic_index_in_dim(v, at, 1, keepdims=False)
            k = v.shape[1] // n
            out += [v[:, q * n : (q + 1) * n] for q in range(k)]
        return jnp.concatenate(out, axis=2) if len(out) > 1 else out[0]

    send, keep = pick(1 - w % 2), pick(w % 2)
    dep = yield send
    yield add(keep, swap(after(send, dep), "wshard", 1))


def other_steps(v):
    nw = lax.axis_size("wshard")
    w = lax.axis_index("wshard")
    n = v.shape[1]
    for bit in [1 << k for k in range(1, (nw - 1).bit_length())]:
        at = (w // bit) % 2
        v = v.reshape(-1, 2, n, v.shape[-1]).swapaxes(0, 1)
        send = lax.dynamic_index_in_dim(v, 1 - at, 0, keepdims=False)
        keep = lax.dynamic_index_in_dim(v, at, 0, keepdims=False)
        dep = yield send
        v = add(keep, swap(after(send, dep), "wshard", bit))
    yield v.reshape(n, -1)


def pairs_of(n):
    bits = [1 << k for k in range((n - 1).bit_length())]
    return [bits[k : k + 2] for k in range(0, len(bits), 2)]


def swap_all(parts, axis, bits):
    got = parts[:1]
    for m in range(1, 1 << len(bits)):
        got.append(swap(parts[m], axis, sum(bit for k, bit in enumerate(bits) if (m >> k) & 1)))
    return got


def by_index(got, at, bits):
    for k, bit in enumerate(bits):
        here = (at // bit) % 2 == 1
        got = [jnp.where(here, got[m ^ (1 << k)], got[m]) for m in range(len(got))]
    return got


def seq_steps(v):
    groups = pairs_of(lax.axis_size("seq"))
    s = lax.axis_index("seq")
    single = groups.pop() if len(groups[-1]) == 1 else None
    for bits in groups:
        n = 1 << len(bits)
        at = (s // bits[0]) % n
        v = v.reshape(n, -1, v.shape[-1])
        send = [lax.dynamic_index_in_dim(v, at ^ m, 0, keepdims=False) for m in range(n)]
        dep = yield tuple(send)
        got = swap_all(after(send, dep), "seq", bits)
        v = sum(g.astype(f32) for g in got).astype(bf16)
    if single:
        dep = yield v
        v = add(v, swap(after(v, dep), "seq", single[0]))
    for bits in reversed(groups):
        dep = yield v
        v = after(v, dep)
        got = swap_all([v] * (1 << len(bits)), "seq", bits)
        dep = yield tuple(got[1:])
        v = jnp.concatenate(by_index(after(tuple(got), dep), s, bits), axis=0)
    yield v.astype(f32)


def small_steps(v):
    for axis in ("wshard", "seq"):
        at = lax.axis_index(axis)
        for bits in pairs_of(lax.axis_size(axis)):
            dep = yield v
            v = after(v, dep)
            v = sum(by_index(swap_all([v] * (1 << len(bits)), axis, bits), at, bits))
    yield v


def pack_state(decay, state):
    hi, lo = two(decay)
    return jnp.concatenate([state.astype(bf16), hi, lo], axis=0)


def unpack_state(v, n):
    return v[n : n + 8].astype(f32)[:1] + v[n + 8 : n + 16].astype(f32)[:1], v[:n].astype(f32)


def carried(send, decay, state, sign, tokens):
    n = state.shape[0]
    span = 1
    while span < -(-LONGEST // tokens):
        if span > 1:
            send = pack_state(decay, state)
        dep = yield send
        d, s = unpack_state(shift(after(send, dep), "seq", sign * span), n)
        state = state + decay[:1] * s
        decay = decay * d
        span *= 2
    send = state.astype(bf16)
    dep = yield send
    yield shift(after(send, dep), "seq", sign)


class Steps:
    def __init__(self, gen):
        self.gen = gen
        self.value = next(gen)

    def step(self, dep=None):
        try:
            self.value = self.gen.send(dep)
        except StopIteration:
            pass
        return self.value

    def finish(self):
        for self.value in self.gen:
            pass
        return self.value


def body(inputs, cotangent, lengths, in_proj, out_proj, conv_weight, conv_bias, a_log, d_skip,
         dt_bias, norm_gain, gate_gain):
    t, d = inputs.shape[1:]
    nw = lax.axis_size("wshard")
    di = out_proj.shape[0] * nw
    heads = a_log.shape[0] * nw
    conv = conv_bias.shape[0] * nw
    taps = conv_weight.shape[0]
    n = (conv - di) // 2
    p = di // heads
    docs = lengths.shape[1]
    nt, nc, nb = t // TB, t // CH, TB // CH
    wide = conv + 128
    first = lax.axis_index("seq") * t
    pos = first - 8 + jnp.arange(t + 16, dtype=jnp.int32)
    ends = jnp.cumsum(lengths[0], dtype=jnp.int32)
    seg = jnp.sum((pos[:, None] >= ends[None]).astype(jnp.int32), axis=1)
    seg = jnp.where(pos < 0, -1, seg)
    here = seg[: t + 8]
    own = seg[8 : t + 8]
    entering = jnp.repeat(seg[7 : t + 7 : CH], CH)
    leaving = jnp.repeat(seg[7 + CH : t + 8 : CH], CH)
    zero8 = jnp.zeros((8,), jnp.int32)
    back = [jnp.concatenate([zero8, (seg[8 - k : t + 8 - k] == own).astype(jnp.int32)]) for k in (3, 2, 1)]
    ahead = [(seg[k : t + 8 + k] == here).astype(jnp.int32) for k in (1, 2, 3)]
    cols = [here, jnp.concatenate([zero8, (entering == own).astype(jnp.int32)]),
            jnp.concatenate([zero8, (leaving == own).astype(jnp.int32)])]
    cols = cols + back + [(here < docs).astype(jnp.int32)] + ahead + [jnp.zeros_like(here)] * 6
    tok_all = jnp.stack(cols, axis=1).astype(f32)
    tok, elink = tok_all[8:], tok_all[:8]
    segr = own.astype(f32)[None]
    ids = jnp.stack(part_ids("wshard")).astype(jnp.int32)
    u, cot = inputs[0], cotangent[0]
    ue = shift(u[t - 16 :], "seq", 1)
    wx, wz = in_proj[:, di:], in_proj[:, :di]
    pc = conv // nw
    width = -(-max(pc, di // nw, 384) // 128) * 128


    def line(*vs):
        vs = [v if v.ndim == 2 else v[None] for v in vs]
        vs = [jnp.pad(v, ((0, 0), (0, (width if k == len(vs) - 1 else 128 * (k + 1)) - 128 * k - v.shape[1])))
              for k, v in enumerate(vs)]
        return jnp.concatenate(vs, axis=1)

    small = jnp.concatenate(
        [line(conv_weight), line(conv_bias), line(gate_gain), line(norm_gain), line(a_log, d_skip, dt_bias)], axis=0)
    wx_parts = gather_parts(wx, "wshard")
    small = in_order(gather_parts(after(small, (wx_parts[nw // 2], wz, tok, ids, ue)), "wshard"), "wshard").astype(f32)
    wz_parts = gather_parts(after(wz, wx_parts[-1]), "wshard")
    wo_parts = gather_parts(after(out_proj, wx_parts[-1]), "wshard")
    hw = heads // nw
    cw = small[:, :taps, :pc].swapaxes(0, 1).reshape(taps, conv)
    cb = small[:, taps, :pc].reshape(1, conv)
    gain_gate = small[:, taps + 1, : di // nw].reshape(1, di)
    gain_in = small[:, taps + 2, : d // nw].reshape(1, d)
    log_rate, skip, dtb = [small[:, taps + 3, 128 * k : 128 * k + hw].reshape(1, heads) for k in range(3)]
    rate = -jnp.exp(log_rate)
    pad = ((0, 0), (0, 128 - heads))
    nr = jnp.pad(rate, pad)
    nr2 = nr * LOG2E
    dtb = jnp.pad(dtb, pad)
    dsk = jnp.repeat(skip, p, axis=1)
    e1 = np.arange(128)[:, None] == np.arange(di)[None] // p
    e2 = jnp.asarray(np.concatenate([e1, e1], axis=0), bf16)
    hot = jnp.asarray(np.arange(heads * CH)[:, None] // CH == np.arange(128)[None], bf16)

    outs = [
        (rows(TB, d), (t, d), bf16),
        (rows(TB, conv), (t, conv), bf16),
        (rows(TB, conv), (t, conv), bf16),
        (rows(TB, conv), (t, conv), bf16),
        (rows(TB, di), (t, di), bf16),
        (rows(TB, 256), (t, 256), f32),
        (rows(TB, 128), (t, 128), f32),
        (pl.BlockSpec((32, TB), lambda i, s: (0, i)), (32, t), f32),
        (pl.BlockSpec((nb, n, di), lambda i, s: (i, 0, 0)), (nc, n, di), bf16),
        (pl.BlockSpec((nb, 8, 128), lambda i, s: (i, 0, 0)), (nc, 8, 128), f32),
        (whole((n, di)), (n, di), f32),
        (whole((8, di)), (8, di), f32),
        (whole((n + 16, di)), (n + 16, di), bf16),
        (whole((16, d)), (16, d), bf16),
        (whole((16, conv)), (16, conv), bf16),
    ]
    ins = [rows(TB, d), whole((16, d)), whole((1, d))] + [whole(v.shape) for v in wx_parts]
    ins += [whole((taps, conv)), whole((1, conv)), whole((1, 128)), whole((1, 128)), rows(TB, 16), whole((256, di))]
    scratch = [
        pltpu.VMEM((d, wide), bf16),
        pltpu.VMEM((TB + 8, conv), f32),
        pltpu.VMEM((n, di), f32),
        pltpu.VMEM((1, 128), f32),
        pltpu.VMEM((2 * TB + 8 * nb, di), f32),
    ]
    (nrm, xbc, xc, slope, xd, dts, cc, ct, st, dbf, end, tot, pack, nrme, xbce) = call(
        front_kernel(nw, di, conv, heads), (nt,), ins, outs, scratch, 15,
        [ids, u, ue, gain_in] + wx_parts + [cw, cb, dtb, nr2, tok, e2], "front")
    chain = Steps(carried(pack, tot, end, 1, t))
    chain.step(wz_parts[1])
    chain.step()
    chain.step(wo_parts[1])
    incoming = chain.finish()

    crow = pl.BlockSpec((32, TI), lambda i, s: (0, i))
    srow = pl.BlockSpec((1, TI), lambda i, s: (0, i))
    crow2 = pl.BlockSpec((32, CH), lambda i, s: (0, i))
    srow2 = pl.BlockSpec((1, CH), lambda i, s: (0, i))
    bspec, cspec = rows(TI, n, di // n), rows(TI, n, di // n + 1)
    (yin,) = call(
        inner_kernel(heads, di), (t // TI,),
        [bspec, cspec, rows(TI, di), rows(TI, 128), crow, rows(TI, 16), srow],
        [(rows(TI, di), (t, di), bf16)], [], 10,
        [ids, xc, xc, xd, cc, ct, tok, segr], "inner")

    blk = pl.BlockSpec((nb, n, di), lambda i, s: (i, 0, 0))
    outs = [
        (rows(TB, d), (t, d), bf16),
        (rows(TB, di), (t, di), bf16),
        (rows(TB, di), (t, di), bf16),
        (rows(TB, di), (t, di), bf16),
        (rows(TB, di), (t, di), bf16),
        (rows(TB, d), (t, d), bf16),
        (blk, (nc, n, di), bf16),
        (blk, (nc, n, di), bf16),
        (rows(TB, 128), (t, 128), f32),
        (whole((8, 128)), (8, 128), f32),
        (whole((n, di)), (n, di), f32),
        (whole((n + 16, di)), (n + 16, di), bf16),
    ]
    ins = [rows(TB, d), rows(TB, di), rows(TB, di), rows(TB, n, di // n + 1), rows(TB, 128), rows(TB, 16), blk,
           pl.BlockSpec((nb, 8, 128), lambda i, s: (i, 0, 0)), whole((n, di)), whole((8, di)), rows(TB, d), rows(TB, d)]
    ins += [whole(v.shape) for v in wz_parts + wo_parts]
    ins += [whole((1, di)), whole((1, di)), whole((256, di))]
    scratch = [pltpu.VMEM((d, di), bf16), pltpu.VMEM((di, d), bf16)]
    scratch += [pltpu.VMEM((TB, di), f32)] * 3
    scratch += [pltpu.VMEM((TB + 8 * nb, di), f32), pltpu.VMEM((TB, di), bf16), pltpu.VMEM((8, di), f32)]
    (mixed, gn, dz, dy, edy, e, sf, dcs, rin, g_skip, reach, reach_pack) = call(
        gate_kernel(nw, di, d), (nt,), ins, outs, scratch, 25,
        [ids, nrm, yin, xc, xc, cc, tok, st, dbf, incoming, tot, u, cot] + wz_parts + wo_parts + [gain_gate, dsk, e2], "gate")
    tn = (((0,), (0,)), ((), ()))

    def outer(a, b):
        return lax.dot_general(a, b, tn, preferred_element_type=f32)

    back_state = Steps(carried(reach_pack, tot, reach, -1, t))
    s1 = back_state.value
    gw_out = outer(after(gn, s1), e).astype(bf16)
    gw_z = outer(nrm, after(dz, s1)).astype(bf16)
    s2 = back_state.step()
    oz_p = Steps(pair_steps([gw_out, gw_z]))
    oz_w = Steps(other_steps(oz_p.step(s2)))
    oz2 = oz_w.value
    hh, hw2 = heads // 2, di // 2

    def at(shape, col):
        return pl.BlockSpec(shape, lambda i, s: (0, col))

    def half_inner(k, dep):
        outs = [
            (rows(CH, hw2), (t, hw2), bf16),
            (rows(CH, n), (t, n), f32),
            (rows(CH, n), (t, n), f32),
            (rows(CH, 128), (t, 128), f32),
        ]
        return call(
            inner_back_kernel(p, hh * k, hh * (k + 1)), (t // CH,),
            [rows(CH, n, di // n), rows(CH, n, di // n + 1), rows(CH, hw2, k), rows(CH, hw2, k), rows(CH, 128), crow2,
             pl.BlockSpec((hh * CH, 128), lambda i, s: (k, 0)), rows(CH, 16), srow2],
            outs, [pltpu.VMEM((128, CH), f32)], 12,
            [ids, xc, xc, xd, after(dy, dep), cc, ct, hot, tok, segr], "inner_back")

    def rev(block, width, col=0):
        return pl.BlockSpec((block, width), lambda i, s: (nt - 1 - i, col))

    def half_back(k, inner, dep, gend, extra):
        gxd, dbi, dci, rk = inner
        last = k == 1
        cols = hw2 + 2 * n if last else hw2
        rblk = pl.BlockSpec((nb, n, hw2), lambda i, s: (nt - 1 - i, 0, k))
        ins = [rev(TB, hw2, k), rev(TB, n, di // n), rev(TB, hw2, k), rev(TB, hw2, k), at((16, hw2), k),
               rev(TB, hw2, k), rev(TB, 256), rev(TB, 128), rev(TB, 16), whole((8, 16)), rev(TB, hw2),
               rev(TB, n), rev(TB, n), rev(TB, 128), rev(TB, 128), rev(TB, hw2, k), rev(TB, hw2, k), rblk, rblk,
               at((n, hw2), k), at((taps, hw2), k), at((1, hw2), k), whole((1, 128)), at((256, hw2), k)]
        args = [ids, xc, xc, slope, xbc, xbce, xd, dts, cc, tok, elink, after(gxd, dep), dbi, dci, rk, rin, dy,
                edy, sf, dcs, gend, cw, dsk, nr, e2]
        outs = [
            (rev(TB, cols + 128 * last), (t, cols + 128 * last), bf16),
            (whole((16, cols)), (16, cols), bf16),
            (whole((8, cols)), (8, cols), f32),
        ]
        if last:
            ins += [rev(TB, 2 * n, di // (2 * n)), rev(TB, 2 * n, di // (2 * n)), at((16, 2 * n), di // (2 * n)),
                    at((taps, 2 * n), di // (2 * n)), rev(TB, n), rev(TB, n), rev(TB, 128), whole((8, 128))]
            args += [slope, xbc, xbce, cw] + list(extra)
        else:
            outs += [(rev(TB, n), (t, n), f32), (rev(TB, n), (t, n), f32), (rev(TB, 128), (t, 128), f32)]
        scratch = [
            pltpu.VMEM((n, hw2), f32),
            pltpu.VMEM((2 * TB + 8 * nb, hw2), f32),
            pltpu.VMEM((TB, hw2), f32),
            pltpu.VMEM((TB + 8, cols), f32),
            pltpu.VMEM((TB, hw2), bf16),
            pltpu.VMEM((TB, hw2), bf16),
            pltpu.VMEM((8 * taps, cols), f32),
            pltpu.VMEM((8, cols), f32),
            pltpu.VMEM((8, 128), f32),
            pltpu.VMEM((8, 128), f32),
        ]
        return call(back_kernel(hw2, n, hh * k, hh * (k + 1), last), (nt,), ins, outs, scratch, 15, args, "back")

    in_a = half_inner(0, (s2, oz2))
    s3 = back_state.step(oz2)
    s3, in_a0 = lax.optimization_barrier((s3, in_a[0]))
    in_b = half_inner(1, (s3, in_a0))
    back_state.step(in_a[0])
    gend = back_state.finish()
    oz_w.step()
    oz_s = Steps(seq_steps(oz_w.finish()))
    oz3 = oz_s.value
    (gpa, edge_a, sum_a, dbp, dcp, ddtp) = half_back(0, in_a, (in_b[0], oz3), gend, None)
    oz4 = oz_s.step(in_b[0])
    gw_xa = (outer(nrm, after(gpa, oz4)) + outer(nrme, edge_a)).astype(bf16)
    xa_p = Steps(pair_steps([gw_xa]))
    xa1 = xa_p.value
    (gpb, edge_b, sum_b) = half_back(1, in_b, (oz4, xa1), gend, (dbp, dcp, ddtp, g_skip))
    oz5 = oz_s.step(gpa)
    oz5, gpb_late = lax.optimization_barrier((oz5, gpb))
    gw_xb = outer(nrm, gpb_late)
    cb2 = conv - hw2
    gw_xb = jnp.concatenate(
        [gw_xb[:, :cb2] + outer(nrme, edge_b), gw_xb[:, cb2 : cb2 + heads]], axis=1).astype(bf16)
    xb_p = Steps(pair_steps([gw_xb]))
    x_w = Steps(other_steps(jnp.concatenate([xa_p.step(), xb_p.step()], axis=2)))
    x2 = x_w.value
    edge_in = shift(jnp.concatenate([edge_a, edge_b], axis=1), "seq", -1)
    oz7 = oz_s.step(x2)

    ins = [rows(TB, di), rows(TB, hw2), rows(TB, wide - hw2), whole((16, conv)), rows(TB, d), rows(TB, d)]
    ins += [whole(v.shape) for v in wz_parts + wx_parts] + [whole((1, d))]
    outs = [(rows(TB, d), (t, d), bf16)]
    (grad_input,) = call(
        input_kernel(nw, di, conv, heads), (nt,), ins, outs,
        [pltpu.VMEM((d, di), bf16), pltpu.VMEM((d, wide), bf16), pltpu.VMEM((TB, d), f32)], 12,
        [ids, dz, after(gpa, x2), gpb, edge_in, u, e] + wz_parts + wx_parts + [gain_in], "input")
    sums = Steps(small_steps(jnp.concatenate([sum_a, sum_b], axis=1)))
    x_s = Steps(seq_steps(x_w.finish()))
    x3 = x_s.value
    sums.step((x3, grad_input))
    x4 = x_s.step((grad_input, oz7))
    sums.step(x4)
    oz_s.step(x4)
    x5 = x_s.step()
    sums.step(x5)
    r_x, r_oz, total = x_s.finish(), oz_s.finish(), sums.finish()
    k = r_oz.shape[1] - di
    r_out = jnp.concatenate([r_oz[:, q * d : (q + 1) * d] for q in range(k // d)], axis=0)
    r_z = r_oz[:, k:]
    w = lax.axis_index("wshard")

    def mine(v):
        width = v.shape[-1] // nw
        return lax.dynamic_slice_in_dim(v, w * width, width, axis=v.ndim - 1)

    by_head = total[5:8, :heads] + total[5:8, hw2 : hw2 + heads]
    by_head = mine(by_head * jnp.concatenate([rate, jnp.ones((2, heads), f32)], axis=0))
    res = [mine(total[:taps]), mine(total[taps]), by_head[0], by_head[2], by_head[1]]
    res.append((jnp.sum(r_z * wz.astype(f32), axis=1) + jnp.sum(r_x * wx.astype(f32), axis=1)) / norm_gain.astype(f32))
    res.append(jnp.sum(r_out * out_proj.astype(f32), axis=1) / gate_gain.astype(f32))
    return (mixed[None], grad_input[None], jnp.concatenate([r_z, r_x], axis=1), r_out) + tuple(res)


def solution(mesh):
    wide = P("wshard", "seq", None)
    mat = P("wshard", None)
    taps = P(None, "wshard")
    vec = P("wshard")
    return jax.shard_map(
        body,
        mesh=mesh,
        in_specs=(wide, wide, mat, mat, mat, taps) + (vec,) * 6,
        out_specs=(wide, wide, mat, mat, taps) + (vec,) * 6,
        check_vma=False,
    )
```
